256 devices in a mesh: rows: 16 (over y, x), vocab: 16 (over z, core).
Axes of the slice: x: 4, y: 4, z: 8, core: 2. Of those that a mesh axis runs over, the one named last changes fastest.
Arguments:
- hidden: bfloat16 [16, 1024, 4096], P('rows', None, 'vocab'), may hold values from -1024 to 1024
- mask_positions: int32 [16, 1024], P('rows'), may hold values from 0 to 1023, each once within a row
- counts: int32 [16], replicated, may hold values from 1 to 64, 512 in all
- targets: int32 [16, 1024], P('rows'), may hold values from 0 to 126463
- mask_ratio: int32 [16], P('rows'), may hold values from 1 to 16
- out_weight: bfloat16 [4096, 126464], P(None, ('rows', 'vocab')), may hold values from -1 to 1
Outputs:
- grad_hidden: float32 [16, 1024, 4096], P('rows', None, 'vocab')
The draws below stay inside these ranges and needn't reach their ends.
Inputs may be any that keep to these rules, and one draw needn't show every extreme that they name: counts sum to 512; some sequence has exactly 64. The first counts[s] entries of row s of mask_positions are its masked positions.
All inputs are finite; a program needn't handle non-finite values.
Results may differ from the reference program's by a relative error of at most 0.0022.
Values may be sent and summed in bfloat16 or wider, within the bound.
No kernel may reach another device: no remote copies, remote signals or barrier semaphores. Data moves between devices by JAX's collectives and lax.ppermute only.
A program may use at most 64 MiB of HBM per device.

```python
import math
import jax
import jax.numpy as jnp
import numpy as np
from jax import lax

D = 4096
VOCAB = 126464
LEN = 1024
ROW_DEV = 32
SEQS = 16
TOTAL = 512
N_ROWS = 16


def weight_table(key):
    base = jax.random.truncated_normal(key, -6.0, 6.0, (D, VOCAB), jnp.float32)
    return base * 0.046875


def draw_out_weight(key, part):
    return weight_table(key).astype(jnp.bfloat16)


def draw_hidden(key, part):
    table = weight_table(key)
    key = jax.random.fold_in(key, 7)
    keys = jax.random.split(key, 5)
    base = jax.random.truncated_normal(keys[4], -6.0, 6.0, (SEQS, LEN, D), jnp.float32)
    chosen = jax.random.randint(keys[2], (SEQS, LEN // 8), 0, VOCAB - 1)
    strength = jax.random.uniform(keys[3], (SEQS, LEN // 8, 1), jnp.float32, 1.0, 2.4)
    first_col = jnp.moveaxis(jnp.sign(table[:, chosen]), 0, -1)
    second_col = jnp.moveaxis(jnp.sign(table[:, chosen + 1]), 0, -1)
    aligned = strength * (first_col + 0.98 * second_col) * (2700.0 / D)
    shaped = base.reshape(SEQS, LEN // 8, 8, D)
    shaped = shaped.at[:, :, 0, :].set(aligned)
    return shaped.reshape(SEQS, LEN, D).astype(jnp.bfloat16)


def touch_ends(drawn, stream_key, smallest, high):
    spot = [jax.random.randint(jax.random.fold_in(stream_key, axis), (), 0, length) for axis, length in enumerate(drawn.shape)]
    widest = drawn.shape.index(max(drawn.shape))
    beside = spot[:widest] + [(spot[widest] + 1) % drawn.shape[widest]] + spot[widest + 1:]
    return drawn.at[tuple(spot)].set(smallest).at[tuple(beside)].set(high)


def wide_ids(own_key, shape, count, skew):
    portions = [min(1 << octave, count + 1 - (1 << octave)) * (1 << 20) // math.isqrt((1 << octave) ** skew) + 1 for octave in range((count + 1).bit_length()) if 1 << octave <= count]
    scale = 1 + sum(portions) // (1 << 30)
    table = np.cumsum(np.array([max(1, weight // scale) for weight in portions]))
    ticket = jax.random.randint(jax.random.fold_in(own_key, 1), shape, 0, int(table[len(portions) - 1]))
    start = jnp.left_shift(1, jnp.searchsorted(jnp.asarray(table, jnp.int32), ticket, side="right").astype(jnp.int32))
    rank = start - 1 + jax.random.randint(jax.random.fold_in(own_key, 4), shape, 0, 1 << 30) % jnp.minimum(start, count + 1 - start)
    return jax.random.permutation(jax.random.fold_in(own_key, 2), count)[rank].astype(jnp.int32)


def profile(number_of, total, reach, skew):
    portions = [(1 << 20) // math.isqrt(grade ** skew) + 1 for grade in range(2, number_of + 1)]
    spare, given = total - reach - (number_of - 1), [1] * (number_of - 1)
    while spare > 0:
        free = [i for i in range(number_of - 1) if given[i] < reach]
        whole, remaining = sum([portions[i] for i in free]), spare
        for i in free:
            extra = min(reach - given[i], max(1, remaining * portions[i] // whole), spare)
            given[i] = given[i] + extra
            spare = spare - extra
    return np.array([reach] + given)


def uneven(key, count, total, most, skew):
    if count == 2:
        one = jax.random.randint(key, (), max(1, total - most), min(most, total - 1) + 1)
        return jnp.stack([one, total - one])
    lengths = jnp.asarray(profile(count, total, most, skew), jnp.int32)
    twos = (count - 1) // 2
    donor, sink = lengths[1:1 + 2 * twos:2], lengths[2:2 + 2 * twos:2]
    slack = jnp.minimum(donor - 1, most - sink)
    passed = jax.random.randint(jax.random.fold_in(key, 1), (twos,), 0, 1 << 20) % (slack + 1)
    lengths = lengths.at[1:1 + 2 * twos:2].set(donor - passed).at[2:2 + 2 * twos:2].set(sink + passed)
    return lengths[jax.random.permutation(jax.random.fold_in(key, 2), count)]


def setup_inputs(seed: int = 0) -> dict:
    streams_of = jax.random.split(jax.random.key(seed), 7)
    hidden = draw_hidden(jax.random.fold_in(streams_of[6], 71), 0)
    mask_positions = jax.vmap(lambda own: jax.random.permutation(own, LEN))(jax.random.split(streams_of[1], SEQS)).reshape((SEQS, LEN)).astype(jnp.int32)
    counts = uneven(streams_of[2], SEQS, ROW_DEV * N_ROWS, 2 * ROW_DEV, 2).astype(jnp.int32)
    targets = touch_ends(wide_ids(streams_of[3], (SEQS, LEN), VOCAB, 2), jax.random.fold_in(streams_of[3], 3), 0, VOCAB - 1).astype(jnp.int32)
    mask_ratio = touch_ends(jax.random.randint(streams_of[4], (SEQS,), 1, 17), jax.random.fold_in(streams_of[4], 1), 1, 16).astype(jnp.int32)
    out_weight = draw_out_weight(jax.random.fold_in(streams_of[6], 71), 0)
    return dict(hidden=hidden, mask_positions=mask_positions, counts=counts, targets=targets, mask_ratio=mask_ratio, out_weight=out_weight)


weight_scale = 4.0


def reference(hidden, mask_positions, counts, targets, mask_ratio, out_weight):
    ends = jnp.cumsum(counts).astype(jnp.int32)
    starts = (ends - counts).astype(jnp.int32)
    index = jnp.arange(TOTAL, dtype=jnp.int32)
    owner = jnp.sum((ends[None, :] <= index[:, None]).astype(jnp.int32), axis=1).astype(jnp.int32)
    local = (index - starts[owner]).astype(jnp.int32)
    places = mask_positions[owner, local].astype(jnp.int32)
    rows_x = hidden[owner, places]
    row_targets = targets[owner, places]
    row_weights = weight_scale / mask_ratio[owner].astype(jnp.float32)
    logits = jnp.dot(rows_x, out_weight, preferred_element_type=jnp.float32)
    top = jnp.max(logits, axis=1)
    total = jnp.sum(jnp.exp(logits - top[:, None]), axis=1)
    columns = jnp.arange(VOCAB, dtype=jnp.int32)
    onehot = (row_targets[:, None] == columns[None, :]).astype(jnp.float32)
    slope = (row_weights[:, None] * (jnp.exp(logits - top[:, None]) / total[:, None] - onehot)).astype(jnp.bfloat16)
    row_grad = lax.dot_general(slope, out_weight, (((1,), (1,)), ((), ())), preferred_element_type=jnp.float32)
    grad_hidden = jnp.zeros((SEQS, LEN, D), jnp.float32).at[owner, places].add(row_grad)
    return grad_hidden
```

```python
import jax
import jax.numpy as jnp
from jax import lax
from jax.sharding import Mesh
from jax.sharding import PartitionSpec as P

weight_scale = 4.0
SIDE = 4
SHARES = 16
SLOTS = 2
AUX = 128
ALL = ("y", "x", "z", "c")
SENT_SCALE = 4096.0


def slot_rows(start, end, share, core):
    first = (start - share + (SHARES - 1)) // SHARES
    first = first + ((first + core) & 1)
    step = jnp.arange(SLOTS, dtype=jnp.int32) * 2
    k = (first[..., None] + step) * SHARES + share[..., None]
    return k, k < end[..., None]


def shift(x, axis, by):
    size = {"y": SIDE, "x": SIDE, "z": 8, "c": 2}[axis]
    return lax.ppermute(x, axis, [(i, (i + by) % size) for i in range(size)])


def merge(parts):
    top = parts[0][0]
    for part in parts[1:]:
        top = jnp.maximum(top, part[0])
    total = sum(part[1] * jnp.exp(part[0] - top) for part in parts)
    return jnp.stack([top, total])


def local(hidden, mask_positions, counts, targets, mask_ratio, own_weight):
    y, x, z, c = [lax.axis_index(a) for a in ALL]
    seq = y * SIDE + x
    share = seq
    vocab_dev = own_weight.shape[1]
    feat = hidden.shape[2]
    near_weight = shift(own_weight, "c", 1)

    ids = jnp.arange(SHARES, dtype=jnp.int32)
    starts = jnp.sum(jnp.where(ids[None, :] < ids[:, None], counts[None, :], 0), axis=1)
    ends = starts + counts
    own_start = jnp.sum(jnp.where(ids < seq, counts, 0))
    own_end = own_start + jnp.sum(jnp.where(ids == seq, counts, 0))

    cores = jnp.arange(2, dtype=jnp.int32)
    to_share = jnp.broadcast_to(ids[:, None], (SHARES, 2))
    to_core = jnp.broadcast_to(cores[None, :], (SHARES, 2))
    k, valid = slot_rows(own_start, own_end, to_share, to_core)
    valid = valid.reshape(-1)
    index = jnp.where(valid, k.reshape(-1) - own_start, 0)
    places = mask_positions[0][index]
    rows = jnp.where(valid[:, None], hidden[0][places], 0)
    row_targets = targets[0][places]
    lane = jnp.arange(AUX, dtype=jnp.int32)[None, :]
    digits = jnp.where(lane == 0, (row_targets & 127)[:, None], 0)
    digits = digits + jnp.where(lane == 1, ((row_targets >> 7) & 127)[:, None], 0)
    digits = digits + jnp.where(lane == 2, (row_targets >> 14)[:, None], 0)
    digits = digits + jnp.where(lane == 3, mask_ratio[0], 0)
    aux = jnp.where(valid[:, None], digits, 0).astype(jnp.bfloat16)
    payload = jnp.concatenate([rows, aux], axis=1).reshape(SHARES, 1, 2, SLOTS, feat + AUX)
    payload = jnp.broadcast_to(payload, (SHARES, 8, 2, SLOTS, feat + AUX))
    payload = payload.reshape(256, SLOTS, feat + AUX)
    got = lax.all_to_all(payload, ALL, 0, 0, tiled=True)
    got = got.reshape(SHARES, 16, SLOTS, feat + AUX)

    slot_k, slot_valid = slot_rows(starts, ends, jnp.broadcast_to(share, (SHARES,)), jnp.broadcast_to(c, (SHARES,)))
    mine = (jnp.arange(16, dtype=jnp.int32) * 2 + c) * SHARES + share
    pick = ((mine[:, None, None] == slot_k[None]) & slot_valid[None]).astype(jnp.bfloat16)
    block = jnp.einsum("jsa,svaf->jvf", pick, got, preferred_element_type=jnp.float32).astype(jnp.bfloat16)
    block_x = block[:, :, :feat].reshape(16, 16 * feat)
    half = 8 * feat
    first = block_x[:, :half]
    second = jnp.concatenate([block_x[:, half:], block[:, 0, feat:]], axis=1)

    first = jnp.stack([first] + [shift(first, "x", e) for e in (1, 2, 3)])
    second = jnp.stack([second] + [shift(second, "y", e) for e in (1, 2, 3)])
    first = jnp.stack([first] + [shift(first, "y", e) for e in (1, 2, 3)])
    second = jnp.stack([second] + [shift(second, "x", e) for e in (1, 2, 3)], axis=1)
    first = first.reshape(256, half)
    second = second.reshape(256, half + AUX)
    all_x = jnp.concatenate([first, second[:, :half]], axis=1)
    digits = second[:, half:half + 4].astype(jnp.int32)
    row_targets = digits[:, 0] + (digits[:, 1] << 7) + (digits[:, 2] << 14)
    row_weights = weight_scale / digits[:, 3].astype(jnp.float32)

    scores = [jnp.dot(all_x, w, preferred_element_type=jnp.float32) for w in (own_weight, near_weight)]
    top = jnp.maximum(jnp.max(scores[0], axis=1), jnp.max(scores[1], axis=1))
    total = sum(jnp.sum(jnp.exp(part - top[:, None]), axis=1) for part in scores)
    stats = jnp.stack([top, total])
    stats = merge([stats] + [shift(stats, "z", e) for e in range(1, 8)])
    wide = stats.reshape(2, SIDE, SIDE, 16)
    wide = merge([wide] + [jnp.roll(shift(stats, "x", e).reshape(wide.shape), e, axis=2) for e in (1, 2, 3)])
    stats = wide.reshape(2, 256)
    wide = merge([wide] + [jnp.roll(shift(stats, "y", e).reshape(wide.shape), e, axis=1) for e in (1, 2, 3)])
    top, total = wide.reshape(2, 256)

    row_sums = 0.0
    for part, w, core in ((scores[0], own_weight, c), (scores[1], near_weight, 1 - c)):
        columns = (seq * 16 + z * 2 + core) * vocab_dev + jnp.arange(vocab_dev, dtype=jnp.int32)
        onehot = (row_targets[:, None] == columns[None, :]).astype(jnp.float32)
        probs = jnp.exp(part - top[:, None]) / total[:, None]
        slope = (row_weights[:, None] * (probs - onehot)).astype(jnp.bfloat16)
        row_sums = row_sums + lax.dot_general(
            slope, w, (((1,), (1,)), ((), ())), preferred_element_type=jnp.float32
        )
    row_sums = (row_sums * SENT_SCALE).reshape(SIDE, SIDE, 16, 16 * feat)
    sent = row_sums.astype(jnp.float16)

    def collect(kept, blocks, axis):
        got = [shift(blocks[e], axis, e) for e in (1, 2, 3)]
        return kept + sum(g.astype(jnp.float32) for g in got)

    first = collect(row_sums[0, :, :, :half], {e: sent[-e, :, :, :half] for e in (1, 2, 3)}, "y")
    second = collect(row_sums[:, 0, :, half:], {e: sent[:, -e, :, half:] for e in (1, 2, 3)}, "x")
    sent = first.astype(jnp.float16)
    first = collect(first[0], {e: sent[-e] for e in (1, 2, 3)}, "x")
    sent = second.astype(jnp.float16)
    second = collect(second[0], {e: sent[-e] for e in (1, 2, 3)}, "y")
    share_sums = jnp.concatenate([first, second], axis=1) * (1.0 / SENT_SCALE)

    slot_row = jnp.where(slot_valid, slot_k // (2 * SHARES), 0).reshape(-1)
    back = jnp.where(slot_valid.reshape(-1)[:, None], share_sums[slot_row], 0.0)
    back = back.reshape(SHARES, SLOTS, 16, feat).transpose(0, 2, 1, 3).reshape(256, SLOTS, feat)
    back = lax.all_to_all(back, ALL, 0, 0, tiled=True)
    back = back.reshape(SHARES, 8, 2, SLOTS, feat).sum(axis=1).reshape(-1, feat)
    grad = jnp.zeros((hidden.shape[1], feat), jnp.float32)
    grad = grad.at[places].add(back)
    return grad[None]


def solution(mesh):
    fine = Mesh(mesh.devices.reshape(SIDE, SIDE, 8, 2), ALL)
    rows, vocab = ("y", "x"), ("z", "c")
    return jax.shard_map(
        local,
        mesh=fine,
        in_specs=(
            P(rows, None, vocab),
            P(rows, None),
            P(),
            P(rows, None),
            P(rows),
            P(None, ("y", "x", "z", "c")),
        ),
        out_specs=P(rows, None, vocab),
        check_vma=False,
    )
```

```python
import jax
import jax.numpy as jnp
from jax import lax
from jax.experimental import pallas as pl
from jax.experimental.pallas import tpu as pltpu
from jax.sharding import Mesh
from jax.sharding import PartitionSpec as P

weight_scale = 4.0
MOST = 64
SIDE = 4
DEEP = 8
SHARES = SIDE * SIDE
SLOTS = 2
HALF = SHARES * SLOTS
AUX = 128
PLANE = ("y", "x")
CHIPS = ("y", "x", "z")
SENT_SCALE = 4096.0


def slot_rows(start, share, core, slot):
    first = (start - share + (SHARES - 1)) >> 4
    first = first + ((first + core) & 1)
    return (first + 2 * slot) * SHARES + share


def pick_rows(counts_ref, ratio_ref, positions_ref, targets_ref, hidden_ref, keep_ref, give_ref, places_ref):
    seq = lax.axis_index("y") * SIDE + lax.axis_index("x")
    core = lax.axis_index("c")
    start = jnp.int32(0)
    count = jnp.int32(0)
    for i in range(SHARES):
        start = start + jnp.where(i < seq, counts_ref[i], 0)
        count = count + jnp.where(i == seq, counts_ref[i], 0)
    length, feat = hidden_ref.shape
    q = lax.broadcasted_iota(jnp.int32, (2 * HALF, 1), 0)
    of_core = (core + (q >> 5)) & 1
    index = slot_rows(start, (q >> 1) & 15, of_core, q & 1) - start
    valid = index < count
    at = lax.broadcasted_iota(jnp.int32, (2 * HALF, 128), 1)
    near = jnp.where(at == index, positions_ref[:, :128].astype(jnp.float32), 0.0)
    places = jnp.sum(near, axis=1, keepdims=True).astype(jnp.int32)
    places_ref[...] = places
    at = lax.broadcasted_iota(jnp.int32, (2 * HALF, length), 1)
    hit = (at == places) & valid
    rows = jnp.dot(jnp.where(hit, 1.0, 0.0).astype(jnp.bfloat16), hidden_ref[...], preferred_element_type=jnp.float32)
    rows = rows.astype(jnp.bfloat16)
    target = jnp.sum(jnp.where(hit, targets_ref[...].astype(jnp.float32), 0.0), axis=1, keepdims=True).astype(jnp.int32)
    lane = lax.broadcasted_iota(jnp.int32, (HALF, AUX), 1)
    own = target[:HALF]
    digits = jnp.where(lane == 0, own & 127, 0)
    digits = jnp.where(lane == 1, (own >> 7) & 127, digits)
    digits = jnp.where(lane == 2, own >> 14, digits)
    digits = jnp.where(lane == 3, ratio_ref[0], digits)
    keep_ref[:, :feat] = rows[:HALF]
    keep_ref[:, feat:] = digits.astype(jnp.float32).astype(jnp.bfloat16)
    give_ref[...] = rows[HALF:]


def swap_cores(x):
    return lax.ppermute(x, "c", [(0, 1), (1, 0)])


def by_core(c, own, near):
    return jnp.where(c == 0, own, near), jnp.where(c == 0, near, own)


def local(hidden, mask_positions, counts, targets, mask_ratio, own_weight):
    y, x, z, c = [lax.axis_index(a) for a in ("y", "x", "z", "c")]
    share = y * SIDE + x
    vocab_dev = own_weight.shape[1]
    wide = -(-vocab_dev // 128) * 128
    length, feat = hidden.shape[1:]
    features = 2 * DEEP * feat

    smem = pl.BlockSpec(memory_space=pltpu.SMEM)
    vmem = pl.BlockSpec(memory_space=pltpu.VMEM)
    keep, give, places = pl.pallas_call(
        pick_rows,
        out_shape=(
            jax.ShapeDtypeStruct((HALF, feat + AUX), jnp.bfloat16),
            jax.ShapeDtypeStruct((HALF, feat), jnp.bfloat16),
            jax.ShapeDtypeStruct((2 * HALF, 1), jnp.int32),
        ),
        in_specs=[smem, smem, vmem, vmem, vmem],
        out_specs=(vmem, vmem, vmem),
    )(counts, mask_ratio, mask_positions, targets, hidden[0])
    got = swap_cores(give)
    near_weight = swap_cores(own_weight)
    low, high = by_core(c, keep[:, :feat], got)
    payload = jnp.concatenate([low, high, keep[:, feat:]], axis=1).reshape(SHARES, 1, SLOTS, 2 * feat + AUX)
    payload = jnp.broadcast_to(payload, (SHARES, DEEP, SLOTS, 2 * feat + AUX))
    got = lax.all_to_all(payload.reshape(SHARES * DEEP, SLOTS, 2 * feat + AUX), CHIPS, 0, 0, tiled=True)
    got = got.reshape(SHARES, DEEP, SLOTS, 2 * feat + AUX)

    ids = jnp.arange(SHARES, dtype=jnp.int32)
    starts = jnp.sum(jnp.where(ids[None, :] < ids[:, None], counts[None, :], 0), axis=1)
    slot_k = slot_rows(starts[:, None], share, c, jnp.arange(SLOTS, dtype=jnp.int32)[None, :])
    slot_valid = slot_k < (starts + counts)[:, None]
    mine = (ids * 2 + c) * SHARES + share
    pick = ((mine[:, None, None] == slot_k[None]) & slot_valid[None]).astype(jnp.bfloat16)
    block = jnp.einsum("jsa,szaf->jzf", pick, got, preferred_element_type=jnp.float32).astype(jnp.bfloat16)
    digits = block[:, 0, 2 * feat:2 * feat + 4].astype(jnp.int32)
    own_targets = digits[:, 0] + (digits[:, 1] << 7) + (digits[:, 2] << 14)
    aux = jnp.stack([own_targets, digits[:, 3]]).astype(jnp.float32)
    block = block[:, :, :2 * feat].reshape(16, features)

    all_x = lax.all_to_all(jnp.broadcast_to(block[None], (SHARES, 16, features)), PLANE, 0, 0, tiled=True)
    all_x = all_x.reshape(SHARES * 16, features)

    pad = ((0, 0), (0, wide - vocab_dev))
    weight = jnp.concatenate([jnp.pad(own_weight, pad), jnp.pad(near_weight, pad)], axis=1)
    lane = jnp.arange(2 * wide, dtype=jnp.int32)
    offset = jnp.where(lane < wide, lane, lane - wide)
    core = jnp.where(lane < wide, c, 1 - c)
    columns = (share * 2 * DEEP + z * 2 + core) * vocab_dev + offset
    columns = jnp.where(offset < vocab_dev, columns, -1)
    scores = jnp.dot(all_x, weight, preferred_element_type=jnp.float32)
    scores = jnp.where((columns >= 0)[None, :], scores, -jnp.inf)
    top = jnp.max(scores, axis=1)
    total = jnp.sum(jnp.exp(scores - top[:, None]), axis=1)

    stats = jnp.concatenate([jnp.stack([top, total]), jnp.pad(aux, ((0, 0), (0, SHARES * 16 - 16)))], axis=0)
    stats = lax.all_to_all(jnp.broadcast_to(stats[None], (SHARES * DEEP,) + stats.shape), CHIPS, 0, 0, tiled=True)
    top = jnp.max(stats[:, 0], axis=0)
    total = jnp.sum(stats[:, 1] * jnp.exp(stats[:, 0] - top[None]), axis=0)
    aux = stats.reshape(SHARES, DEEP, 4, -1)[:, 0, 2:, :16]
    row_targets = aux[:, 0].reshape(-1).astype(jnp.int32)
    row_weights = weight_scale / aux[:, 1].reshape(-1)

    probs = jnp.exp(scores - top[:, None]) / total[:, None]
    onehot = (row_targets[:, None] == columns[None, :]).astype(jnp.float32)
    slope = (row_weights[:, None] * (probs - onehot)).astype(jnp.bfloat16)
    row_sums = lax.dot_general(slope, weight, (((1,), (1,)), ((), ())), preferred_element_type=jnp.float32)
    sent = (row_sums * SENT_SCALE).astype(jnp.float16).reshape(SHARES, 16, features)
    sent = lax.all_to_all(sent, PLANE, 0, 0, tiled=True)
    share_sums = jnp.sum(sent.astype(jnp.float32), axis=0) * (1.0 / SENT_SCALE)

    slot_row = jnp.where(slot_valid, slot_k >> 5, 0).reshape(-1)
    back = jnp.where(slot_valid.reshape(-1)[:, None], share_sums[slot_row], 0.0)
    back = back.reshape(SHARES, SLOTS, DEEP, 2 * feat).transpose(0, 2, 1, 3).reshape(SHARES * DEEP, SLOTS, 2 * feat)
    back = lax.all_to_all(back, CHIPS, 0, 0, tiled=True)
    back = back.reshape(SHARES, DEEP, SLOTS, 2 * feat).sum(axis=1).reshape(HALF, 2 * feat)
    keep, give = by_core(c, back[:, :feat], back[:, feat:])
    back = jnp.concatenate([keep, swap_cores(give)], axis=0)
    grad = jnp.zeros((length, feat), jnp.float32)
    grad = grad.at[places[:, 0]].add(back)
    return grad[None]


def solution(mesh):
    fine = Mesh(mesh.devices.reshape(SIDE, SIDE, DEEP, 2), CHIPS + ("c",))
    vocab = ("z", "c")
    return jax.shard_map(
        local,
        mesh=fine,
        in_specs=(
            P(PLANE, None, vocab),
            P(PLANE, None),
            P(),
            P(PLANE, None),
            P(PLANE),
            P(None, CHIPS + ("c",)),
        ),
        out_specs=P(PLANE, None, vocab),
        check_vma=False,
    )
```

```python
import jax
import jax.numpy as jnp
from jax import lax
from jax.experimental import pallas as pl
from jax.experimental.pallas import tpu as pltpu
from jax.sharding import Mesh
from jax.sharding import PartitionSpec as P

weight_scale = 4.0
MOST = 64
SIDE = 4
DEEP = 8
SHARES = SIDE * SIDE
SLOTS = 2
HALF = SHARES * SLOTS
AUX = 128
PLANE = ("y", "x")
CHIPS = ("y", "x", "z")
SENT_SCALE = 4096.0


def slot_rows(start, share, core, slot):
    first = (start - share + (SHARES - 1)) >> 4
    first = first + ((first + core) & 1)
    return (first + 2 * slot) * SHARES + share


def pick_rows(counts_ref, ratio_ref, positions_ref, targets_ref, hidden_ref, keep_ref, give_ref, places_ref):
    seq = lax.axis_index("y") * SIDE + lax.axis_index("x")
    core = lax.axis_index("c")
    start = jnp.int32(0)
    count = jnp.int32(0)
    for i in range(SHARES):
        start = start + jnp.where(i < seq, counts_ref[i], 0)
        count = count + jnp.where(i == seq, counts_ref[i], 0)
    length, feat = hidden_ref.shape
    q = lax.broadcasted_iota(jnp.int32, (2 * HALF, 1), 0)
    of_core = (core + (q >> 5)) & 1
    index = slot_rows(start, (q >> 1) & 15, of_core, q & 1) - start
    valid = index < count
    at = lax.broadcasted_iota(jnp.int32, (2 * HALF, 128), 1)
    near = jnp.where(at == index, positions_ref[:, :128].astype(jnp.float32), 0.0)
    places = jnp.sum(near, axis=1, keepdims=True).astype(jnp.int32)
    places_ref[...] = places
    at = lax.broadcasted_iota(jnp.int32, (2 * HALF, length), 1)
    hit = (at == places) & valid
    rows = jnp.dot(jnp.where(hit, 1.0, 0.0).astype(jnp.bfloat16), hidden_ref[...], preferred_element_type=jnp.float32)
    rows = rows.astype(jnp.bfloat16)
    target = jnp.sum(jnp.where(hit, targets_ref[...].astype(jnp.float32), 0.0), axis=1, keepdims=True).astype(jnp.int32)
    lane = lax.broadcasted_iota(jnp.int32, (HALF, AUX), 1)
    own = target[:HALF]
    digits = jnp.where(lane == 0, own & 127, 0)
    digits = jnp.where(lane == 1, (own >> 7) & 127, digits)
    digits = jnp.where(lane == 2, own >> 14, digits)
    digits = jnp.where(lane == 3, ratio_ref[0], digits)
    keep_ref[:, :feat] = rows[:HALF]
    keep_ref[:, feat:] = digits.astype(jnp.float32).astype(jnp.bfloat16)
    give_ref[...] = rows[HALF:]


def score_rows(x_ref, aux_ref, own_ref, near_ref, own_scores_ref, near_scores_ref, stats_ref, row_ref):
    step = pl.program_id(0)
    count = own_ref.shape[0]

    @pl.when(step == 0)
    def _():
        for ref in (own_scores_ref, near_scores_ref):
            ref[...] = jnp.zeros_like(ref)

    for w_ref, ref in ((own_ref, own_scores_ref), (near_ref, near_scores_ref)):
        ref[:count] += lax.dot_general(
            w_ref[...], x_ref[...], (((1,), (1,)), ((), ())), preferred_element_type=jnp.float32
        )

    @pl.when(step == pl.num_programs(0) - 1)
    def _():
        at = lax.broadcasted_iota(jnp.int32, own_scores_ref.shape, 0)
        parts = [jnp.where(at < count, ref[...], -jnp.inf) for ref in (own_scores_ref, near_scores_ref)]
        own_scores_ref[...], near_scores_ref[...] = parts
        top = jnp.maximum(*[jnp.max(part, axis=0, keepdims=True) for part in parts])
        total = sum(jnp.sum(jnp.exp(part - top), axis=0, keepdims=True) for part in parts)
        stats = jnp.concatenate([top, total], axis=0)
        stats_ref[...] = jnp.broadcast_to(stats[None], stats_ref.shape)
        digits = jnp.transpose(aux_ref[...].astype(jnp.float32))
        row_ref[0:1] = digits[0:1] + 128.0 * digits[1:2] + 16384.0 * digits[2:3]
        row_ref[1:2] = weight_scale / digits[3:4]


def grad_rows(stats_ref, row_ref, own_scores_ref, near_scores_ref, own_ref, near_ref, sent_ref, own_slope, near_slope):
    count = own_ref.shape[0]

    @pl.when(pl.program_id(0) == 0)
    def _():
        tops = stats_ref[:, 0, :]
        top = jnp.max(tops, axis=0, keepdims=True)
        total = jnp.sum(stats_ref[:, 1, :] * jnp.exp(tops - top), axis=0, keepdims=True)
        chip = (lax.axis_index("y") * SIDE + lax.axis_index("x")) * DEEP + lax.axis_index("z")
        core = lax.axis_index("c")
        target = row_ref[0:1].astype(jnp.int32)
        at = lax.broadcasted_iota(jnp.int32, own_scores_ref.shape, 0)
        for ref, out, of_core in ((own_scores_ref, own_slope, core), (near_scores_ref, near_slope, 1 - core)):
            local_target = target - (chip * 2 + of_core) * count
            probs = jnp.exp(ref[...] - top) / total
            onehot = jnp.where((at == local_target) & (at < count), 1.0, 0.0)
            out[...] = jnp.transpose(row_ref[1:2] * (probs - onehot)).astype(jnp.bfloat16)

    row_sums = jnp.dot(own_slope[:, :count], own_ref[...], preferred_element_type=jnp.float32)
    row_sums += jnp.dot(near_slope[:, :count], near_ref[...], preferred_element_type=jnp.float32)
    sent_ref[...] = (row_sums * SENT_SCALE).reshape(sent_ref.shape)


def swap_cores(x):
    return lax.ppermute(x, "c", [(0, 1), (1, 0)])


def by_core(c, own, near):
    return jnp.where(c == 0, own, near), jnp.where(c == 0, near, own)


def local(hidden, mask_positions, counts, targets, mask_ratio, own_weight):
    y, x, z, c = [lax.axis_index(a) for a in ("y", "x", "z", "c")]
    share = y * SIDE + x
    vocab_dev = own_weight.shape[1]
    length, feat = hidden.shape[1:]
    features = 2 * DEEP * feat

    smem = pl.BlockSpec(memory_space=pltpu.SMEM)
    vmem = pl.BlockSpec(memory_space=pltpu.VMEM)
    keep, give, places = pl.pallas_call(
        pick_rows,
        out_shape=(
            jax.ShapeDtypeStruct((HALF, feat + AUX), jnp.bfloat16),
            jax.ShapeDtypeStruct((HALF, feat), jnp.bfloat16),
            jax.ShapeDtypeStruct((2 * HALF, 1), jnp.int32),
        ),
        in_specs=[smem, smem, vmem, vmem, vmem],
        out_specs=(vmem, vmem, vmem),
    )(counts, mask_ratio, mask_positions, targets, hidden[0])
    got = swap_cores(give)
    near_weight = swap_cores(own_weight)
    payload = jnp.concatenate([keep[:, :feat], got, keep[:, feat:]], axis=1).reshape(SHARES, 1, SLOTS, 2 * feat + AUX)
    payload = jnp.broadcast_to(payload, (SHARES, DEEP, SLOTS, 2 * feat + AUX))
    got = lax.all_to_all(payload.reshape(SHARES * DEEP, SLOTS, 2 * feat + AUX), CHIPS, 0, 0, tiled=True)
    got = got.reshape(SHARES, DEEP, SLOTS, 2 * feat + AUX)

    ids = jnp.arange(SHARES, dtype=jnp.int32)
    starts = jnp.sum(jnp.where(ids[None, :] < ids[:, None], counts[None, :], 0), axis=1)
    slot_k = slot_rows(starts[:, None], share, c, jnp.arange(SLOTS, dtype=jnp.int32)[None, :])
    slot_valid = slot_k < (starts + counts)[:, None]
    mine = (ids * 2 + c) * SHARES + share
    pick = ((mine[:, None, None] == slot_k[None]) & slot_valid[None]).astype(jnp.bfloat16)
    block = jnp.einsum("jsa,szaf->jzf", pick, got, preferred_element_type=jnp.float32).astype(jnp.bfloat16)
    aux = block[:, 0, 2 * feat:]
    low, high = by_core(c, block[:, :, :feat], block[:, :, feat:2 * feat])
    block = jnp.concatenate([low, high], axis=2).reshape(16, features)
    block = jnp.concatenate([block, aux], axis=1)

    all_x = lax.all_to_all(jnp.broadcast_to(block[None], (SHARES, 16, features + AUX)), PLANE, 0, 0, tiled=True)
    rows = SHARES * 16
    all_x = all_x.reshape(rows, features + AUX)

    wide = -(-vocab_dev // 128) * 128
    step = 512
    steps = features // step
    whole = lambda *shape: pl.BlockSpec(shape, lambda i: (0,) * len(shape))
    along = lambda size: pl.BlockSpec((size, step), lambda i: (0, i))
    own_t, near_t = own_weight.T, near_weight.T
    own_scores, near_scores, stats, row_data = pl.pallas_call(
        score_rows,
        grid=(steps,),
        out_shape=(
            jax.ShapeDtypeStruct((wide, rows), jnp.float32),
            jax.ShapeDtypeStruct((wide, rows), jnp.float32),
            jax.ShapeDtypeStruct((SHARES * DEEP, 2, rows), jnp.float32),
            jax.ShapeDtypeStruct((2, rows), jnp.float32),
        ),
        in_specs=[
            along(rows),
            pl.BlockSpec((rows, AUX), lambda i: (0, features // AUX)),
            along(vocab_dev),
            along(vocab_dev),
        ],
        out_specs=(whole(wide, rows), whole(wide, rows), whole(SHARES * DEEP, 2, rows), whole(2, rows)),
        compiler_params=pltpu.CompilerParams(vmem_limit_bytes=32 << 20),
        cost_estimate=pl.CostEstimate(flops=4 * rows * vocab_dev * features, bytes_accessed=12 << 20, transcendentals=0),
    )(all_x, all_x, own_t, near_t)

    stats = lax.all_to_all(stats, CHIPS, 0, 0, tiled=True)
    sent = pl.pallas_call(
        grad_rows,
        grid=(steps,),
        out_shape=jax.ShapeDtypeStruct((SHARES, 16, features), jnp.float32),
        in_specs=[
            whole(SHARES * DEEP, 2, rows),
            whole(2, rows),
            whole(wide, rows),
            whole(wide, rows),
            along(vocab_dev),
            along(vocab_dev),
        ],
        out_specs=pl.BlockSpec((SHARES, 16, step), lambda i: (0, 0, i)),
        scratch_shapes=[pltpu.VMEM((rows, wide), jnp.bfloat16)] * 2,
        compiler_params=pltpu.CompilerParams(vmem_limit_bytes=32 << 20),
        cost_estimate=pl.CostEstimate(flops=4 * rows * vocab_dev * features, bytes_accessed=12 << 20, transcendentals=0),
    )(stats, row_data, own_scores, near_scores, own_t, near_t)
    sent = lax.all_to_all(sent.astype(jnp.float16), PLANE, 0, 0, tiled=True)
    share_sums = jnp.sum(sent.astype(jnp.float32), axis=0).reshape(16, DEEP, 2 * feat)

    back = jnp.einsum(
        "jsa,jzf->szaf", pick.astype(jnp.float32), share_sums, precision=lax.Precision.HIGHEST
    ).astype(jnp.float16)
    back = lax.all_to_all(back.reshape(SHARES * DEEP, SLOTS, 2 * feat), CHIPS, 0, 0, tiled=True)
    back = back.reshape(SHARES, DEEP, SLOTS, 2 * feat).astype(jnp.float32).sum(axis=1).reshape(HALF, 2 * feat)
    back = back * (1.0 / SENT_SCALE)
    kept, given = by_core(c, back[:, :feat], back[:, feat:])
    back = jnp.concatenate([kept, swap_cores(given)], axis=0)
    at = (places == jnp.arange(length, dtype=jnp.int32)[None, :]).astype(jnp.float32)
    grad = lax.dot_general(at, back, (((0,), (0,)), ((), ())), precision=lax.Precision.HIGHEST)
    return grad[None]


def solution(mesh):
    fine = Mesh(mesh.devices.reshape(SIDE, SIDE, DEEP, 2), CHIPS + ("c",))
    vocab = ("z", "c")
    return jax.shard_map(
        local,
        mesh=fine,
        in_specs=(
            P(PLANE, None, vocab),
            P(PLANE, None),
            P(),
            P(PLANE, None),
            P(PLANE),
            P(None, CHIPS + ("c",)),
        ),
        out_specs=P(PLANE, None, vocab),
        check_vma=False,
    )
```

```python
import jax
import jax.numpy as jnp
from jax import lax
from jax.experimental import pallas as pl
from jax.experimental.pallas import tpu as pltpu
from jax.sharding import Mesh
from jax.sharding import PartitionSpec as P

weight_scale = 4.0
SIDE = 4
DEEP = 8
SEQS = SIDE * SIDE
SLOTS = 32
ROWS = 256
CHUNK = ROWS // 2
AUX = 128
PLANE = ("y", "x")
CHIPS = ("y", "x", "z")
NT = (((1,), (1,)), ((), ()))
SENT_SCALE = 4096.0


def chip_index():
    return lax.axis_index("y") * SIDE + lax.axis_index("x")


def first_row(start, core):
    return start + ((start + core) & 1)


def own_rows(counts_ref, ratio_ref, positions_ref, targets_ref, hidden_ref, keep_ref, aux_ref, give_ref, places_ref):
    seq = chip_index()
    core = lax.axis_index("c")
    start = jnp.int32(0)
    count = jnp.int32(0)
    for i in range(SEQS):
        start = start + jnp.where(i < seq, counts_ref[i], 0)
        count = count + jnp.where(i == seq, counts_ref[i], 0)
    length = hidden_ref.shape[0]
    q = lax.broadcasted_iota(jnp.int32, (2 * SLOTS, 1), 0)
    index = jnp.where(q < SLOTS, first_row(start, core), first_row(start, 1 - core)) - start + 2 * (q & (SLOTS - 1))
    valid = index < count
    at = lax.broadcasted_iota(jnp.int32, (2 * SLOTS, 128), 1)
    near = jnp.where(at == index, positions_ref[:, :128].astype(jnp.float32), 0.0)
    places = jnp.where(valid, jnp.sum(near, axis=1, keepdims=True), -1.0)
    places_ref[...] = jnp.transpose(jnp.broadcast_to(places, (2 * SLOTS, 128)))[:8].astype(jnp.int32)
    at = lax.broadcasted_iota(jnp.int32, (2 * SLOTS, length), 1)
    hit = at == places.astype(jnp.int32)
    rows = jnp.dot(jnp.where(hit, 1.0, 0.0).astype(jnp.bfloat16), hidden_ref[...], preferred_element_type=jnp.float32)
    rows = rows.astype(jnp.bfloat16)
    target = jnp.sum(jnp.where(hit, targets_ref[...].astype(jnp.float32), 0.0), axis=1, keepdims=True).astype(jnp.int32)
    lane = lax.broadcasted_iota(jnp.int32, (SLOTS, AUX), 1)
    own = target[:SLOTS]
    digits = jnp.where(lane == 0, own & 127, 0)
    digits = jnp.where(lane == 1, (own >> 7) & 127, digits)
    digits = jnp.where(lane == 2, own >> 14, digits)
    digits = jnp.where(lane == 3, ratio_ref[0], digits)
    keep_ref[...] = rows[:SLOTS]
    aux_ref[...] = digits.astype(jnp.float32).astype(jnp.bfloat16)
    give_ref[...] = rows[SLOTS:]


def slot_dest(counts_ref, slot_index, core):
    slot = slot_index & (SLOTS - 1)
    dest = jnp.full_like(slot_index, -1)
    start = jnp.int32(0)
    for i in range(SEQS):
        end = start + counts_ref[i]
        first = first_row(start, core)
        mine = ((slot_index >> 5) == i) & (first + 2 * slot < end)
        dest = jnp.where(mine, (first >> 1) + slot, dest)
        start = end
    return dest


def pack_rows(counts_ref, slots_ref, low_ref, high_ref, row_ref):
    core = lax.axis_index("c")
    dest = slot_dest(counts_ref, lax.broadcasted_iota(jnp.int32, (1, SEQS * SLOTS), 1), core)
    at = lax.broadcasted_iota(jnp.int32, (ROWS, SEQS * SLOTS), 0)
    pick = jnp.where(at == dest, 1.0, 0.0).astype(jnp.bfloat16)
    packed = jnp.dot(pick, slots_ref[...], preferred_element_type=jnp.float32)
    feat = (slots_ref.shape[1] - AUX) // 2
    own, near = packed[:, :feat], packed[:, feat:2 * feat]
    for at, part in ((0, jnp.where(core == 0, own, near)), (feat, jnp.where(core == 0, near, own))):
        part = part.astype(jnp.bfloat16)
        low_ref[:, at:at + feat] = part[:CHUNK]
        high_ref[:, at:at + feat] = part[CHUNK:]
    digits = jnp.transpose(packed[:, 2 * feat:])
    row_ref[0:1] = digits[0:1] + 128.0 * digits[1:2] + 16384.0 * digits[2:3]
    row_ref[1:2] = weight_scale / digits[3:4]


def score_rows(own_ref, near_ref, *refs):
    chunks, (own_scores_ref, near_scores_ref, stats_ref) = refs[:2 * DEEP], refs[2 * DEEP:]
    z = lax.axis_index("z")
    count = own_ref.shape[0]
    span = chunks[0].shape[1]
    for away in range(DEEP):
        block = jnp.concatenate([chunks[2 * away][...], chunks[2 * away + 1][...]], axis=0)
        features = pl.ds(pl.multiple_of(((z + away) & (DEEP - 1)) * span, span), span)
        for w_ref, ref in ((own_ref, own_scores_ref), (near_ref, near_scores_ref)):
            part = lax.dot_general(w_ref[:, features], block, NT, preferred_element_type=jnp.float32)
            if away == 0:
                ref[:count] = part
            else:
                ref[:count] += part
    at = lax.broadcasted_iota(jnp.int32, own_scores_ref.shape, 0)
    parts = [jnp.where(at < count, ref[...], -jnp.inf) for ref in (own_scores_ref, near_scores_ref)]
    own_scores_ref[...], near_scores_ref[...] = parts
    top = jnp.maximum(*[jnp.max(part, axis=0, keepdims=True) for part in parts])
    total = sum(jnp.sum(jnp.exp(part - top), axis=0, keepdims=True) for part in parts)
    stats = jnp.concatenate([top, total], axis=0)
    stats_ref[...] = jnp.broadcast_to(stats[None], stats_ref.shape)


def grad_rows(stats_ref, row_ref, own_scores_ref, near_scores_ref, own_ref, near_ref, *refs):
    sums_refs, (own_slope, near_slope) = refs[:2 * DEEP], refs[2 * DEEP:]
    count = own_ref.shape[0]
    tops = stats_ref[:, 0, :]
    top = jnp.max(tops, axis=0, keepdims=True)
    total = jnp.sum(stats_ref[:, 1, :] * jnp.exp(tops - top), axis=0, keepdims=True)
    z = lax.axis_index("z")
    core = lax.axis_index("c")
    target = row_ref[0:1].astype(jnp.int32)
    at = lax.broadcasted_iota(jnp.int32, own_scores_ref.shape, 0)
    for ref, out, of_core in ((own_scores_ref, own_slope, core), (near_scores_ref, near_slope, 1 - core)):
        local_target = target - ((chip_index() * DEEP + z) * 2 + of_core) * count
        probs = jnp.exp(ref[...] - top) / total
        onehot = jnp.where((at == local_target) & (at < count), 1.0, 0.0)
        out[...] = jnp.transpose(row_ref[1:2] * (probs - onehot)).astype(jnp.bfloat16)
    span = sums_refs[0].shape[-1]
    for away in range(DEEP):
        features = pl.ds(pl.multiple_of(((z + away) & (DEEP - 1)) * span, span), span)
        sums = jnp.dot(own_slope[:, :count], own_ref[:, features], preferred_element_type=jnp.float32)
        sums += jnp.dot(near_slope[:, :count], near_ref[:, features], preferred_element_type=jnp.float32)
        sums = sums * SENT_SCALE
        sums_refs[2 * away][...] = sums[:CHUNK]
        sums_refs[2 * away + 1][...] = sums[CHUNK:]


def spread_rows(counts_ref, low_ref, high_ref, slots_ref):
    dest = slot_dest(counts_ref, lax.broadcasted_iota(jnp.int32, (SEQS * SLOTS, 1), 0), lax.axis_index("c"))
    at = lax.broadcasted_iota(jnp.int32, (SEQS * SLOTS, ROWS), 1)
    pick = jnp.where(at == dest, 1.0, 0.0).astype(jnp.bfloat16)
    rest = jnp.concatenate([low_ref[...], high_ref[...]], axis=0)
    part = rest.astype(jnp.bfloat16)
    rest = (rest - part.astype(jnp.float32)).astype(jnp.bfloat16)
    slots = jnp.dot(pick, part, preferred_element_type=jnp.float32)
    slots_ref[...] = slots + jnp.dot(pick, rest, preferred_element_type=jnp.float32)


def place_rows(places_ref, kept_ref, got_ref, out_ref):
    length = out_ref.shape[0]
    at = lax.broadcasted_iota(jnp.int32, (length, 2 * SLOTS), 0)
    hit = jnp.where(at == places_ref[0:1], 1.0, 0.0).astype(jnp.bfloat16)
    rest = jnp.concatenate([kept_ref[...], got_ref[...]], axis=0)
    out = None
    for _ in range(3):
        part = rest.astype(jnp.bfloat16)
        rest = rest - part.astype(jnp.float32)
        part = jnp.dot(hit, part, preferred_element_type=jnp.float32)
        out = part if out is None else out + part
    out_ref[...] = out


def swap_cores(x):
    return lax.ppermute(x, "c", [(0, 1), (1, 0)])


def pass_on(x, by):
    return lax.ppermute(x, "z", [(i, (i + by) % DEEP) for i in range(DEEP)])


def gather_chips(low, high):
    lows, highs = {0: low}, {0: high}
    for hop in range(1, DEEP // 2 + 1):
        lows[-hop] = pass_on(lows[1 - hop], 1)
        highs[hop] = pass_on(highs[hop - 1], -1)
        if hop < DEEP // 2:
            highs[-hop] = pass_on(highs[1 - hop], 1)
            lows[hop] = pass_on(lows[hop - 1], -1)
    lows[DEEP // 2] = lows[-(DEEP // 2)]
    return [chunk for away in range(DEEP) for chunk in (lows[(away + 3) % DEEP - 3], highs[(away + 3) % DEEP - 3])]


def reduce_chips(lows, highs):
    def send(x, by):
        return pass_on(x.astype(jnp.float16), by).astype(jnp.float32)

    half = DEEP // 2
    low_right, high_left = lows[half], highs[half]
    low_left, high_right = lows[half + 1], highs[half - 1]
    for hop in range(1, half):
        low_right = send(low_right, 1) + lows[half - hop]
        high_left = send(high_left, -1) + highs[half + hop]
        if hop < half - 1:
            low_left = send(low_left, -1) + lows[half + 1 + hop]
            high_right = send(high_right, 1) + highs[half - 1 - hop]
    low = lows[0] + send(low_left, -1) + send(low_right, 1)
    high = highs[0] + send(high_right, 1) + send(high_left, -1)
    return low, high


def local(hidden, mask_positions, counts, targets, mask_ratio, own_weight):
    c = lax.axis_index("c")
    vocab_dev = own_weight.shape[1]
    wide = -(-vocab_dev // 128) * 128
    length, feat = hidden.shape[1:]
    span = 2 * feat
    smem = pl.BlockSpec(memory_space=pltpu.SMEM)
    vmem = pl.BlockSpec(memory_space=pltpu.VMEM)
    params = pltpu.CompilerParams(vmem_limit_bytes=40 << 20)
    shape = jax.ShapeDtypeStruct

    keep, aux, give, places = pl.pallas_call(
        own_rows,
        out_shape=(
            shape((SLOTS, feat), jnp.bfloat16),
            shape((SLOTS, AUX), jnp.bfloat16),
            shape((SLOTS, feat), jnp.bfloat16),
            shape((8, 2 * SLOTS), jnp.int32),
        ),
        in_specs=[smem, smem, vmem, vmem, vmem],
        out_specs=(vmem,) * 4,
    )(counts, mask_ratio, mask_positions, targets, hidden[0])
    got = swap_cores(give)
    near_weight = swap_cores(own_weight)
    own_t, near_t = own_weight.T, near_weight.T

    slots = jnp.concatenate([keep, got, aux], axis=1)
    slots = lax.all_to_all(jnp.broadcast_to(slots[None], (SEQS,) + slots.shape), PLANE, 0, 0, tiled=True)
    low, high, row_data = pl.pallas_call(
        pack_rows,
        out_shape=(
            shape((CHUNK, span), jnp.bfloat16),
            shape((CHUNK, span), jnp.bfloat16),
            shape((2, ROWS), jnp.float32),
        ),
        in_specs=[smem, vmem],
        out_specs=(vmem,) * 3,
    )(counts, slots.reshape(SEQS * SLOTS, span + AUX))

    chunks = gather_chips(low, high)
    own_scores, near_scores, stats = pl.pallas_call(
        score_rows,
        out_shape=(
            shape((wide, ROWS), jnp.float32),
            shape((wide, ROWS), jnp.float32),
            shape((SEQS * DEEP, 2, ROWS), jnp.float32),
        ),
        in_specs=[vmem] * (2 + 2 * DEEP),
        out_specs=(vmem,) * 3,
        compiler_params=params,
    )(own_t, near_t, *chunks)

    stats = lax.all_to_all(stats, CHIPS, 0, 0, tiled=True)
    sums = pl.pallas_call(
        grad_rows,
        out_shape=(shape((CHUNK, span), jnp.float32),) * (2 * DEEP),
        in_specs=[vmem] * 6,
        out_specs=(vmem,) * (2 * DEEP),
        scratch_shapes=[pltpu.VMEM((ROWS, wide), jnp.bfloat16)] * 2,
        compiler_params=params,
    )(stats, row_data, own_scores, near_scores, own_t, near_t)

    low, high = reduce_chips(sums[::2], sums[1::2])
    back = pl.pallas_call(
        spread_rows,
        out_shape=shape((SEQS * SLOTS, span), jnp.float32),
        in_specs=[smem, vmem, vmem],
        out_specs=vmem,
    )(counts, low, high)
    back = back.astype(jnp.float16).reshape(SEQS, SLOTS, span)
    back = lax.all_to_all(back, PLANE, 0, 0, tiled=True)
    back = jnp.sum(back.astype(jnp.float32), axis=0) * (1.0 / SENT_SCALE)
    kept = jnp.where(c == 0, back[:, :feat], back[:, feat:])
    given = jnp.where(c == 0, back[:, feat:], back[:, :feat])
    grad = pl.pallas_call(
        place_rows,
        out_shape=shape((length, feat), jnp.float32),
        in_specs=[vmem] * 3,
        out_specs=vmem,
    )(places, kept, swap_cores(given))
    return grad[None]


def solution(mesh):
    fine = Mesh(mesh.devices.reshape(SIDE, SIDE, DEEP, 2), CHIPS + ("c",))
    vocab = ("z", "c")
    return jax.shard_map(
        local,
        mesh=fine,
        in_specs=(
            P(PLANE, None, vocab),
            P(PLANE, None),
            P(),
            P(PLANE, None),
            P(PLANE),
            P(None, CHIPS + ("c",)),
        ),
        out_specs=P(PLANE, None, vocab),
        check_vma=False,
    )
```

```python
import functools

import jax
import jax.numpy as jnp
from jax import lax
from jax.experimental import pallas as pl
from jax.experimental.pallas import tpu as pltpu
from jax.sharding import Mesh
from jax.sharding import PartitionSpec as P

weight_scale = 4.0
SIDE = 4
DEEP = 8
SEQS = SIDE * SIDE
SLOTS = 32
ROWS = 256
CHUNK = ROWS // 2
AUX = 128
PLANE = ("y", "x")
CHIPS = ("y", "x", "z")
NT = (((1,), (1,)), ((), ()))
SENT_SCALE = 4096.0


def chip_index():
    return lax.axis_index("y") * SIDE + lax.axis_index("x")


def first_row(start, core):
    return start + ((start + core) & 1)


def own_rows(counts_ref, ratio_ref, positions_ref, targets_ref, hidden_ref, keep_ref, aux_ref, give_ref, places_ref):
    seq = chip_index()
    core = lax.axis_index("c")
    start = jnp.int32(0)
    count = jnp.int32(0)
    for i in range(SEQS):
        start = start + jnp.where(i < seq, counts_ref[i], 0)
        count = count + jnp.where(i == seq, counts_ref[i], 0)
    length = hidden_ref.shape[0]
    q = lax.broadcasted_iota(jnp.int32, (2 * SLOTS, 1), 0)
    index = jnp.where(q < SLOTS, first_row(start, core), first_row(start, 1 - core)) - start + 2 * (q & (SLOTS - 1))
    valid = index < count
    at = lax.broadcasted_iota(jnp.int32, (2 * SLOTS, 128), 1)
    near = jnp.where(at == index, positions_ref[:, :128].astype(jnp.float32), 0.0)
    places = jnp.where(valid, jnp.sum(near, axis=1, keepdims=True), -1.0)
    places_ref[...] = jnp.transpose(jnp.broadcast_to(places, (2 * SLOTS, 128)))[:8].astype(jnp.int32)
    at = lax.broadcasted_iota(jnp.int32, (2 * SLOTS, length), 1)
    hit = at == places.astype(jnp.int32)
    rows = jnp.dot(jnp.where(hit, 1.0, 0.0).astype(jnp.bfloat16), hidden_ref[...], preferred_element_type=jnp.float32)
    rows = rows.astype(jnp.bfloat16)
    target = jnp.sum(jnp.where(hit, targets_ref[...].astype(jnp.float32), 0.0), axis=1, keepdims=True).astype(jnp.int32)
    lane = lax.broadcasted_iota(jnp.int32, (SLOTS, AUX), 1)
    own = target[:SLOTS]
    digits = jnp.where(lane == 0, own & 127, 0)
    digits = jnp.where(lane == 1, (own >> 7) & 127, digits)
    digits = jnp.where(lane == 2, own >> 14, digits)
    digits = jnp.where(lane == 3, ratio_ref[0], digits)
    keep_ref[...] = rows[:SLOTS]
    aux_ref[...] = digits.astype(jnp.float32).astype(jnp.bfloat16)
    give_ref[...] = rows[SLOTS:]


def slot_dest(counts_ref, slot_index, core):
    slot = slot_index & (SLOTS - 1)
    dest = jnp.full_like(slot_index, -1)
    start = jnp.int32(0)
    for i in range(SEQS):
        end = start + counts_ref[i]
        first = first_row(start, core)
        mine = ((slot_index >> 5) == i) & (first + 2 * slot < end)
        dest = jnp.where(mine, (first >> 1) + slot, dest)
        start = end
    return dest


def fetch(weight_ref, held_ref, sem):
    copy = pltpu.make_async_copy(weight_ref, held_ref, sem)
    copy.start()
    copy.wait()


def pack_rows(counts_ref, slots_ref, low_ref, high_ref, row_ref):
    core = lax.axis_index("c")
    dest = slot_dest(counts_ref, lax.broadcasted_iota(jnp.int32, (1, SEQS * SLOTS), 1), core)
    at = lax.broadcasted_iota(jnp.int32, (ROWS, SEQS * SLOTS), 0)
    pick = jnp.where(at == dest, 1.0, 0.0).astype(jnp.bfloat16)
    packed = jnp.dot(pick, slots_ref[...], preferred_element_type=jnp.float32)
    feat = (slots_ref.shape[1] - AUX) // 2
    own, near = packed[:, :feat], packed[:, feat:2 * feat]
    for at, part in ((0, jnp.where(core == 0, own, near)), (feat, jnp.where(core == 0, near, own))):
        part = part.astype(jnp.bfloat16)
        low_ref[:, at:at + feat] = part[:CHUNK]
        high_ref[:, at:at + feat] = part[CHUNK:]
    digits = jnp.transpose(packed[:, 2 * feat:])
    row_ref[0:1] = digits[0:1] + 128.0 * digits[1:2] + 16384.0 * digits[2:3]
    row_ref[1:2] = weight_scale / digits[3:4]


def features_of(away, span):
    return pl.ds(pl.multiple_of(((lax.axis_index("z") + away) & (DEEP - 1)) * span, span), span)


def score_rows(own_ref, near_ref, *refs):
    chunks, (own_scores_ref, near_scores_ref, stats_ref, rows) = refs[:2 * DEEP], refs[2 * DEEP:]
    count = own_ref.shape[0]
    for away in range(DEEP):
        features = features_of(away, chunks[0].shape[1])
        rows[:CHUNK, features] = chunks[2 * away][...]
        rows[CHUNK:, features] = chunks[2 * away + 1][...]
    for w_ref, ref in ((own_ref, own_scores_ref), (near_ref, near_scores_ref)):
        ref[:count] = lax.dot_general(w_ref[...], rows[...], NT, preferred_element_type=jnp.float32)
    at = lax.broadcasted_iota(jnp.int32, own_scores_ref.shape, 0)
    parts = [jnp.where(at < count, ref[...], -jnp.inf) for ref in (own_scores_ref, near_scores_ref)]
    own_scores_ref[...], near_scores_ref[...] = parts
    top = jnp.maximum(*[jnp.max(part, axis=0, keepdims=True) for part in parts])
    total = sum(jnp.sum(jnp.exp(part - top), axis=0, keepdims=True) for part in parts)
    stats = jnp.concatenate([top, total], axis=0)
    stats_ref[...] = jnp.broadcast_to(stats[None], stats_ref.shape)


def grad_rows(aways, own_slope_ref, near_slope_ref, own_ref, near_ref, *sums_refs):
    count = own_ref.shape[0]
    for i, away in enumerate(aways):
        features = features_of(away, sums_refs[0].shape[1])
        sums = jnp.dot(own_slope_ref[:, :count], own_ref[:, features], preferred_element_type=jnp.float32)
        sums += jnp.dot(near_slope_ref[:, :count], near_ref[:, features], preferred_element_type=jnp.float32)
        sums = sums * SENT_SCALE
        sums_refs[2 * i][...] = sums[:CHUNK]
        sums_refs[2 * i + 1][...] = sums[CHUNK:]


def slope_rows(aways, stats_ref, row_ref, own_scores_ref, near_scores_ref, own_ref, near_ref, own_slope_ref, near_slope_ref, *sums_refs):
    count = own_ref.shape[0]
    tops = stats_ref[:, 0, :]
    top = jnp.max(tops, axis=0, keepdims=True)
    total = jnp.sum(stats_ref[:, 1, :] * jnp.exp(tops - top), axis=0, keepdims=True)
    chip = chip_index() * DEEP + lax.axis_index("z")
    core = lax.axis_index("c")
    target = row_ref[0:1].astype(jnp.int32)
    at = lax.broadcasted_iota(jnp.int32, own_scores_ref.shape, 0)
    for ref, out, of_core in ((own_scores_ref, own_slope_ref, core), (near_scores_ref, near_slope_ref, 1 - core)):
        local_target = target - (chip * 2 + of_core) * count
        probs = jnp.exp(ref[...] - top) / total
        onehot = jnp.where((at == local_target) & (at < count), 1.0, 0.0)
        out[...] = jnp.transpose(row_ref[1:2] * (probs - onehot)).astype(jnp.bfloat16)
    grad_rows(aways, own_slope_ref, near_slope_ref, own_ref, near_ref, *sums_refs)


def spread_rows(counts_ref, low_ref, high_ref, slots_ref):
    dest = slot_dest(counts_ref, lax.broadcasted_iota(jnp.int32, (SEQS * SLOTS, 1), 0), lax.axis_index("c"))
    at = lax.broadcasted_iota(jnp.int32, (SEQS * SLOTS, ROWS), 1)
    pick = jnp.where(at == dest, 1.0, 0.0).astype(jnp.bfloat16)
    rest = jnp.concatenate([low_ref[...], high_ref[...]], axis=0)
    part = rest.astype(jnp.bfloat16)
    rest = (rest - part.astype(jnp.float32)).astype(jnp.bfloat16)
    slots = jnp.dot(pick, part, preferred_element_type=jnp.float32)
    slots_ref[...] = slots + jnp.dot(pick, rest, preferred_element_type=jnp.float32)


def place_rows(places_ref, kept_ref, got_ref, out_ref):
    length = out_ref.shape[0]
    at = lax.broadcasted_iota(jnp.int32, (length, 2 * SLOTS), 0)
    hit = jnp.where(at == places_ref[0:1], 1.0, 0.0).astype(jnp.bfloat16)
    rest = jnp.concatenate([kept_ref[...], got_ref[...]], axis=0)
    out = None
    for _ in range(3):
        part = rest.astype(jnp.bfloat16)
        rest = rest - part.astype(jnp.float32)
        part = jnp.dot(hit, part, preferred_element_type=jnp.float32)
        out = part if out is None else out + part
    out_ref[...] = out


def swap_cores(x):
    return lax.ppermute(x, "c", [(0, 1), (1, 0)])


def pass_on(x, by):
    return lax.ppermute(x, "z", [(i, (i + by) % DEEP) for i in range(DEEP)])


def gather_chips(low, high):
    lows, highs = {0: low}, {0: high}
    for hop in range(1, DEEP // 2 + 1):
        lows[-hop] = pass_on(lows[1 - hop], 1)
        highs[hop] = pass_on(highs[hop - 1], -1)
        if hop < DEEP // 2:
            highs[-hop] = pass_on(highs[1 - hop], 1)
            lows[hop] = pass_on(lows[hop - 1], -1)
    lows[DEEP // 2] = lows[-(DEEP // 2)]
    return [chunk for away in range(DEEP) for chunk in (lows[(away + 3) % DEEP - 3], highs[(away + 3) % DEEP - 3])]


def reduce_chips(lows, highs):
    def send(x, by):
        return pass_on(x.astype(jnp.float16), by).astype(jnp.float32)

    half = DEEP // 2
    low_right, high_left = lows[half], highs[half]
    low_left, high_right = lows[half + 1], highs[half - 1]
    for hop in range(1, half):
        low_right = send(low_right, 1) + lows[half - hop]
        high_left = send(high_left, -1) + highs[half + hop]
        if hop < half - 1:
            low_left = send(low_left, -1) + lows[half + 1 + hop]
            high_right = send(high_right, 1) + highs[half - 1 - hop]
    low = lows[0] + send(low_left, -1) + send(low_right, 1)
    high = highs[0] + send(high_right, 1) + send(high_left, -1)
    return low, high


def local(hidden, mask_positions, counts, targets, mask_ratio, own_weight):
    c = lax.axis_index("c")
    vocab_dev = own_weight.shape[1]
    wide = -(-vocab_dev // 128) * 128
    length, feat = hidden.shape[1:]
    span = 2 * feat
    smem = pl.BlockSpec(memory_space=pltpu.SMEM)
    vmem = pl.BlockSpec(memory_space=pltpu.VMEM)
    params = pltpu.CompilerParams(vmem_limit_bytes=20 << 20)
    shape = jax.ShapeDtypeStruct

    keep, aux, give, places = pl.pallas_call(
        own_rows,
        out_shape=(
            shape((SLOTS, feat), jnp.bfloat16),
            shape((SLOTS, AUX), jnp.bfloat16),
            shape((SLOTS, feat), jnp.bfloat16),
            shape((8, 2 * SLOTS), jnp.int32),
        ),
        in_specs=[smem, smem, vmem, vmem, vmem],
        out_specs=(vmem,) * 4,
    )(counts, mask_ratio, mask_positions, targets, hidden[0])
    got = swap_cores(give)

    slots = jnp.concatenate([keep, got, aux], axis=1)
    slots, own_weight = lax.optimization_barrier((slots, own_weight))
    near_weight = swap_cores(own_weight)
    own_t, near_t = own_weight.T, near_weight.T
    slots = lax.all_to_all(jnp.broadcast_to(slots[None], (SEQS,) + slots.shape), PLANE, 0, 0, tiled=True)
    own_t = pl.pallas_call(
        fetch,
        out_shape=shape(own_t.shape, own_t.dtype),
        in_specs=[pl.BlockSpec(memory_space=pltpu.HBM)],
        out_specs=vmem,
        scratch_shapes=[pltpu.SemaphoreType.DMA],
        cost_estimate=pl.CostEstimate(flops=0, bytes_accessed=8 << 20, transcendentals=0),
    )(own_t)
    slots, own_t = lax.optimization_barrier((slots, own_t))
    low, high, row_data = pl.pallas_call(
        pack_rows,
        out_shape=(
            shape((CHUNK, span), jnp.bfloat16),
            shape((CHUNK, span), jnp.bfloat16),
            shape((2, ROWS), jnp.float32),
        ),
        in_specs=[smem, vmem],
        out_specs=(vmem,) * 3,
    )(counts, slots.reshape(SEQS * SLOTS, span + AUX))

    chunks = gather_chips(low, high)
    own_scores, near_scores, stats = pl.pallas_call(
        score_rows,
        out_shape=(
            shape((wide, ROWS), jnp.float32),
            shape((wide, ROWS), jnp.float32),
            shape((SEQS * DEEP, 2, ROWS), jnp.float32),
        ),
        in_specs=[vmem] * (2 + 2 * DEEP),
        out_specs=(vmem,) * 3,
        scratch_shapes=[pltpu.VMEM((ROWS, DEEP * span), jnp.bfloat16)],
        compiler_params=params,
    )(own_t, near_t, *chunks)

    stats = lax.all_to_all(stats, CHIPS, 0, 0, tiled=True)
    early, late = (3, 4, 5), (2, 6, 1, 7, 0)
    sums_shape = shape((CHUNK, span), jnp.float32)
    slope_shape = shape((ROWS, wide), jnp.bfloat16)
    own_slope, near_slope, *sums = pl.pallas_call(
        functools.partial(slope_rows, early),
        out_shape=(slope_shape, slope_shape) + (sums_shape,) * (2 * len(early)),
        in_specs=[vmem] * 6,
        out_specs=(vmem,) * (2 + 2 * len(early)),
        compiler_params=params,
    )(stats, row_data, own_scores, near_scores, own_t, near_t)
    sums += pl.pallas_call(
        functools.partial(grad_rows, late),
        out_shape=(sums_shape,) * (2 * len(late)),
        in_specs=[vmem] * 4,
        out_specs=(vmem,) * (2 * len(late)),
        compiler_params=params,
        cost_estimate=pl.CostEstimate(
            flops=4 * ROWS * vocab_dev * span * len(late), bytes_accessed=8 << 20, transcendentals=0
        ),
    )(own_slope, near_slope, own_t, near_t)
    lows = dict(zip(early + late, sums[::2]))
    highs = dict(zip(early + late, sums[1::2]))

    low, high = reduce_chips(lows, highs)
    back = pl.pallas_call(
        spread_rows,
        out_shape=shape((SEQS * SLOTS, span), jnp.float32),
        in_specs=[smem, vmem, vmem],
        out_specs=vmem,
    )(counts, low, high)
    back = back.astype(jnp.float16).reshape(SEQS, SLOTS, span)
    back = lax.all_to_all(back, PLANE, 0, 0, tiled=True)
    back = jnp.sum(back.astype(jnp.float32), axis=0) * (1.0 / SENT_SCALE)
    kept = jnp.where(c == 0, back[:, :feat], back[:, feat:])
    given = jnp.where(c == 0, back[:, feat:], back[:, :feat])
    grad = pl.pallas_call(
        place_rows,
        out_shape=shape((length, feat), jnp.float32),
        in_specs=[vmem] * 3,
        out_specs=vmem,
    )(places, kept, swap_cores(given))
    return grad[None]


def solution(mesh):
    fine = Mesh(mesh.devices.reshape(SIDE, SIDE, DEEP, 2), CHIPS + ("c",))
    vocab = ("z", "c")
    return jax.shard_map(
        local,
        mesh=fine,
        in_specs=(
            P(PLANE, None, vocab),
            P(PLANE, None),
            P(),
            P(PLANE, None),
            P(PLANE),
            P(None, CHIPS + ("c",)),
        ),
        out_specs=P(PLANE, None, vocab),
        check_vma=False,
    )
```

```python
import functools

import jax
import jax.numpy as jnp
from jax import lax
from jax.experimental import pallas as pl
from jax.experimental.pallas import tpu as pltpu
from jax.sharding import Mesh
from jax.sharding import PartitionSpec as P

weight_scale = 4.0
SIDE = 4
DEEP = 8
SEQS = SIDE * SIDE
SLOTS = 32
ROWS = 256
CHUNK = ROWS // 2
AUX = 128
PLANE = ("y", "x")
CHIPS = ("y", "x", "z")
NT = (((1,), (1,)), ((), ()))
SENT_SCALE = 4096.0


def chip_index():
    return lax.axis_index("y") * SIDE + lax.axis_index("x")


def first_row(start, core):
    return start + ((start + core) & 1)


def own_rows(counts_ref, ratio_ref, positions_ref, targets_ref, hidden_ref, keep_ref, aux_ref, give_ref, places_ref):
    seq = chip_index()
    core = lax.axis_index("c")
    start = jnp.int32(0)
    count = jnp.int32(0)
    for i in range(SEQS):
        start = start + jnp.where(i < seq, counts_ref[i], 0)
        count = count + jnp.where(i == seq, counts_ref[i], 0)
    length = hidden_ref.shape[0]
    q = lax.broadcasted_iota(jnp.int32, (2 * SLOTS, 1), 0)
    index = jnp.where(q < SLOTS, first_row(start, core), first_row(start, 1 - core)) - start + 2 * (q & (SLOTS - 1))
    valid = index < count
    at = lax.broadcasted_iota(jnp.int32, (2 * SLOTS, 128), 1)
    near = jnp.where(at == index, positions_ref[:, :128].astype(jnp.float32), 0.0)
    places = jnp.where(valid, jnp.sum(near, axis=1, keepdims=True), -1.0)
    places_ref[...] = jnp.transpose(jnp.broadcast_to(places, (2 * SLOTS, 128)))[:8].astype(jnp.int32)
    at = lax.broadcasted_iota(jnp.int32, (2 * SLOTS, length), 1)
    hit = at == places.astype(jnp.int32)
    rows = jnp.dot(jnp.where(hit, 1.0, 0.0).astype(jnp.bfloat16), hidden_ref[...], preferred_element_type=jnp.float32)
    rows = rows.astype(jnp.bfloat16)
    target = jnp.sum(jnp.where(hit, targets_ref[...].astype(jnp.float32), 0.0), axis=1, keepdims=True).astype(jnp.int32)
    lane = lax.broadcasted_iota(jnp.int32, (SLOTS, AUX), 1)
    own = target[:SLOTS]
    digits = jnp.where(lane == 0, own & 127, 0)
    digits = jnp.where(lane == 1, (own >> 7) & 127, digits)
    digits = jnp.where(lane == 2, own >> 14, digits)
    digits = jnp.where(lane == 3, ratio_ref[0], digits)
    keep_ref[...] = rows[:SLOTS]
    aux_ref[...] = digits.astype(jnp.float32).astype(jnp.bfloat16)
    give_ref[...] = rows[SLOTS:]


def slot_dest(counts_ref, slot_index, core):
    slot = slot_index & (SLOTS - 1)
    dest = jnp.full_like(slot_index, -1)
    start = jnp.int32(0)
    for i in range(SEQS):
        end = start + counts_ref[i]
        first = first_row(start, core)
        mine = ((slot_index >> 5) == i) & (first + 2 * slot < end)
        dest = jnp.where(mine, (first >> 1) + slot, dest)
        start = end
    return dest


def fetch(weight_ref, held_ref, sem):
    copy = pltpu.make_async_copy(weight_ref, held_ref, sem)
    copy.start()
    copy.wait()


def pack_rows(counts_ref, slots_ref, low_ref, high_ref, row_ref):
    core = lax.axis_index("c")
    dest = slot_dest(counts_ref, lax.broadcasted_iota(jnp.int32, (1, SEQS * SLOTS), 1), core)
    at = lax.broadcasted_iota(jnp.int32, (ROWS, SEQS * SLOTS), 0)
    pick = jnp.where(at == dest, 1.0, 0.0).astype(jnp.bfloat16)
    packed = jnp.dot(pick, slots_ref[...], preferred_element_type=jnp.float32)
    feat = (slots_ref.shape[1] - AUX) // 2
    own, near = packed[:, :feat], packed[:, feat:2 * feat]
    for at, part in ((0, jnp.where(core == 0, own, near)), (feat, jnp.where(core == 0, near, own))):
        part = part.astype(jnp.bfloat16)
        low_ref[:, at:at + feat] = part[:CHUNK]
        high_ref[:, at:at + feat] = part[CHUNK:]
    digits = jnp.transpose(packed[:, 2 * feat:])
    row_ref[0:1] = digits[0:1] + 128.0 * digits[1:2] + 16384.0 * digits[2:3]
    row_ref[1:2] = weight_scale / digits[3:4]


def features_of(away, span):
    return pl.ds(pl.multiple_of(((lax.axis_index("z") + away) & (DEEP - 1)) * span, span), span)


def score_rows(own_ref, near_ref, *refs):
    chunks, (own_scores_ref, near_scores_ref, stats_ref, rows) = refs[:2 * DEEP], refs[2 * DEEP:]
    count = own_ref.shape[0]
    for away in range(DEEP):
        features = features_of(away, chunks[0].shape[1])
        rows[:CHUNK, features] = chunks[2 * away][...]
        rows[CHUNK:, features] = chunks[2 * away + 1][...]
    for w_ref, ref in ((own_ref, own_scores_ref), (near_ref, near_scores_ref)):
        ref[:count] = lax.dot_general(w_ref[...], rows[...], NT, preferred_element_type=jnp.float32)
    at = lax.broadcasted_iota(jnp.int32, own_scores_ref.shape, 0)
    parts = [jnp.where(at < count, ref[...], -jnp.inf) for ref in (own_scores_ref, near_scores_ref)]
    own_scores_ref[...], near_scores_ref[...] = parts
    top = jnp.maximum(*[jnp.max(part, axis=0, keepdims=True) for part in parts])
    total = sum(jnp.sum(jnp.exp(part - top), axis=0, keepdims=True) for part in parts)
    stats = jnp.concatenate([top, total], axis=0)
    stats_ref[...] = jnp.broadcast_to(stats[None], stats_ref.shape)


def grad_rows(aways, own_slope_ref, near_slope_ref, own_ref, near_ref, *sums_refs):
    count = own_ref.shape[0]
    for i, away in enumerate(aways):
        features = features_of(away, sums_refs[0].shape[1])
        sums = jnp.dot(own_slope_ref[:, :count], own_ref[:, features], preferred_element_type=jnp.float32)
        sums += jnp.dot(near_slope_ref[:, :count], near_ref[:, features], preferred_element_type=jnp.float32)
        sums = sums * SENT_SCALE
        sums_refs[2 * i][...] = sums[:CHUNK]
        sums_refs[2 * i + 1][...] = sums[CHUNK:]


def slope_rows(aways, stats_ref, row_ref, own_scores_ref, near_scores_ref, own_ref, near_ref, own_slope_ref, near_slope_ref, *sums_refs):
    count = own_ref.shape[0]
    tops = stats_ref[:, 0, :]
    top = jnp.max(tops, axis=0, keepdims=True)
    total = jnp.sum(stats_ref[:, 1, :] * jnp.exp(tops - top), axis=0, keepdims=True)
    chip = chip_index() * DEEP + lax.axis_index("z")
    core = lax.axis_index("c")
    target = row_ref[0:1].astype(jnp.int32)
    at = lax.broadcasted_iota(jnp.int32, own_scores_ref.shape, 0)
    for ref, out, of_core in ((own_scores_ref, own_slope_ref, core), (near_scores_ref, near_slope_ref, 1 - core)):
        local_target = target - (chip * 2 + of_core) * count
        probs = jnp.exp(ref[...] - top) / total
        onehot = jnp.where((at == local_target) & (at < count), 1.0, 0.0)
        out[...] = jnp.transpose(row_ref[1:2] * (probs - onehot)).astype(jnp.bfloat16)
    grad_rows(aways, own_slope_ref, near_slope_ref, own_ref, near_ref, *sums_refs)


def spread_rows(counts_ref, low_ref, high_ref, slots_ref):
    dest = slot_dest(counts_ref, lax.broadcasted_iota(jnp.int32, (SEQS * SLOTS, 1), 0), lax.axis_index("c"))
    at = lax.broadcasted_iota(jnp.int32, (SEQS * SLOTS, ROWS), 1)
    pick = jnp.where(at == dest, 1.0, 0.0).astype(jnp.bfloat16)
    rest = jnp.concatenate([low_ref[...], high_ref[...]], axis=0)
    part = rest.astype(jnp.bfloat16)
    rest = (rest - part.astype(jnp.float32)).astype(jnp.bfloat16)
    slots = jnp.dot(pick, part, preferred_element_type=jnp.float32)
    slots_ref[...] = slots + jnp.dot(pick, rest, preferred_element_type=jnp.float32)


def place_rows(places_ref, kept_ref, got_ref, out_ref):
    length = out_ref.shape[0]
    at = lax.broadcasted_iota(jnp.int32, (length, 2 * SLOTS), 0)
    hit = jnp.where(at == places_ref[0:1], 1.0, 0.0).astype(jnp.bfloat16)
    rest = jnp.concatenate([kept_ref[...], got_ref[...]], axis=0)
    out = None
    for _ in range(3):
        part = rest.astype(jnp.bfloat16)
        rest = rest - part.astype(jnp.float32)
        part = jnp.dot(hit, part, preferred_element_type=jnp.float32)
        out = part if out is None else out + part
    out_ref[...] = out


def swap_cores(x):
    return lax.ppermute(x, "c", [(0, 1), (1, 0)])


def pass_on(x, by):
    return lax.ppermute(x, "z", [(i, (i + by) % DEEP) for i in range(DEEP)])


def gather_chips(low, high):
    lows, highs = {0: low}, {0: high}
    for hop in range(1, DEEP // 2 + 1):
        lows[-hop] = pass_on(lows[1 - hop], 1)
        highs[hop] = pass_on(highs[hop - 1], -1)
        if hop < DEEP // 2:
            highs[-hop] = pass_on(highs[1 - hop], 1)
            lows[hop] = pass_on(lows[hop - 1], -1)
    lows[DEEP // 2] = lows[-(DEEP // 2)]
    return [chunk for away in range(DEEP) for chunk in (lows[(away + 3) % DEEP - 3], highs[(away + 3) % DEEP - 3])]


def reduce_chips(lows, highs):
    def send(x, by):
        return pass_on(x.astype(jnp.float16), by).astype(jnp.float32)

    half = DEEP // 2
    low_right, high_left = lows[half], highs[half]
    low_left, high_right = lows[half + 1], highs[half - 1]
    for hop in range(1, half):
        low_right = send(low_right, 1) + lows[half - hop]
        high_left = send(high_left, -1) + highs[half + hop]
        if hop < half - 1:
            low_left = send(low_left, -1) + lows[half + 1 + hop]
            high_right = send(high_right, 1) + highs[half - 1 - hop]
    low = lows[0] + send(low_left, -1) + send(low_right, 1)
    high = highs[0] + send(high_right, 1) + send(high_left, -1)
    return low, high


def local(hidden, mask_positions, counts, targets, mask_ratio, own_weight):
    c = lax.axis_index("c")
    vocab_dev = own_weight.shape[1]
    wide = -(-vocab_dev // 128) * 128
    length, feat = hidden.shape[1:]
    span = 2 * feat
    smem = pl.BlockSpec(memory_space=pltpu.SMEM)
    vmem = pl.BlockSpec(memory_space=pltpu.VMEM)
    params = pltpu.CompilerParams(vmem_limit_bytes=20 << 20)
    small = pltpu.CompilerParams(vmem_limit_bytes=8 << 20)
    shape = jax.ShapeDtypeStruct

    keep, aux, give, places = pl.pallas_call(
        own_rows,
        out_shape=(
            shape((SLOTS, feat), jnp.bfloat16),
            shape((SLOTS, AUX), jnp.bfloat16),
            shape((SLOTS, feat), jnp.bfloat16),
            shape((8, 2 * SLOTS), jnp.int32),
        ),
        in_specs=[smem, smem, vmem, vmem, vmem],
        out_specs=(vmem,) * 4,
        compiler_params=small,
    )(counts, mask_ratio, mask_positions, targets, hidden[0])
    got = swap_cores(give)

    slots = jnp.concatenate([keep, got, aux], axis=1)
    slots, own_weight = lax.optimization_barrier((slots, own_weight))
    near_weight = swap_cores(own_weight)
    own_t, near_t = own_weight.T, near_weight.T
    slots = lax.all_to_all(jnp.broadcast_to(slots[None], (SEQS,) + slots.shape), PLANE, 0, 0, tiled=True)
    own_t = pl.pallas_call(
        fetch,
        out_shape=shape(own_t.shape, own_t.dtype),
        in_specs=[pl.BlockSpec(memory_space=pltpu.HBM)],
        out_specs=vmem,
        scratch_shapes=[pltpu.SemaphoreType.DMA],
        compiler_params=small,
        cost_estimate=pl.CostEstimate(flops=0, bytes_accessed=8 << 20, transcendentals=0),
    )(own_t)
    slots, own_t = lax.optimization_barrier((slots, own_t))
    low, high, row_data = pl.pallas_call(
        pack_rows,
        out_shape=(
            shape((CHUNK, span), jnp.bfloat16),
            shape((CHUNK, span), jnp.bfloat16),
            shape((2, ROWS), jnp.float32),
        ),
        in_specs=[smem, vmem],
        out_specs=(vmem,) * 3,
        compiler_params=small,
    )(counts, slots.reshape(SEQS * SLOTS, span + AUX))

    chunks = gather_chips(low, high)
    own_scores, near_scores, stats = pl.pallas_call(
        score_rows,
        out_shape=(
            shape((wide, ROWS), jnp.float32),
            shape((wide, ROWS), jnp.float32),
            shape((SEQS * DEEP, 2, ROWS), jnp.float32),
        ),
        in_specs=[vmem] * (2 + 2 * DEEP),
        out_specs=(vmem,) * 3,
        scratch_shapes=[pltpu.VMEM((ROWS, DEEP * span), jnp.bfloat16)],
        compiler_params=params,
    )(own_t, near_t, *chunks)

    stats = lax.all_to_all(stats, CHIPS, 0, 0, tiled=True)
    parts = (4,), (3, 5), (2, 6, 1, 7, 0)
    sums_shape = shape((CHUNK, span), jnp.float32)
    slope_shape = shape((ROWS, wide), jnp.bfloat16)
    own_slope, near_slope, *sums = pl.pallas_call(
        functools.partial(slope_rows, parts[0]),
        out_shape=(slope_shape, slope_shape) + (sums_shape,) * (2 * len(parts[0])),
        in_specs=[vmem] * 6,
        out_specs=(vmem,) * (2 + 2 * len(parts[0])),
        compiler_params=params,
    )(stats, row_data, own_scores, near_scores, own_t, near_t)
    for part in parts[1:]:
        sums += pl.pallas_call(
            functools.partial(grad_rows, part),
            out_shape=(sums_shape,) * (2 * len(part)),
            in_specs=[vmem] * 4,
            out_specs=(vmem,) * (2 * len(part)),
            compiler_params=params,
            cost_estimate=pl.CostEstimate(
                flops=4 * ROWS * vocab_dev * span * len(part), bytes_accessed=2 * len(part) << 20, transcendentals=0
            ),
        )(own_slope, near_slope, own_t, near_t)
    lows = dict(zip(sum(parts, ()), sums[::2]))
    highs = dict(zip(sum(parts, ()), sums[1::2]))

    low, high = reduce_chips(lows, highs)
    back = pl.pallas_call(
        spread_rows,
        out_shape=shape((SEQS * SLOTS, span), jnp.float32),
        in_specs=[smem, vmem, vmem],
        out_specs=vmem,
        compiler_params=small,
    )(counts, low, high)
    back = back.astype(jnp.float16).reshape(SEQS, SLOTS, span)
    back = lax.all_to_all(back, PLANE, 0, 0, tiled=True)
    back = jnp.sum(back.astype(jnp.float32), axis=0) * (1.0 / SENT_SCALE)
    kept = jnp.where(c == 0, back[:, :feat], back[:, feat:])
    given = jnp.where(c == 0, back[:, feat:], back[:, :feat])
    grad = pl.pallas_call(
        place_rows,
        out_shape=shape((length, feat), jnp.float32),
        in_specs=[vmem] * 3,
        out_specs=vmem,
        compiler_params=small,
    )(places, kept, swap_cores(given))
    return grad[None]


def solution(mesh):
    fine = Mesh(mesh.devices.reshape(SIDE, SIDE, DEEP, 2), CHIPS + ("c",))
    vocab = ("z", "c")
    return jax.shard_map(
        local,
        mesh=fine,
        in_specs=(
            P(PLANE, None, vocab),
            P(PLANE, None),
            P(),
            P(PLANE, None),
            P(PLANE),
            P(None, CHIPS + ("c",)),
        ),
        out_specs=P(PLANE, None, vocab),
        check_vma=False,
    )
```

```python
import functools

import jax
import jax.numpy as jnp
from jax import lax
from jax.experimental import pallas as pl
from jax.experimental.pallas import tpu as pltpu
from jax.sharding import Mesh
from jax.sharding import PartitionSpec as P

weight_scale = 4.0
SIDE = 4
DEEP = 8
SEQS = SIDE * SIDE
SLOTS = 32
ROWS = 256
CHUNK = ROWS // 2
AUX = 128
PLANE = ("y", "x")
CHIPS = ("y", "x", "z")
NT = (((1,), (1,)), ((), ()))
SENT_SCALE = 4096.0


def chip_index():
    return lax.axis_index("y") * SIDE + lax.axis_index("x")


def first_row(start, core):
    return start + ((start + core) & 1)


def own_rows(counts_ref, ratio_ref, positions_ref, targets_ref, hidden_ref, keep_ref, aux_ref, give_ref, places_ref):
    seq = chip_index()
    core = lax.axis_index("c")
    start = jnp.int32(0)
    count = jnp.int32(0)
    for i in range(SEQS):
        start = start + jnp.where(i < seq, counts_ref[i], 0)
        count = count + jnp.where(i == seq, counts_ref[i], 0)
    length = hidden_ref.shape[0]
    q = lax.broadcasted_iota(jnp.int32, (2 * SLOTS, 1), 0)
    index = jnp.where(q < SLOTS, first_row(start, core), first_row(start, 1 - core)) - start + 2 * (q & (SLOTS - 1))
    valid = index < count
    at = lax.broadcasted_iota(jnp.int32, (2 * SLOTS, 128), 1)
    near = jnp.where(at == index, positions_ref[:, :128].astype(jnp.float32), 0.0)
    places = jnp.where(valid, jnp.sum(near, axis=1, keepdims=True), -1.0)
    places_ref[...] = jnp.transpose(jnp.broadcast_to(places, (2 * SLOTS, 128)))[:8].astype(jnp.int32)
    at = lax.broadcasted_iota(jnp.int32, (2 * SLOTS, length), 1)
    hit = at == places.astype(jnp.int32)
    rows = jnp.dot(jnp.where(hit, 1.0, 0.0).astype(jnp.bfloat16), hidden_ref[...], preferred_element_type=jnp.float32)
    rows = rows.astype(jnp.bfloat16)
    target = jnp.sum(jnp.where(hit, targets_ref[...].astype(jnp.float32), 0.0), axis=1, keepdims=True).astype(jnp.int32)
    lane = lax.broadcasted_iota(jnp.int32, (SLOTS, AUX), 1)
    own = target[:SLOTS]
    digits = jnp.where(lane == 0, own & 127, 0)
    digits = jnp.where(lane == 1, (own >> 7) & 127, digits)
    digits = jnp.where(lane == 2, own >> 14, digits)
    digits = jnp.where(lane == 3, ratio_ref[0], digits)
    keep_ref[...] = rows[:SLOTS]
    aux_ref[...] = digits.astype(jnp.float32).astype(jnp.bfloat16)
    give_ref[...] = rows[SLOTS:]


def slot_dest(counts_ref, slot_index, core):
    slot = slot_index & (SLOTS - 1)
    dest = jnp.full_like(slot_index, -1)
    start = jnp.int32(0)
    for i in range(SEQS):
        end = start + counts_ref[i]
        first = first_row(start, core)
        mine = ((slot_index >> 5) == i) & (first + 2 * slot < end)
        dest = jnp.where(mine, (first >> 1) + slot, dest)
        start = end
    return dest


def pack_rows(counts_ref, slots_ref, low_ref, high_ref, row_ref):
    core = lax.axis_index("c")
    dest = slot_dest(counts_ref, lax.broadcasted_iota(jnp.int32, (1, SEQS * SLOTS), 1), core)
    at = lax.broadcasted_iota(jnp.int32, (ROWS, SEQS * SLOTS), 0)
    pick = jnp.where(at == dest, 1.0, 0.0).astype(jnp.bfloat16)
    packed = jnp.dot(pick, slots_ref[...], preferred_element_type=jnp.float32)
    feat = (slots_ref.shape[1] - AUX) // 2
    own, near = packed[:, :feat], packed[:, feat:2 * feat]
    for at, part in ((0, jnp.where(core == 0, own, near)), (feat, jnp.where(core == 0, near, own))):
        part = part.astype(jnp.bfloat16)
        low_ref[:, at:at + feat] = part[:CHUNK]
        high_ref[:, at:at + feat] = part[CHUNK:]
    digits = jnp.transpose(packed[:, 2 * feat:])
    row_ref[0:1] = digits[0:1] + 128.0 * digits[1:2] + 16384.0 * digits[2:3]
    row_ref[1:2] = weight_scale / digits[3:4]


def features_of(away, span):
    return pl.ds(pl.multiple_of(((lax.axis_index("z") + away) & (DEEP - 1)) * span, span), span)


def score_rows(own_ref, near_ref, *refs):
    chunks, (own_scores_ref, near_scores_ref, stats_ref, rows) = refs[:2 * DEEP], refs[2 * DEEP:]
    count = own_ref.shape[0]
    for away in range(DEEP):
        features = features_of(away, chunks[0].shape[1])
        rows[:CHUNK, features] = chunks[2 * away][...]
        rows[CHUNK:, features] = chunks[2 * away + 1][...]
    for w_ref, ref in ((own_ref, own_scores_ref), (near_ref, near_scores_ref)):
        ref[:count] = lax.dot_general(w_ref[...], rows[...], NT, preferred_element_type=jnp.float32)
    at = lax.broadcasted_iota(jnp.int32, own_scores_ref.shape, 0)
    parts = [jnp.where(at < count, ref[...], -jnp.inf) for ref in (own_scores_ref, near_scores_ref)]
    own_scores_ref[...], near_scores_ref[...] = parts
    top = jnp.maximum(*[jnp.max(part, axis=0, keepdims=True) for part in parts])
    total = sum(jnp.sum(jnp.exp(part - top), axis=0, keepdims=True) for part in parts)
    stats = jnp.concatenate([top, total], axis=0)
    stats_ref[...] = jnp.broadcast_to(stats[None], stats_ref.shape)


def grad_rows(aways, own_slope_ref, near_slope_ref, own_ref, near_ref, *sums_refs):
    count = own_ref.shape[0]
    for i, away in enumerate(aways):
        features = features_of(away, sums_refs[0].shape[1])
        sums = jnp.dot(own_slope_ref[:, :count], own_ref[:, features], preferred_element_type=jnp.float32)
        sums += jnp.dot(near_slope_ref[:, :count], near_ref[:, features], preferred_element_type=jnp.float32)
        sums = sums * SENT_SCALE
        sums_refs[2 * i][...] = sums[:CHUNK]
        sums_refs[2 * i + 1][...] = sums[CHUNK:]


def slope_rows(aways, stats_ref, row_ref, own_scores_ref, near_scores_ref, own_ref, near_ref, own_slope_ref, near_slope_ref, *sums_refs):
    count = own_ref.shape[0]
    tops = stats_ref[:, 0, :]
    top = jnp.max(tops, axis=0, keepdims=True)
    total = jnp.sum(stats_ref[:, 1, :] * jnp.exp(tops - top), axis=0, keepdims=True)
    chip = chip_index() * DEEP + lax.axis_index("z")
    core = lax.axis_index("c")
    target = row_ref[0:1].astype(jnp.int32)
    at = lax.broadcasted_iota(jnp.int32, own_scores_ref.shape, 0)
    for ref, out, of_core in ((own_scores_ref, own_slope_ref, core), (near_scores_ref, near_slope_ref, 1 - core)):
        local_target = target - (chip * 2 + of_core) * count
        probs = jnp.exp(ref[...] - top) / total
        onehot = jnp.where((at == local_target) & (at < count), 1.0, 0.0)
        out[...] = jnp.transpose(row_ref[1:2] * (probs - onehot)).astype(jnp.bfloat16)
    grad_rows(aways, own_slope_ref, near_slope_ref, own_ref, near_ref, *sums_refs)


def spread_rows(counts_ref, low_ref, high_ref, slots_ref):
    dest = slot_dest(counts_ref, lax.broadcasted_iota(jnp.int32, (SEQS * SLOTS, 1), 0), lax.axis_index("c"))
    at = lax.broadcasted_iota(jnp.int32, (SEQS * SLOTS, ROWS), 1)
    pick = jnp.where(at == dest, 1.0, 0.0).astype(jnp.bfloat16)
    rest = jnp.concatenate([low_ref[...], high_ref[...]], axis=0)
    part = rest.astype(jnp.bfloat16)
    rest = (rest - part.astype(jnp.float32)).astype(jnp.bfloat16)
    slots = jnp.dot(pick, part, preferred_element_type=jnp.float32)
    slots_ref[...] = slots + jnp.dot(pick, rest, preferred_element_type=jnp.float32)


def place_rows(places_ref, kept_ref, got_ref, out_ref):
    length = out_ref.shape[0]
    at = lax.broadcasted_iota(jnp.int32, (length, 2 * SLOTS), 0)
    hit = jnp.where(at == places_ref[0:1], 1.0, 0.0).astype(jnp.bfloat16)
    rest = jnp.concatenate([kept_ref[...], got_ref[...]], axis=0)
    out = None
    for _ in range(3):
        part = rest.astype(jnp.bfloat16)
        rest = rest - part.astype(jnp.float32)
        part = jnp.dot(hit, part, preferred_element_type=jnp.float32)
        out = part if out is None else out + part
    out_ref[...] = out


def swap_cores(x):
    return lax.ppermute(x, "c", [(0, 1), (1, 0)])


def pass_on(x, by):
    return lax.ppermute(x, "z", [(i, (i + by) % DEEP) for i in range(DEEP)])


def gather_chips(low, high):
    lows, highs = {0: low}, {0: high}
    for hop in range(1, DEEP // 2 + 1):
        lows[-hop] = pass_on(lows[1 - hop], 1)
        highs[hop] = pass_on(highs[hop - 1], -1)
        if hop < DEEP // 2:
            highs[-hop] = pass_on(highs[1 - hop], 1)
            lows[hop] = pass_on(lows[hop - 1], -1)
    lows[DEEP // 2] = lows[-(DEEP // 2)]
    return [chunk for away in range(DEEP) for chunk in (lows[(away + 3) % DEEP - 3], highs[(away + 3) % DEEP - 3])]


def reduce_chips(lows, highs):
    def send(x, by):
        return pass_on(x.astype(jnp.float16), by).astype(jnp.float32)

    half = DEEP // 2
    low_right, high_left = lows[half], highs[half]
    low_left, high_right = lows[half + 1], highs[half - 1]
    for hop in range(1, half):
        low_right = send(low_right, 1) + lows[half - hop]
        high_left = send(high_left, -1) + highs[half + hop]
        if hop < half - 1:
            low_left = send(low_left, -1) + lows[half + 1 + hop]
            high_right = send(high_right, 1) + highs[half - 1 - hop]
    low = lows[0] + send(low_left, -1) + send(low_right, 1)
    high = highs[0] + send(high_right, 1) + send(high_left, -1)
    return low, high


def local(hidden, mask_positions, counts, targets, mask_ratio, own_weight):
    c = lax.axis_index("c")
    features, vocab_dev = own_weight.shape
    wide = -(-vocab_dev // 128) * 128
    length, feat = hidden.shape[1:]
    span = 2 * feat
    smem = pl.BlockSpec(memory_space=pltpu.SMEM)
    vmem = pl.BlockSpec(memory_space=pltpu.VMEM)
    params = pltpu.CompilerParams(vmem_limit_bytes=20 << 20)
    small = pltpu.CompilerParams(vmem_limit_bytes=8 << 20)
    shape = jax.ShapeDtypeStruct

    keep, aux, give, places = pl.pallas_call(
        own_rows,
        out_shape=(
            shape((SLOTS, feat), jnp.bfloat16),
            shape((SLOTS, AUX), jnp.bfloat16),
            shape((SLOTS, feat), jnp.bfloat16),
            shape((8, 2 * SLOTS), jnp.int32),
        ),
        in_specs=[smem, smem, vmem, vmem, vmem],
        out_specs=(vmem,) * 4,
        compiler_params=pltpu.CompilerParams(vmem_limit_bytes=56 << 20),
    )(counts, mask_ratio, mask_positions, targets, hidden[0])
    got = swap_cores(give)

    slots = jnp.concatenate([keep, got, aux], axis=1)
    give, own_weight = lax.optimization_barrier((give, own_weight))
    held = jnp.where(counts[0] > 0, own_weight, 0)
    slots, held = lax.optimization_barrier((slots, held))
    own_t, near_t = held.T, swap_cores(held).T
    slots = lax.all_to_all(jnp.broadcast_to(slots[None], (SEQS,) + slots.shape), PLANE, 0, 0, tiled=True)
    low, high, row_data = pl.pallas_call(
        pack_rows,
        out_shape=(
            shape((CHUNK, span), jnp.bfloat16),
            shape((CHUNK, span), jnp.bfloat16),
            shape((2, ROWS), jnp.float32),
        ),
        in_specs=[smem, vmem],
        out_specs=(vmem,) * 3,
        compiler_params=small,
    )(counts, slots.reshape(SEQS * SLOTS, span + AUX))

    chunks = gather_chips(low, high)
    own_scores, near_scores, stats = pl.pallas_call(
        score_rows,
        out_shape=(
            shape((wide, ROWS), jnp.float32),
            shape((wide, ROWS), jnp.float32),
            shape((SEQS * DEEP, 2, ROWS), jnp.float32),
        ),
        in_specs=[vmem] * (2 + 2 * DEEP),
        out_specs=(vmem,) * 3,
        scratch_shapes=[pltpu.VMEM((ROWS, DEEP * span), jnp.bfloat16)],
        compiler_params=params,
    )(own_t, near_t, *chunks)

    stats = lax.all_to_all(stats, CHIPS, 0, 0, tiled=True)
    parts = (4,), (3, 5), (2, 6, 1, 7, 0)
    sums_shape = shape((CHUNK, span), jnp.float32)
    slope_shape = shape((ROWS, wide), jnp.bfloat16)
    own_slope, near_slope, *sums = pl.pallas_call(
        functools.partial(slope_rows, parts[0]),
        out_shape=(slope_shape, slope_shape) + (sums_shape,) * (2 * len(parts[0])),
        in_specs=[vmem] * 6,
        out_specs=(vmem,) * (2 + 2 * len(parts[0])),
        compiler_params=params,
    )(stats, row_data, own_scores, near_scores, own_t, near_t)
    for part in parts[1:]:
        sums += pl.pallas_call(
            functools.partial(grad_rows, part),
            out_shape=(sums_shape,) * (2 * len(part)),
            in_specs=[vmem] * 4,
            out_specs=(vmem,) * (2 * len(part)),
            compiler_params=params,
            cost_estimate=pl.CostEstimate(
                flops=4 * ROWS * vocab_dev * span * len(part), bytes_accessed=2 * len(part) << 20, transcendentals=0
            ),
        )(own_slope, near_slope, own_t, near_t)
    lows = dict(zip(sum(parts, ()), sums[::2]))
    highs = dict(zip(sum(parts, ()), sums[1::2]))

    low, high = reduce_chips(lows, highs)
    back = pl.pallas_call(
        spread_rows,
        out_shape=shape((SEQS * SLOTS, span), jnp.float32),
        in_specs=[smem, vmem, vmem],
        out_specs=vmem,
        compiler_params=small,
    )(counts, low, high)
    back = back.astype(jnp.float16).reshape(SEQS, SLOTS, span)
    back = lax.all_to_all(back, PLANE, 0, 0, tiled=True)
    back = jnp.sum(back.astype(jnp.float32), axis=0) * (1.0 / SENT_SCALE)
    kept = jnp.where(c == 0, back[:, :feat], back[:, feat:])
    given = jnp.where(c == 0, back[:, feat:], back[:, :feat])
    grad = pl.pallas_call(
        place_rows,
        out_shape=shape((length, feat), jnp.float32),
        in_specs=[vmem] * 3,
        out_specs=vmem,
        compiler_params=small,
    )(places, kept, swap_cores(given))
    return grad[None]


def solution(mesh):
    fine = Mesh(mesh.devices.reshape(SIDE, SIDE, DEEP, 2), CHIPS + ("c",))
    vocab = ("z", "c")
    return jax.shard_map(
        local,
        mesh=fine,
        in_specs=(
            P(PLANE, None, vocab),
            P(PLANE, None),
            P(),
            P(PLANE, None),
            P(PLANE),
            P(None, CHIPS + ("c",)),
        ),
        out_specs=P(PLANE, None, vocab),
        check_vma=False,
    )
```

```python
import jax
import jax.numpy as jnp
from jax import lax
from jax.experimental import pallas as pl
from jax.experimental.pallas import tpu as pltpu
from jax.sharding import Mesh
from jax.sharding import PartitionSpec as P

weight_scale = 4.0
SIDE = 4
DEEP = 8
SEQS = SIDE * SIDE
SLOTS = 32
ROWS = 256
CHUNK = ROWS // 2
AUX = 128
PLANE = ("y", "x")
CHIPS = ("y", "x", "z")
NT = (((1,), (1,)), ((), ()))
TN = (((0,), (0,)), ((), ()))
SENT_SCALE = 4096.0


def chip_index():
    return lax.axis_index("y") * SIDE + lax.axis_index("x")


def first_row(start, core):
    return start + ((start + core) & 1)


def own_rows(counts_ref, ratio_ref, positions_ref, targets_ref, hidden_ref, keep_ref, aux_ref, give_ref, places_ref):
    seq = chip_index()
    core = lax.axis_index("c")
    start = jnp.int32(0)
    count = jnp.int32(0)
    for i in range(SEQS):
        start = start + jnp.where(i < seq, counts_ref[i], 0)
        count = count + jnp.where(i == seq, counts_ref[i], 0)
    length = hidden_ref.shape[0]
    q = lax.broadcasted_iota(jnp.int32, (2 * SLOTS, 1), 0)
    index = jnp.where(q < SLOTS, first_row(start, core), first_row(start, 1 - core)) - start + 2 * (q & (SLOTS - 1))
    valid = index < count
    at = lax.broadcasted_iota(jnp.int32, (2 * SLOTS, 128), 1)
    near = jnp.where(at == index, positions_ref[:, :128].astype(jnp.float32), 0.0)
    places = jnp.where(valid, jnp.sum(near, axis=1, keepdims=True), -1.0)
    places_ref[...] = jnp.transpose(jnp.broadcast_to(places, (2 * SLOTS, 128)))[:8].astype(jnp.int32)
    at = lax.broadcasted_iota(jnp.int32, (2 * SLOTS, length), 1)
    hit = at == places.astype(jnp.int32)
    rows = jnp.dot(jnp.where(hit, 1.0, 0.0).astype(jnp.bfloat16), hidden_ref[...], preferred_element_type=jnp.float32)
    rows = rows.astype(jnp.bfloat16)
    target = jnp.sum(jnp.where(hit, targets_ref[...].astype(jnp.float32), 0.0), axis=1, keepdims=True).astype(jnp.int32)
    lane = lax.broadcasted_iota(jnp.int32, (SLOTS, AUX), 1)
    own = target[:SLOTS]
    digits = jnp.where(lane == 0, own & 127, 0)
    digits = jnp.where(lane == 1, (own >> 7) & 127, digits)
    digits = jnp.where(lane == 2, own >> 14, digits)
    digits = jnp.where(lane == 3, ratio_ref[0], digits)
    keep_ref[...] = rows[:SLOTS]
    aux_ref[...] = digits.astype(jnp.float32).astype(jnp.bfloat16)
    give_ref[...] = rows[SLOTS:]


def slot_dest(counts_ref, slot_index, core):
    slot = slot_index & (SLOTS - 1)
    dest = jnp.full_like(slot_index, -1)
    start = jnp.int32(0)
    for i in range(SEQS):
        end = start + counts_ref[i]
        first = first_row(start, core)
        mine = ((slot_index >> 5) == i) & (first + 2 * slot < end)
        dest = jnp.where(mine, (first >> 1) + slot, dest)
        start = end
    return dest


def pack_rows(counts_ref, slots_ref, low_ref, high_ref, row_ref):
    core = lax.axis_index("c")
    dest = slot_dest(counts_ref, lax.broadcasted_iota(jnp.int32, (1, SEQS * SLOTS), 1), core)
    at = lax.broadcasted_iota(jnp.int32, (ROWS, SEQS * SLOTS), 0)
    pick = jnp.where(at == dest, 1.0, 0.0).astype(jnp.bfloat16)
    packed = jnp.dot(pick, slots_ref[...], preferred_element_type=jnp.float32)
    feat = (slots_ref.shape[1] - AUX) // 2
    own, near = packed[:, :feat], packed[:, feat:2 * feat]
    for at, part in ((0, jnp.where(core == 0, own, near)), (feat, jnp.where(core == 0, near, own))):
        part = part.astype(jnp.bfloat16)
        low_ref[:, at:at + feat] = part[:CHUNK]
        high_ref[:, at:at + feat] = part[CHUNK:]
    digits = jnp.transpose(packed[:, 2 * feat:])
    row_ref[0:1] = digits[0:1] + 128.0 * digits[1:2] + 16384.0 * digits[2:3]
    row_ref[1:2] = weight_scale / digits[3:4]


def features_of(away, span):
    return pl.ds(pl.multiple_of(((lax.axis_index("z") + away) & (DEEP - 1)) * span, span), span)


def score_rows(own_ref, near_ref, *refs):
    chunks, (own_scores_ref, near_scores_ref, stats_ref, rows) = refs[:2 * DEEP], refs[2 * DEEP:]
    count = own_ref.shape[0]
    for away in range(DEEP):
        features = features_of(away, chunks[0].shape[1])
        rows[:CHUNK, features] = chunks[2 * away][...]
        rows[CHUNK:, features] = chunks[2 * away + 1][...]
    for w_ref, ref in ((own_ref, own_scores_ref), (near_ref, near_scores_ref)):
        ref[:count] = lax.dot_general(w_ref[...], rows[...], NT, preferred_element_type=jnp.float32)
    at = lax.broadcasted_iota(jnp.int32, own_scores_ref.shape, 0)
    parts = [jnp.where(at < count, ref[...], -jnp.inf) for ref in (own_scores_ref, near_scores_ref)]
    own_scores_ref[...], near_scores_ref[...] = parts
    top = jnp.maximum(*[jnp.max(part, axis=0, keepdims=True) for part in parts])
    total = sum(jnp.sum(jnp.exp(part - top), axis=0, keepdims=True) for part in parts)
    stats = jnp.concatenate([top, total], axis=0)
    stats_ref[...] = jnp.broadcast_to(stats[None], stats_ref.shape)


def grad_rows(stats_ref, row_ref, own_scores_ref, near_scores_ref, own_ref, near_ref, *refs):
    sums_refs, slopes = refs[:2 * DEEP], refs[2 * DEEP:]
    count = own_ref.shape[0]
    tops = stats_ref[:, 0, :]
    top = jnp.max(tops, axis=0, keepdims=True)
    total = jnp.sum(stats_ref[:, 1, :] * jnp.exp(tops - top), axis=0, keepdims=True)
    chip = chip_index() * DEEP + lax.axis_index("z")
    core = lax.axis_index("c")
    target = row_ref[0:1].astype(jnp.int32)
    at = lax.broadcasted_iota(jnp.int32, own_scores_ref.shape, 0)
    for ref, slope, of_core in ((own_scores_ref, slopes[0], core), (near_scores_ref, slopes[1], 1 - core)):
        local_target = target - (chip * 2 + of_core) * count
        probs = jnp.exp(ref[...] - top) / total
        onehot = jnp.where((at == local_target) & (at < count), 1.0, 0.0)
        slope[...] = jnp.transpose(row_ref[1:2] * (probs - onehot)).astype(jnp.bfloat16)
    for away in range(DEEP):
        features = features_of(away, sums_refs[0].shape[1])
        sums = jnp.dot(slopes[0][:, :count], own_ref[:, features], preferred_element_type=jnp.float32)
        sums += jnp.dot(slopes[1][:, :count], near_ref[:, features], preferred_element_type=jnp.float32)
        sums = sums * SENT_SCALE
        sums_refs[2 * away][...] = sums[:CHUNK]
        sums_refs[2 * away + 1][...] = sums[CHUNK:]


def spread_rows(counts_ref, low_ref, high_ref, slots_ref):
    dest = slot_dest(counts_ref, lax.broadcasted_iota(jnp.int32, (1, SEQS * SLOTS), 1), lax.axis_index("c"))
    at = lax.broadcasted_iota(jnp.int32, (ROWS, SEQS * SLOTS), 0)
    pick = jnp.where(at == dest, 1.0, 0.0).astype(jnp.bfloat16)
    rest = jnp.concatenate([low_ref[...], high_ref[...]], axis=0)
    part = rest.astype(jnp.bfloat16)
    rest = (rest - part.astype(jnp.float32)).astype(jnp.bfloat16)
    slots = lax.dot_general(pick, part, TN, preferred_element_type=jnp.float32)
    slots_ref[...] = slots + lax.dot_general(pick, rest, TN, preferred_element_type=jnp.float32)


def place_rows(places_ref, kept_ref, got_ref, out_ref):
    length = out_ref.shape[0]
    at = lax.broadcasted_iota(jnp.int32, (length, 2 * SLOTS), 0)
    hit = jnp.where(at == places_ref[0:1], 1.0, 0.0).astype(jnp.bfloat16)
    rest = jnp.concatenate([kept_ref[...], got_ref[...]], axis=0)
    out = None
    for _ in range(3):
        part = rest.astype(jnp.bfloat16)
        rest = rest - part.astype(jnp.float32)
        part = jnp.dot(hit, part, preferred_element_type=jnp.float32)
        out = part if out is None else out + part
    out_ref[...] = out


def swap_cores(x):
    return lax.ppermute(x, "c", [(0, 1), (1, 0)])


def pass_on(x, by):
    return lax.ppermute(x, "z", [(i, (i + by) % DEEP) for i in range(DEEP)])


def gather_chips(low, high):
    lows, highs = {0: low}, {0: high}
    for hop in range(1, DEEP // 2 + 1):
        lows[-hop] = pass_on(lows[1 - hop], 1)
        highs[hop] = pass_on(highs[hop - 1], -1)
        if hop < DEEP // 2:
            highs[-hop] = pass_on(highs[1 - hop], 1)
            lows[hop] = pass_on(lows[hop - 1], -1)
    lows[DEEP // 2] = lows[-(DEEP // 2)]
    return [chunk for away in range(DEEP) for chunk in (lows[(away + 3) % DEEP - 3], highs[(away + 3) % DEEP - 3])]


def reduce_chips(lows, highs):
    def send(x, by):
        return pass_on(x.astype(jnp.float16), by).astype(jnp.float32)

    half = DEEP // 2
    low_right, high_left = lows[half], highs[half]
    low_left, high_right = lows[half + 1], highs[half - 1]
    for hop in range(1, half):
        low_right = send(low_right, 1) + lows[half - hop]
        high_left = send(high_left, -1) + highs[half + hop]
        if hop < half - 1:
            low_left = send(low_left, -1) + lows[half + 1 + hop]
            high_right = send(high_right, 1) + highs[half - 1 - hop]
    low = lows[0] + send(low_left, -1) + send(low_right, 1)
    high = highs[0] + send(high_right, 1) + send(high_left, -1)
    return low, high


def local(hidden, mask_positions, counts, targets, mask_ratio, own_weight):
    c = lax.axis_index("c")
    features, vocab_dev = own_weight.shape
    wide = -(-vocab_dev // 128) * 128
    length, feat = hidden.shape[1:]
    span = 2 * feat
    smem = pl.BlockSpec(memory_space=pltpu.SMEM)
    vmem = pl.BlockSpec(memory_space=pltpu.VMEM)
    params = pltpu.CompilerParams(vmem_limit_bytes=20 << 20)
    small = pltpu.CompilerParams(vmem_limit_bytes=8 << 20)
    shape = jax.ShapeDtypeStruct

    keep, aux, give, places = pl.pallas_call(
        own_rows,
        out_shape=(
            shape((SLOTS, feat), jnp.bfloat16),
            shape((SLOTS, AUX), jnp.bfloat16),
            shape((SLOTS, feat), jnp.bfloat16),
            shape((8, 2 * SLOTS), jnp.int32),
        ),
        in_specs=[smem, smem, vmem, vmem, vmem],
        out_specs=(vmem,) * 4,
        compiler_params=pltpu.CompilerParams(vmem_limit_bytes=56 << 20),
    )(counts, mask_ratio, mask_positions, targets, hidden[0])
    got = swap_cores(give)

    slots = jnp.concatenate([keep, got, aux], axis=1)
    give, own_weight = lax.optimization_barrier((give, own_weight))
    held = jnp.where(counts[0] > 0, own_weight, 0)
    slots, held = lax.optimization_barrier((slots, held))
    own_t, near_t = held.T, swap_cores(held).T
    slots = lax.all_to_all(jnp.broadcast_to(slots[None], (SEQS,) + slots.shape), PLANE, 0, 0, tiled=True)
    low, high, row_data = pl.pallas_call(
        pack_rows,
        out_shape=(
            shape((CHUNK, span), jnp.bfloat16),
            shape((CHUNK, span), jnp.bfloat16),
            shape((2, ROWS), jnp.float32),
        ),
        in_specs=[smem, vmem],
        out_specs=(vmem,) * 3,
        compiler_params=small,
    )(counts, slots.reshape(SEQS * SLOTS, span + AUX))

    chunks = gather_chips(low, high)
    own_scores, near_scores, stats = pl.pallas_call(
        score_rows,
        out_shape=(
            shape((wide, ROWS), jnp.float32),
            shape((wide, ROWS), jnp.float32),
            shape((SEQS * DEEP, 2, ROWS), jnp.float32),
        ),
        in_specs=[vmem] * (2 + 2 * DEEP),
        out_specs=(vmem,) * 3,
        scratch_shapes=[pltpu.VMEM((ROWS, DEEP * span), jnp.bfloat16)],
        compiler_params=params,
    )(own_t, near_t, *chunks)

    stats = lax.all_to_all(stats, CHIPS, 0, 0, tiled=True)
    sums = pl.pallas_call(
        grad_rows,
        out_shape=(shape((CHUNK, span), jnp.float32),) * (2 * DEEP),
        in_specs=[vmem] * 6,
        out_specs=(vmem,) * (2 * DEEP),
        scratch_shapes=[pltpu.VMEM((ROWS, wide), jnp.bfloat16)] * 2,
        compiler_params=params,
    )(stats, row_data, own_scores, near_scores, own_t, near_t)

    low, high = reduce_chips(sums[::2], sums[1::2])
    back = pl.pallas_call(
        spread_rows,
        out_shape=shape((SEQS * SLOTS, span), jnp.float32),
        in_specs=[smem, vmem, vmem],
        out_specs=vmem,
        compiler_params=small,
    )(counts, low, high)
    back = back.astype(jnp.float16).reshape(SEQS, SLOTS, span)
    back, c = lax.optimization_barrier((back, c))
    back = lax.all_to_all(back, PLANE, 0, 0, tiled=True)
    back = jnp.sum(back.astype(jnp.float32), axis=0) * (1.0 / SENT_SCALE)
    kept = jnp.where(c == 0, back[:, :feat], back[:, feat:])
    given = jnp.where(c == 0, back[:, feat:], back[:, :feat])
    grad = pl.pallas_call(
        place_rows,
        out_shape=shape((length, feat), jnp.float32),
        in_specs=[vmem] * 3,
        out_specs=vmem,
        compiler_params=small,
    )(places, kept, swap_cores(given))
    return grad[None]


def solution(mesh):
    fine = Mesh(mesh.devices.reshape(SIDE, SIDE, DEEP, 2), CHIPS + ("c",))
    vocab = ("z", "c")
    return jax.shard_map(
        local,
        mesh=fine,
        in_specs=(
            P(PLANE, None, vocab),
            P(PLANE, None),
            P(),
            P(PLANE, None),
            P(PLANE),
            P(None, CHIPS + ("c",)),
        ),
        out_specs=P(PLANE, None, vocab),
        check_vma=False,
    )
```

```python
import jax
import jax.numpy as jnp
from jax import lax
from jax.experimental import pallas as pl
from jax.experimental.pallas import tpu as pltpu
from jax.sharding import Mesh
from jax.sharding import PartitionSpec as P

weight_scale = 4.0
SIDE = 4
DEEP = 8
SEQS = SIDE * SIDE
SLOTS = 32
ROWS = 256
CHUNK = ROWS // 2
AUX = 128
PLANE = ("y", "x")
CHIPS = ("y", "x", "z")
NT = (((1,), (1,)), ((), ()))
TN = (((0,), (0,)), ((), ()))
SENT_SCALE = 4096.0


def chip_index():
    return lax.axis_index("y") * SIDE + lax.axis_index("x")


def first_row(start, core):
    return start + ((start + core) & 1)


def own_rows(counts_ref, ratio_ref, positions_ref, targets_ref, hidden_ref, keep_ref, aux_ref, give_ref, places_ref):
    seq = chip_index()
    core = lax.axis_index("c")
    start = jnp.int32(0)
    count = jnp.int32(0)
    for i in range(SEQS):
        start = start + jnp.where(i < seq, counts_ref[i], 0)
        count = count + jnp.where(i == seq, counts_ref[i], 0)
    length = hidden_ref.shape[0]
    q = lax.broadcasted_iota(jnp.int32, (2 * SLOTS, 1), 0)
    index = jnp.where(q < SLOTS, first_row(start, core), first_row(start, 1 - core)) - start + 2 * (q & (SLOTS - 1))
    valid = index < count
    at = lax.broadcasted_iota(jnp.int32, (2 * SLOTS, 128), 1)
    near = jnp.where(at == index, positions_ref[:, :128].astype(jnp.float32), 0.0)
    places = jnp.where(valid, jnp.sum(near, axis=1, keepdims=True), -1.0)
    places_ref[...] = jnp.transpose(jnp.broadcast_to(places, (2 * SLOTS, 128)))[:8].astype(jnp.int32)
    at = lax.broadcasted_iota(jnp.int32, (2 * SLOTS, length), 1)
    hit = at == places.astype(jnp.int32)
    rows = jnp.dot(jnp.where(hit, 1.0, 0.0).astype(jnp.bfloat16), hidden_ref[...], preferred_element_type=jnp.float32)
    rows = rows.astype(jnp.bfloat16)
    target = jnp.sum(jnp.where(hit, targets_ref[...].astype(jnp.float32), 0.0), axis=1, keepdims=True).astype(jnp.int32)
    lane = lax.broadcasted_iota(jnp.int32, (SLOTS, AUX), 1)
    own = target[:SLOTS]
    digits = jnp.where(lane == 0, own & 127, 0)
    digits = jnp.where(lane == 1, (own >> 7) & 127, digits)
    digits = jnp.where(lane == 2, own >> 14, digits)
    digits = jnp.where(lane == 3, ratio_ref[0], digits)
    keep_ref[...] = rows[:SLOTS]
    aux_ref[...] = digits.astype(jnp.float32).astype(jnp.bfloat16)
    give_ref[...] = rows[SLOTS:]


def slot_dest(counts_ref, slot_index, core):
    slot = slot_index & (SLOTS - 1)
    dest = jnp.full_like(slot_index, -1)
    start = jnp.int32(0)
    for i in range(SEQS):
        end = start + counts_ref[i]
        first = first_row(start, core)
        mine = ((slot_index >> 5) == i) & (first + 2 * slot < end)
        dest = jnp.where(mine, (first >> 1) + slot, dest)
        start = end
    return dest


def pack_rows(counts_ref, slots_ref, low_ref, high_ref, row_ref):
    core = lax.axis_index("c")
    dest = slot_dest(counts_ref, lax.broadcasted_iota(jnp.int32, (1, SEQS * SLOTS), 1), core)
    at = lax.broadcasted_iota(jnp.int32, (ROWS, SEQS * SLOTS), 0)
    pick = jnp.where(at == dest, 1.0, 0.0).astype(jnp.bfloat16)
    packed = jnp.dot(pick, slots_ref[...], preferred_element_type=jnp.float32)
    feat = (slots_ref.shape[1] - AUX) // 2
    own, near = packed[:, :feat], packed[:, feat:2 * feat]
    for at, part in ((0, jnp.where(core == 0, own, near)), (feat, jnp.where(core == 0, near, own))):
        part = part.astype(jnp.bfloat16)
        low_ref[:, at:at + feat] = part[:CHUNK]
        high_ref[:, at:at + feat] = part[CHUNK:]
    digits = jnp.transpose(packed[:, 2 * feat:])
    row_ref[0:1] = digits[0:1] + 128.0 * digits[1:2] + 16384.0 * digits[2:3]
    row_ref[1:2] = weight_scale / digits[3:4]


def features_of(away, span):
    return pl.ds(pl.multiple_of(((lax.axis_index("z") + away) & (DEEP - 1)) * span, span), span)


def score_rows(own_ref, near_ref, *refs):
    chunks, (own_scores_ref, near_scores_ref, stats_ref, rows) = refs[:2 * DEEP], refs[2 * DEEP:]
    count = own_ref.shape[0]
    for away in range(DEEP):
        features = features_of(away, chunks[0].shape[1])
        rows[:CHUNK, features] = chunks[2 * away][...]
        rows[CHUNK:, features] = chunks[2 * away + 1][...]
    for w_ref, ref in ((own_ref, own_scores_ref), (near_ref, near_scores_ref)):
        ref[:count] = lax.dot_general(w_ref[...], rows[...], NT, preferred_element_type=jnp.float32)
    at = lax.broadcasted_iota(jnp.int32, own_scores_ref.shape, 0)
    parts = [jnp.where(at < count, ref[...], -jnp.inf) for ref in (own_scores_ref, near_scores_ref)]
    own_scores_ref[...], near_scores_ref[...] = parts
    top = jnp.maximum(*[jnp.max(part, axis=0, keepdims=True) for part in parts])
    total = sum(jnp.sum(jnp.exp(part - top), axis=0, keepdims=True) for part in parts)
    stats = jnp.concatenate([top, total], axis=0)
    stats_ref[...] = jnp.broadcast_to(stats[None], stats_ref.shape)


def grad_rows(stats_ref, row_ref, own_scores_ref, near_scores_ref, own_ref, near_ref, *refs):
    sums_refs, slopes = refs[:2 * DEEP], refs[2 * DEEP:]
    count = own_ref.shape[0]
    tops = stats_ref[:, 0, :]
    top = jnp.max(tops, axis=0, keepdims=True)
    total = jnp.sum(stats_ref[:, 1, :] * jnp.exp(tops - top), axis=0, keepdims=True)
    chip = chip_index() * DEEP + lax.axis_index("z")
    core = lax.axis_index("c")
    target = row_ref[0:1].astype(jnp.int32)
    at = lax.broadcasted_iota(jnp.int32, own_scores_ref.shape, 0)
    for ref, slope, of_core in ((own_scores_ref, slopes[0], core), (near_scores_ref, slopes[1], 1 - core)):
        local_target = target - (chip * 2 + of_core) * count
        probs = jnp.exp(ref[...] - top) / total
        onehot = jnp.where((at == local_target) & (at < count), 1.0, 0.0)
        slope[...] = jnp.transpose(row_ref[1:2] * (probs - onehot)).astype(jnp.bfloat16)
    for away in range(DEEP):
        features = features_of(away, sums_refs[0].shape[1])
        sums = jnp.dot(slopes[0][:, :count], own_ref[:, features], preferred_element_type=jnp.float32)
        sums += jnp.dot(slopes[1][:, :count], near_ref[:, features], preferred_element_type=jnp.float32)
        sums = sums * SENT_SCALE
        sums_refs[2 * away][...] = sums[:CHUNK]
        sums_refs[2 * away + 1][...] = sums[CHUNK:]


def spread_rows(counts_ref, low_ref, high_ref, slots_ref):
    dest = slot_dest(counts_ref, lax.broadcasted_iota(jnp.int32, (1, SEQS * SLOTS), 1), lax.axis_index("c"))
    at = lax.broadcasted_iota(jnp.int32, (ROWS, SEQS * SLOTS), 0)
    pick = jnp.where(at == dest, 1.0, 0.0).astype(jnp.bfloat16)
    rest = jnp.concatenate([low_ref[...], high_ref[...]], axis=0)
    part = rest.astype(jnp.bfloat16)
    rest = (rest - part.astype(jnp.float32)).astype(jnp.bfloat16)
    slots = lax.dot_general(pick, part, TN, preferred_element_type=jnp.float32)
    slots_ref[...] = slots + lax.dot_general(pick, rest, TN, preferred_element_type=jnp.float32)


def place_rows(places_ref, kept_ref, got_ref, out_ref):
    length = out_ref.shape[0]
    at = lax.broadcasted_iota(jnp.int32, (length, 2 * SLOTS), 0)
    hit = jnp.where(at == places_ref[0:1], 1.0, 0.0).astype(jnp.bfloat16)
    rest = jnp.concatenate([kept_ref[...], got_ref[...]], axis=0)
    out = None
    for _ in range(3):
        part = rest.astype(jnp.bfloat16)
        rest = rest - part.astype(jnp.float32)
        part = jnp.dot(hit, part, preferred_element_type=jnp.float32)
        out = part if out is None else out + part
    out_ref[...] = out


def swap_cores(x):
    return lax.ppermute(x, "c", [(0, 1), (1, 0)])


def pass_on(x, by):
    return lax.ppermute(x, "z", [(i, (i + by) % DEEP) for i in range(DEEP)])


def gather_chips(low, high):
    lows, highs = {0: low}, {0: high}
    for hop in range(1, DEEP // 2 + 1):
        lows[-hop] = pass_on(lows[1 - hop], 1)
        highs[hop] = pass_on(highs[hop - 1], -1)
        if hop < DEEP // 2:
            highs[-hop] = pass_on(highs[1 - hop], 1)
            lows[hop] = pass_on(lows[hop - 1], -1)
    lows[DEEP // 2] = lows[-(DEEP // 2)]
    return [chunk for away in range(DEEP) for chunk in (lows[(away + 3) % DEEP - 3], highs[(away + 3) % DEEP - 3])]


def reduce_chips(lows, highs):
    def send(x, by):
        return pass_on(x.astype(jnp.float16), by).astype(jnp.float32)

    half = DEEP // 2
    low_right, high_left = lows[half], highs[half]
    low_left, high_right = lows[half + 1], highs[half - 1]
    for hop in range(1, half):
        low_right = send(low_right, 1) + lows[half - hop]
        high_left = send(high_left, -1) + highs[half + hop]
        if hop < half - 1:
            low_left = send(low_left, -1) + lows[half + 1 + hop]
            high_right = send(high_right, 1) + highs[half - 1 - hop]
    low = lows[0] + send(low_left, -1) + send(low_right, 1)
    high = highs[0] + send(high_right, 1) + send(high_left, -1)
    return low, high


def local(hidden, mask_positions, counts, targets, mask_ratio, own_weight):
    c = lax.axis_index("c")
    features, vocab_dev = own_weight.shape
    wide = -(-vocab_dev // 128) * 128
    length, feat = hidden.shape[1:]
    span = 2 * feat
    smem = pl.BlockSpec(memory_space=pltpu.SMEM)
    vmem = pl.BlockSpec(memory_space=pltpu.VMEM)
    params = pltpu.CompilerParams(vmem_limit_bytes=16 << 20)
    small = pltpu.CompilerParams(vmem_limit_bytes=8 << 20)
    shape = jax.ShapeDtypeStruct

    keep, aux, give, places = pl.pallas_call(
        own_rows,
        out_shape=(
            shape((SLOTS, feat), jnp.bfloat16),
            shape((SLOTS, AUX), jnp.bfloat16),
            shape((SLOTS, feat), jnp.bfloat16),
            shape((8, 2 * SLOTS), jnp.int32),
        ),
        in_specs=[smem, smem, vmem, vmem, vmem],
        out_specs=(vmem,) * 4,
        compiler_params=pltpu.CompilerParams(vmem_limit_bytes=56 << 20),
    )(counts, mask_ratio, mask_positions, targets, hidden[0])
    got = swap_cores(give)

    slots = jnp.concatenate([keep, got, aux], axis=1)
    give, own_weight = lax.optimization_barrier((give, own_weight))
    held = jnp.where(counts[0] > 0, own_weight, 0)
    slots, held = lax.optimization_barrier((slots, held))
    own_t, near_t = held.T, swap_cores(held).T
    slots = lax.all_to_all(jnp.broadcast_to(slots[None], (SEQS,) + slots.shape), PLANE, 0, 0, tiled=True)
    low, high, row_data = pl.pallas_call(
        pack_rows,
        out_shape=(
            shape((CHUNK, span), jnp.bfloat16),
            shape((CHUNK, span), jnp.bfloat16),
            shape((2, ROWS), jnp.float32),
        ),
        in_specs=[smem, vmem],
        out_specs=(vmem,) * 3,
        compiler_params=small,
    )(counts, slots.reshape(SEQS * SLOTS, span + AUX))

    chunks = gather_chips(low, high)
    own_scores, near_scores, stats = pl.pallas_call(
        score_rows,
        out_shape=(
            shape((wide, ROWS), jnp.float32),
            shape((wide, ROWS), jnp.float32),
            shape((SEQS * DEEP, 2, ROWS), jnp.float32),
        ),
        in_specs=[vmem] * (2 + 2 * DEEP),
        out_specs=(vmem,) * 3,
        scratch_shapes=[pltpu.VMEM((ROWS, DEEP * span), jnp.bfloat16)],
        compiler_params=params,
    )(own_t, near_t, *chunks)

    stats = lax.all_to_all(stats, CHIPS, 0, 0, tiled=True)
    sums = pl.pallas_call(
        grad_rows,
        out_shape=(shape((CHUNK, span), jnp.float32),) * (2 * DEEP),
        in_specs=[vmem] * 6,
        out_specs=(vmem,) * (2 * DEEP),
        scratch_shapes=[pltpu.VMEM((ROWS, wide), jnp.bfloat16)] * 2,
        compiler_params=params,
    )(stats, row_data, own_scores, near_scores, own_t, near_t)

    low, high = reduce_chips(sums[::2], sums[1::2])
    back = pl.pallas_call(
        spread_rows,
        out_shape=shape((SEQS * SLOTS, span), jnp.float32),
        in_specs=[smem, vmem, vmem],
        out_specs=vmem,
        compiler_params=small,
    )(counts, low, high)
    back = back.astype(jnp.float16).reshape(SEQS, SLOTS, span)
    back, first_core = lax.optimization_barrier((back, c == 0))
    back = lax.all_to_all(back, PLANE, 0, 0, tiled=True)
    back = jnp.sum(back.astype(jnp.float32), axis=0) * (1.0 / SENT_SCALE)
    kept = jnp.where(first_core, back[:, :feat], back[:, feat:])
    given = jnp.where(first_core, back[:, feat:], back[:, :feat])
    grad = pl.pallas_call(
        place_rows,
        out_shape=shape((length, feat), jnp.float32),
        in_specs=[vmem] * 3,
        out_specs=vmem,
        compiler_params=small,
    )(places, kept, swap_cores(given))
    return grad[None]


def solution(mesh):
    fine = Mesh(mesh.devices.reshape(SIDE, SIDE, DEEP, 2), CHIPS + ("c",))
    vocab = ("z", "c")
    return jax.shard_map(
        local,
        mesh=fine,
        in_specs=(
            P(PLANE, None, vocab),
            P(PLANE, None),
            P(),
            P(PLANE, None),
            P(PLANE),
            P(None, CHIPS + ("c",)),
        ),
        out_specs=P(PLANE, None, vocab),
        check_vma=False,
    )
```

```python
import functools

import jax
import jax.numpy as jnp
from jax import lax
from jax.experimental import pallas as pl
from jax.experimental.pallas import tpu as pltpu
from jax.sharding import Mesh
from jax.sharding import PartitionSpec as P

weight_scale = 4.0
SIDE = 4
DEEP = 8
SEQS = SIDE * SIDE
SLOTS = 32
ROWS = 256
CHUNK = ROWS // 2
AUX = 128
PLANE = ("y", "x")
CHIPS = ("y", "x", "z")
NT = (((1,), (1,)), ((), ()))
TN = (((0,), (0,)), ((), ()))
SENT_SCALE = 4096.0


def chip_index():
    return lax.axis_index("y") * SIDE + lax.axis_index("x")


def first_row(start, core):
    return start + ((start + core) & 1)


def own_rows(counts_ref, ratio_ref, positions_ref, targets_ref, hidden_ref, keep_ref, aux_ref, give_ref, places_ref):
    seq = chip_index()
    core = lax.axis_index("c")
    start = jnp.int32(0)
    count = jnp.int32(0)
    for i in range(SEQS):
        start = start + jnp.where(i < seq, counts_ref[i], 0)
        count = count + jnp.where(i == seq, counts_ref[i], 0)
    length = hidden_ref.shape[0]
    q = lax.broadcasted_iota(jnp.int32, (2 * SLOTS, 1), 0)
    index = jnp.where(q < SLOTS, first_row(start, core), first_row(start, 1 - core)) - start + 2 * (q & (SLOTS - 1))
    valid = index < count
    at = lax.broadcasted_iota(jnp.int32, (2 * SLOTS, 128), 1)
    near = jnp.where(at == index, positions_ref[:, :128].astype(jnp.float32), 0.0)
    places = jnp.where(valid, jnp.sum(near, axis=1, keepdims=True), -1.0)
    places_ref[...] = jnp.transpose(jnp.broadcast_to(places, (2 * SLOTS, 128)))[:8].astype(jnp.int32)
    at = lax.broadcasted_iota(jnp.int32, (2 * SLOTS, length), 1)
    hit = at == places.astype(jnp.int32)
    rows = jnp.dot(jnp.where(hit, 1.0, 0.0).astype(jnp.bfloat16), hidden_ref[...], preferred_element_type=jnp.float32)
    rows = rows.astype(jnp.bfloat16)
    target = jnp.sum(jnp.where(hit, targets_ref[...].astype(jnp.float32), 0.0), axis=1, keepdims=True).astype(jnp.int32)
    lane = lax.broadcasted_iota(jnp.int32, (SLOTS, AUX), 1)
    own = target[:SLOTS]
    digits = jnp.where(lane == 0, own & 127, 0)
    digits = jnp.where(lane == 1, (own >> 7) & 127, digits)
    digits = jnp.where(lane == 2, own >> 14, digits)
    digits = jnp.where(lane == 3, ratio_ref[0], digits)
    keep_ref[...] = rows[:SLOTS]
    aux_ref[...] = digits.astype(jnp.float32).astype(jnp.bfloat16)
    give_ref[...] = rows[SLOTS:]


def slot_dest(counts_ref, slot_index, core):
    slot = slot_index & (SLOTS - 1)
    dest = jnp.full_like(slot_index, -1)
    start = jnp.int32(0)
    for i in range(SEQS):
        end = start + counts_ref[i]
        first = first_row(start, core)
        mine = ((slot_index >> 5) == i) & (first + 2 * slot < end)
        dest = jnp.where(mine, (first >> 1) + slot, dest)
        start = end
    return dest


def pack_rows(counts_ref, slots_ref, low_ref, high_ref, row_ref):
    core = lax.axis_index("c")
    dest = slot_dest(counts_ref, lax.broadcasted_iota(jnp.int32, (1, SEQS * SLOTS), 1), core)
    at = lax.broadcasted_iota(jnp.int32, (ROWS, SEQS * SLOTS), 0)
    pick = jnp.where(at == dest, 1.0, 0.0).astype(jnp.bfloat16)
    packed = jnp.dot(pick, slots_ref[...], preferred_element_type=jnp.float32)
    feat = (slots_ref.shape[1] - AUX) // 2
    own, near = packed[:, :feat], packed[:, feat:2 * feat]
    for at, part in ((0, jnp.where(core == 0, own, near)), (feat, jnp.where(core == 0, near, own))):
        part = part.astype(jnp.bfloat16)
        low_ref[:, at:at + feat] = part[:CHUNK]
        high_ref[:, at:at + feat] = part[CHUNK:]
    digits = jnp.transpose(packed[:, 2 * feat:])
    row_ref[0:1] = digits[0:1] + 128.0 * digits[1:2] + 16384.0 * digits[2:3]
    row_ref[1:2] = weight_scale / digits[3:4]


def features_of(away, span):
    return pl.ds(pl.multiple_of(((lax.axis_index("z") + away) & (DEEP - 1)) * span, span), span)


def score_rows(own_ref, near_ref, *refs):
    chunks, (own_scores_ref, near_scores_ref, stats_ref, rows) = refs[:2 * DEEP], refs[2 * DEEP:]
    count = own_ref.shape[0]
    for away in range(DEEP):
        features = features_of(away, chunks[0].shape[1])
        rows[:CHUNK, features] = chunks[2 * away][...]
        rows[CHUNK:, features] = chunks[2 * away + 1][...]
    for w_ref, ref in ((own_ref, own_scores_ref), (near_ref, near_scores_ref)):
        ref[:count] = lax.dot_general(w_ref[...], rows[...], NT, preferred_element_type=jnp.float32)
    at = lax.broadcasted_iota(jnp.int32, own_scores_ref.shape, 0)
    parts = [jnp.where(at < count, ref[...], -jnp.inf) for ref in (own_scores_ref, near_scores_ref)]
    own_scores_ref[...], near_scores_ref[...] = parts
    top = jnp.maximum(*[jnp.max(part, axis=0, keepdims=True) for part in parts])
    total = sum(jnp.sum(jnp.exp(part - top), axis=0, keepdims=True) for part in parts)
    stats = jnp.concatenate([top, total], axis=0)
    stats_ref[...] = jnp.broadcast_to(stats[None], stats_ref.shape)


def grad_rows(aways, own_slope_ref, near_slope_ref, own_ref, near_ref, *sums_refs):
    count = own_ref.shape[0]
    for i, away in enumerate(aways):
        features = features_of(away, sums_refs[0].shape[1])
        sums = jnp.dot(own_slope_ref[:, :count], own_ref[:, features], preferred_element_type=jnp.float32)
        sums += jnp.dot(near_slope_ref[:, :count], near_ref[:, features], preferred_element_type=jnp.float32)
        sums = sums * SENT_SCALE
        sums_refs[2 * i][...] = sums[:CHUNK]
        sums_refs[2 * i + 1][...] = sums[CHUNK:]


def slope_rows(aways, stats_ref, row_ref, own_scores_ref, near_scores_ref, own_ref, near_ref, own_slope_ref, near_slope_ref, *sums_refs):
    count = own_ref.shape[0]
    tops = stats_ref[:, 0, :]
    top = jnp.max(tops, axis=0, keepdims=True)
    total = jnp.sum(stats_ref[:, 1, :] * jnp.exp(tops - top), axis=0, keepdims=True)
    chip = chip_index() * DEEP + lax.axis_index("z")
    core = lax.axis_index("c")
    target = row_ref[0:1].astype(jnp.int32)
    at = lax.broadcasted_iota(jnp.int32, own_scores_ref.shape, 0)
    for ref, slope, of_core in ((own_scores_ref, own_slope_ref, core), (near_scores_ref, near_slope_ref, 1 - core)):
        local_target = target - (chip * 2 + of_core) * count
        probs = jnp.exp(ref[...] - top) / total
        onehot = jnp.where((at == local_target) & (at < count), 1.0, 0.0)
        slope[...] = jnp.transpose(row_ref[1:2] * (probs - onehot)).astype(jnp.bfloat16)
    grad_rows(aways, own_slope_ref, near_slope_ref, own_ref, near_ref, *sums_refs)


def spread_rows(counts_ref, low_ref, high_ref, slots_ref):
    dest = slot_dest(counts_ref, lax.broadcasted_iota(jnp.int32, (1, SEQS * SLOTS), 1), lax.axis_index("c"))
    at = lax.broadcasted_iota(jnp.int32, (ROWS, SEQS * SLOTS), 0)
    pick = jnp.where(at == dest, 1.0, 0.0).astype(jnp.bfloat16)
    rest = jnp.concatenate([low_ref[...], high_ref[...]], axis=0)
    part = rest.astype(jnp.bfloat16)
    rest = (rest - part.astype(jnp.float32)).astype(jnp.bfloat16)
    slots = lax.dot_general(pick, part, TN, preferred_element_type=jnp.float32)
    slots_ref[...] = slots + lax.dot_general(pick, rest, TN, preferred_element_type=jnp.float32)


def place_rows(places_ref, kept_ref, got_ref, out_ref):
    length = out_ref.shape[0]
    at = lax.broadcasted_iota(jnp.int32, (length, 2 * SLOTS), 0)
    hit = jnp.where(at == places_ref[0:1], 1.0, 0.0).astype(jnp.bfloat16)
    rest = jnp.concatenate([kept_ref[...], got_ref[...]], axis=0)
    out = None
    for _ in range(3):
        part = rest.astype(jnp.bfloat16)
        rest = rest - part.astype(jnp.float32)
        part = jnp.dot(hit, part, preferred_element_type=jnp.float32)
        out = part if out is None else out + part
    out_ref[...] = out


def swap_cores(x):
    return lax.ppermute(x, "c", [(0, 1), (1, 0)])


def pass_on(x, by):
    return lax.ppermute(x, "z", [(i, (i + by) % DEEP) for i in range(DEEP)])


def gather_chips(low, high):
    lows, highs = {0: low}, {0: high}
    for hop in range(1, DEEP // 2 + 1):
        lows[-hop] = pass_on(lows[1 - hop], 1)
        highs[hop] = pass_on(highs[hop - 1], -1)
        if hop < DEEP // 2:
            highs[-hop] = pass_on(highs[1 - hop], 1)
            lows[hop] = pass_on(lows[hop - 1], -1)
    lows[DEEP // 2] = lows[-(DEEP // 2)]
    return [chunk for away in range(DEEP) for chunk in (lows[(away + 3) % DEEP - 3], highs[(away + 3) % DEEP - 3])]


def reduce_chips(lows, highs):
    def send(x, by):
        return pass_on(x.astype(jnp.float16), by).astype(jnp.float32)

    half = DEEP // 2
    low_right, high_left = lows[half], highs[half]
    low_left, high_right = lows[half + 1], highs[half - 1]
    for hop in range(1, half):
        low_right = send(low_right, 1) + lows[half - hop]
        high_left = send(high_left, -1) + highs[half + hop]
        if hop < half - 1:
            low_left = send(low_left, -1) + lows[half + 1 + hop]
            high_right = send(high_right, 1) + highs[half - 1 - hop]
    low = lows[0] + send(low_left, -1) + send(low_right, 1)
    high = highs[0] + send(high_right, 1) + send(high_left, -1)
    return low, high


def local(hidden, mask_positions, counts, targets, mask_ratio, own_weight):
    c = lax.axis_index("c")
    features, vocab_dev = own_weight.shape
    wide = -(-vocab_dev // 128) * 128
    length, feat = hidden.shape[1:]
    span = 2 * feat
    smem = pl.BlockSpec(memory_space=pltpu.SMEM)
    vmem = pl.BlockSpec(memory_space=pltpu.VMEM)
    params = pltpu.CompilerParams(vmem_limit_bytes=16 << 20)
    small = pltpu.CompilerParams(vmem_limit_bytes=8 << 20)
    shape = jax.ShapeDtypeStruct

    keep, aux, give, places = pl.pallas_call(
        own_rows,
        out_shape=(
            shape((SLOTS, feat), jnp.bfloat16),
            shape((SLOTS, AUX), jnp.bfloat16),
            shape((SLOTS, feat), jnp.bfloat16),
            shape((8, 2 * SLOTS), jnp.int32),
        ),
        in_specs=[smem, smem, vmem, vmem, vmem],
        out_specs=(vmem,) * 4,
        compiler_params=pltpu.CompilerParams(vmem_limit_bytes=56 << 20),
    )(counts, mask_ratio, mask_positions, targets, hidden[0])
    got = swap_cores(give)

    slots = jnp.concatenate([keep, got, aux], axis=1)
    give, own_weight = lax.optimization_barrier((give, own_weight))
    held = jnp.where(counts[0] > 0, own_weight, 0)
    slots, held = lax.optimization_barrier((slots, held))
    own_t, near_t = held.T, swap_cores(held).T
    slots = lax.all_to_all(jnp.broadcast_to(slots[None], (SEQS,) + slots.shape), PLANE, 0, 0, tiled=True)
    low, high, row_data = pl.pallas_call(
        pack_rows,
        out_shape=(
            shape((CHUNK, span), jnp.bfloat16),
            shape((CHUNK, span), jnp.bfloat16),
            shape((2, ROWS), jnp.float32),
        ),
        in_specs=[smem, vmem],
        out_specs=(vmem,) * 3,
        compiler_params=small,
    )(counts, slots.reshape(SEQS * SLOTS, span + AUX))

    chunks = gather_chips(low, high)
    own_scores, near_scores, stats = pl.pallas_call(
        score_rows,
        out_shape=(
            shape((wide, ROWS), jnp.float32),
            shape((wide, ROWS), jnp.float32),
            shape((SEQS * DEEP, 2, ROWS), jnp.float32),
        ),
        in_specs=[vmem] * (2 + 2 * DEEP),
        out_specs=(vmem,) * 3,
        scratch_shapes=[pltpu.VMEM((ROWS, DEEP * span), jnp.bfloat16)],
        compiler_params=params,
    )(own_t, near_t, *chunks)

    stats = lax.all_to_all(stats, CHIPS, 0, 0, tiled=True)
    parts = (4, 5, 3), (6, 2, 7, 1, 0)
    sums_shape = shape((CHUNK, span), jnp.float32)
    slope_shape = shape((ROWS, wide), jnp.bfloat16)
    own_slope, near_slope, *sums = pl.pallas_call(
        functools.partial(slope_rows, parts[0]),
        out_shape=(slope_shape, slope_shape) + (sums_shape,) * (2 * len(parts[0])),
        in_specs=[vmem] * 6,
        out_specs=(vmem,) * (2 + 2 * len(parts[0])),
        compiler_params=params,
    )(stats, row_data, own_scores, near_scores, own_t, near_t)
    more = pl.pallas_call(
        functools.partial(grad_rows, parts[1]),
        out_shape=(sums_shape,) * (2 * len(parts[1])),
        in_specs=[vmem] * 4,
        out_specs=(vmem,) * (2 * len(parts[1])),
        compiler_params=params,
    )(own_slope, near_slope, own_t, near_t)
    sums = lax.optimization_barrier((*sums, *more))
    lows = dict(zip(parts[0] + parts[1], sums[::2]))
    highs = dict(zip(parts[0] + parts[1], sums[1::2]))

    low, high = reduce_chips(lows, highs)
    back = pl.pallas_call(
        spread_rows,
        out_shape=shape((SEQS * SLOTS, span), jnp.float32),
        in_specs=[smem, vmem, vmem],
        out_specs=vmem,
        compiler_params=small,
    )(counts, low, high)
    back = back.astype(jnp.float16).reshape(SEQS, SLOTS, span)
    back, first_core = lax.optimization_barrier((back, c == 0))
    back = lax.all_to_all(back, PLANE, 0, 0, tiled=True)
    back = jnp.sum(back.astype(jnp.float32), axis=0) * (1.0 / SENT_SCALE)
    kept = jnp.where(first_core, back[:, :feat], back[:, feat:])
    given = jnp.where(first_core, back[:, feat:], back[:, :feat])
    grad = pl.pallas_call(
        place_rows,
        out_shape=shape((length, feat), jnp.float32),
        in_specs=[vmem] * 3,
        out_specs=vmem,
        compiler_params=small,
    )(places, kept, swap_cores(given))
    return grad[None]


def solution(mesh):
    fine = Mesh(mesh.devices.reshape(SIDE, SIDE, DEEP, 2), CHIPS + ("c",))
    vocab = ("z", "c")
    return jax.shard_map(
        local,
        mesh=fine,
        in_specs=(
            P(PLANE, None, vocab),
            P(PLANE, None),
            P(),
            P(PLANE, None),
            P(PLANE),
            P(None, CHIPS + ("c",)),
        ),
        out_specs=P(PLANE, None, vocab),
        check_vma=False,
    )
```

```python
import functools

import jax
import jax.numpy as jnp
from jax import lax
from jax.experimental import pallas as pl
from jax.experimental.pallas import tpu as pltpu
from jax.sharding import Mesh
from jax.sharding import PartitionSpec as P

weight_scale = 4.0
SIDE = 4
DEEP = 8
SEQS = SIDE * SIDE
SLOTS = 32
ROWS = 256
CHUNK = ROWS // 2
AUX = 128
PLANE = ("y", "x")
CHIPS = ("y", "x", "z")
NT = (((1,), (1,)), ((), ()))
TN = (((0,), (0,)), ((), ()))
SENT_SCALE = 4096.0


def chip_index():
    return lax.axis_index("y") * SIDE + lax.axis_index("x")


def first_row(start, core):
    return start + ((start + core) & 1)


def own_rows(counts_ref, ratio_ref, positions_ref, targets_ref, hidden_ref, keep_ref, aux_ref, give_ref, places_ref):
    seq = chip_index()
    core = lax.axis_index("c")
    start = jnp.int32(0)
    count = jnp.int32(0)
    for i in range(SEQS):
        start = start + jnp.where(i < seq, counts_ref[i], 0)
        count = count + jnp.where(i == seq, counts_ref[i], 0)
    length = hidden_ref.shape[0]
    q = lax.broadcasted_iota(jnp.int32, (2 * SLOTS, 1), 0)
    index = jnp.where(q < SLOTS, first_row(start, core), first_row(start, 1 - core)) - start + 2 * (q & (SLOTS - 1))
    valid = index < count
    at = lax.broadcasted_iota(jnp.int32, (2 * SLOTS, 128), 1)
    near = jnp.where(at == index, positions_ref[:, :128].astype(jnp.float32), 0.0)
    places = jnp.where(valid, jnp.sum(near, axis=1, keepdims=True), -1.0)
    places_ref[...] = jnp.transpose(jnp.broadcast_to(places, (2 * SLOTS, 128)))[:8].astype(jnp.int32)
    at = lax.broadcasted_iota(jnp.int32, (2 * SLOTS, length), 1)
    hit = at == places.astype(jnp.int32)
    rows = jnp.dot(jnp.where(hit, 1.0, 0.0).astype(jnp.bfloat16), hidden_ref[...], preferred_element_type=jnp.float32)
    rows = rows.astype(jnp.bfloat16)
    target = jnp.sum(jnp.where(hit, targets_ref[...].astype(jnp.float32), 0.0), axis=1, keepdims=True).astype(jnp.int32)
    lane = lax.broadcasted_iota(jnp.int32, (SLOTS, AUX), 1)
    own = target[:SLOTS]
    digits = jnp.where(lane == 0, own & 127, 0)
    digits = jnp.where(lane == 1, (own >> 7) & 127, digits)
    digits = jnp.where(lane == 2, own >> 14, digits)
    digits = jnp.where(lane == 3, ratio_ref[0], digits)
    keep_ref[...] = rows[:SLOTS]
    aux_ref[...] = digits.astype(jnp.float32).astype(jnp.bfloat16)
    give_ref[...] = rows[SLOTS:]


def slot_dest(counts_ref, slot_index, core):
    slot = slot_index & (SLOTS - 1)
    dest = jnp.full_like(slot_index, -1)
    start = jnp.int32(0)
    for i in range(SEQS):
        end = start + counts_ref[i]
        first = first_row(start, core)
        mine = ((slot_index >> 5) == i) & (first + 2 * slot < end)
        dest = jnp.where(mine, (first >> 1) + slot, dest)
        start = end
    return dest


def pack_rows(counts_ref, slots_ref, low_ref, high_ref, row_ref):
    core = lax.axis_index("c")
    dest = slot_dest(counts_ref, lax.broadcasted_iota(jnp.int32, (1, SEQS * SLOTS), 1), core)
    at = lax.broadcasted_iota(jnp.int32, (ROWS, SEQS * SLOTS), 0)
    pick = jnp.where(at == dest, 1.0, 0.0).astype(jnp.bfloat16)
    packed = jnp.dot(pick, slots_ref[...], preferred_element_type=jnp.float32)
    feat = (slots_ref.shape[1] - AUX) // 2
    own, near = packed[:, :feat], packed[:, feat:2 * feat]
    for at, part in ((0, jnp.where(core == 0, own, near)), (feat, jnp.where(core == 0, near, own))):
        part = part.astype(jnp.bfloat16)
        low_ref[:, at:at + feat] = part[:CHUNK]
        high_ref[:, at:at + feat] = part[CHUNK:]
    digits = jnp.transpose(packed[:, 2 * feat:])
    row_ref[0:1] = digits[0:1] + 128.0 * digits[1:2] + 16384.0 * digits[2:3]
    row_ref[1:2] = weight_scale / digits[3:4]


def features_of(away, span):
    return pl.ds(pl.multiple_of(((lax.axis_index("z") + away) & (DEEP - 1)) * span, span), span)


def score_rows(own_ref, near_ref, *refs):
    chunks, (own_scores_ref, near_scores_ref, stats_ref, rows) = refs[:2 * DEEP], refs[2 * DEEP:]
    count = own_ref.shape[0]
    for away in range(DEEP):
        features = features_of(away, chunks[0].shape[1])
        rows[:CHUNK, features] = chunks[2 * away][...]
        rows[CHUNK:, features] = chunks[2 * away + 1][...]
    for w_ref, ref in ((own_ref, own_scores_ref), (near_ref, near_scores_ref)):
        ref[:count] = lax.dot_general(w_ref[...], rows[...], NT, preferred_element_type=jnp.float32)
    at = lax.broadcasted_iota(jnp.int32, own_scores_ref.shape, 0)
    parts = [jnp.where(at < count, ref[...], -jnp.inf) for ref in (own_scores_ref, near_scores_ref)]
    own_scores_ref[...], near_scores_ref[...] = parts
    top = jnp.maximum(*[jnp.max(part, axis=0, keepdims=True) for part in parts])
    total = sum(jnp.sum(jnp.exp(part - top), axis=0, keepdims=True) for part in parts)
    stats = jnp.concatenate([top, total], axis=0)
    stats_ref[...] = jnp.broadcast_to(stats[None], stats_ref.shape)


def grad_rows(aways, own_slope_ref, near_slope_ref, own_ref, near_ref, *sums_refs):
    count = own_ref.shape[0]
    for i, away in enumerate(aways):
        features = features_of(away, sums_refs[0].shape[1])
        sums = jnp.dot(own_slope_ref[:, :count], own_ref[:, features], preferred_element_type=jnp.float32)
        sums += jnp.dot(near_slope_ref[:, :count], near_ref[:, features], preferred_element_type=jnp.float32)
        sums = sums * SENT_SCALE
        sums_refs[2 * i][...] = sums[:CHUNK]
        sums_refs[2 * i + 1][...] = sums[CHUNK:]


def slope_rows(aways, stats_ref, row_ref, own_scores_ref, near_scores_ref, own_ref, near_ref, own_slope_ref, near_slope_ref, *sums_refs):
    count = own_ref.shape[0]
    tops = stats_ref[:, 0, :]
    top = jnp.max(tops, axis=0, keepdims=True)
    total = jnp.sum(stats_ref[:, 1, :] * jnp.exp(tops - top), axis=0, keepdims=True)
    chip = chip_index() * DEEP + lax.axis_index("z")
    core = lax.axis_index("c")
    target = row_ref[0:1].astype(jnp.int32)
    at = lax.broadcasted_iota(jnp.int32, own_scores_ref.shape, 0)
    for ref, slope, of_core in ((own_scores_ref, own_slope_ref, core), (near_scores_ref, near_slope_ref, 1 - core)):
        local_target = target - (chip * 2 + of_core) * count
        probs = jnp.exp(ref[...] - top) / total
        onehot = jnp.where((at == local_target) & (at < count), 1.0, 0.0)
        slope[...] = jnp.transpose(row_ref[1:2] * (probs - onehot)).astype(jnp.bfloat16)
    grad_rows(aways, own_slope_ref, near_slope_ref, own_ref, near_ref, *sums_refs)


def spread_rows(counts_ref, low_ref, high_ref, slots_ref):
    dest = slot_dest(counts_ref, lax.broadcasted_iota(jnp.int32, (1, SEQS * SLOTS), 1), lax.axis_index("c"))
    at = lax.broadcasted_iota(jnp.int32, (ROWS, SEQS * SLOTS), 0)
    pick = jnp.where(at == dest, 1.0, 0.0).astype(jnp.bfloat16)
    rest = jnp.concatenate([low_ref[...], high_ref[...]], axis=0)
    part = rest.astype(jnp.bfloat16)
    rest = (rest - part.astype(jnp.float32)).astype(jnp.bfloat16)
    slots = lax.dot_general(pick, part, TN, preferred_element_type=jnp.float32)
    slots_ref[...] = slots + lax.dot_general(pick, rest, TN, preferred_element_type=jnp.float32)


def place_rows(places_ref, kept_ref, got_ref, out_ref):
    length = out_ref.shape[0]
    at = lax.broadcasted_iota(jnp.int32, (length, 2 * SLOTS), 0)
    hit = jnp.where(at == places_ref[0:1], 1.0, 0.0).astype(jnp.bfloat16)
    rest = jnp.concatenate([kept_ref[...], got_ref[...]], axis=0)
    out = None
    for _ in range(3):
        part = rest.astype(jnp.bfloat16)
        rest = rest - part.astype(jnp.float32)
        part = jnp.dot(hit, part, preferred_element_type=jnp.float32)
        out = part if out is None else out + part
    out_ref[...] = out


def swap_cores(x):
    return lax.ppermute(x, "c", [(0, 1), (1, 0)])


def pass_on(x, by):
    return lax.ppermute(x, "z", [(i, (i + by) % DEEP) for i in range(DEEP)])


def gather_chips(low, high):
    lows, highs = {0: low}, {0: high}
    for hop in range(1, DEEP // 2 + 1):
        lows[-hop] = pass_on(lows[1 - hop], 1)
        highs[hop] = pass_on(highs[hop - 1], -1)
        if hop < DEEP // 2:
            highs[-hop] = pass_on(highs[1 - hop], 1)
            lows[hop] = pass_on(lows[hop - 1], -1)
    lows[DEEP // 2] = lows[-(DEEP // 2)]
    return [chunk for away in range(DEEP) for chunk in (lows[(away + 3) % DEEP - 3], highs[(away + 3) % DEEP - 3])]


def reduce_chips(lows, highs):
    def send(x, by):
        return pass_on(x.astype(jnp.float16), by).astype(jnp.float32)

    half = DEEP // 2
    low_right, high_left = lows[half], highs[half]
    low_left, high_right = lows[half + 1], highs[half - 1]
    for hop in range(1, half):
        low_right = send(low_right, 1) + lows[half - hop]
        high_left = send(high_left, -1) + highs[half + hop]
        if hop < half - 1:
            low_left = send(low_left, -1) + lows[half + 1 + hop]
            high_right = send(high_right, 1) + highs[half - 1 - hop]
    low = lows[0] + send(low_left, -1) + send(low_right, 1)
    high = highs[0] + send(high_right, 1) + send(high_left, -1)
    return low, high


def local(hidden, mask_positions, counts, targets, mask_ratio, own_weight):
    c = lax.axis_index("c")
    features, vocab_dev = own_weight.shape
    wide = -(-vocab_dev // 128) * 128
    length, feat = hidden.shape[1:]
    span = 2 * feat
    smem = pl.BlockSpec(memory_space=pltpu.SMEM)
    vmem = pl.BlockSpec(memory_space=pltpu.VMEM)
    params = pltpu.CompilerParams(vmem_limit_bytes=16 << 20)
    small = pltpu.CompilerParams(vmem_limit_bytes=8 << 20)
    shape = jax.ShapeDtypeStruct

    keep, aux, give, places = pl.pallas_call(
        own_rows,
        out_shape=(
            shape((SLOTS, feat), jnp.bfloat16),
            shape((SLOTS, AUX), jnp.bfloat16),
            shape((SLOTS, feat), jnp.bfloat16),
            shape((8, 2 * SLOTS), jnp.int32),
        ),
        in_specs=[smem, smem, vmem, vmem, vmem],
        out_specs=(vmem,) * 4,
        compiler_params=pltpu.CompilerParams(vmem_limit_bytes=56 << 20),
    )(counts, mask_ratio, mask_positions, targets, hidden[0])
    got = swap_cores(give)

    slots = jnp.concatenate([keep, got, aux], axis=1)
    give, own_weight = lax.optimization_barrier((give, own_weight))
    held = jnp.where(counts[0] > 0, own_weight, 0)
    slots, held = lax.optimization_barrier((slots, held))
    own_t, near_t = held.T, swap_cores(held).T
    slots = lax.all_to_all(jnp.broadcast_to(slots[None], (SEQS,) + slots.shape), PLANE, 0, 0, tiled=True)
    low, high, row_data = pl.pallas_call(
        pack_rows,
        out_shape=(
            shape((CHUNK, span), jnp.bfloat16),
            shape((CHUNK, span), jnp.bfloat16),
            shape((2, ROWS), jnp.float32),
        ),
        in_specs=[smem, vmem],
        out_specs=(vmem,) * 3,
        compiler_params=small,
    )(counts, slots.reshape(SEQS * SLOTS, span + AUX))

    chunks = gather_chips(low, high)
    own_scores, near_scores, stats = pl.pallas_call(
        score_rows,
        out_shape=(
            shape((wide, ROWS), jnp.float32),
            shape((wide, ROWS), jnp.float32),
            shape((SEQS * DEEP, 2, ROWS), jnp.float32),
        ),
        in_specs=[vmem] * (2 + 2 * DEEP),
        out_specs=(vmem,) * 3,
        scratch_shapes=[pltpu.VMEM((ROWS, DEEP * span), jnp.bfloat16)],
        compiler_params=params,
    )(own_t, near_t, *chunks)

    stats = lax.all_to_all(stats, CHIPS, 0, 0, tiled=True)
    parts = (4, 5, 3), (6, 2, 7, 1, 0)
    sums_shape = shape((CHUNK, span), jnp.float32)
    slope_shape = shape((ROWS, wide), jnp.bfloat16)
    own_slope, near_slope, *sums = pl.pallas_call(
        functools.partial(slope_rows, parts[0]),
        out_shape=(slope_shape, slope_shape) + (sums_shape,) * (2 * len(parts[0])),
        in_specs=[vmem] * 6,
        out_specs=(vmem,) * (2 + 2 * len(parts[0])),
        compiler_params=params,
    )(stats, row_data, own_scores, near_scores, own_t, near_t)
    more = pl.pallas_call(
        functools.partial(grad_rows, parts[1]),
        out_shape=(sums_shape,) * (2 * len(parts[1])),
        in_specs=[vmem] * 4,
        out_specs=(vmem,) * (2 * len(parts[1])),
        compiler_params=params,
    )(own_slope, near_slope, own_t, near_t)
    sums = lax.optimization_barrier((*sums, *more))
    lows = dict(zip(parts[0] + parts[1], sums[::2]))
    highs = dict(zip(parts[0] + parts[1], sums[1::2]))

    low, high = reduce_chips(lows, highs)
    back = pl.pallas_call(
        spread_rows,
        out_shape=shape((SEQS * SLOTS, span), jnp.float32),
        in_specs=[smem, vmem, vmem],
        out_specs=vmem,
        compiler_params=small,
    )(counts, low, high)
    back = back.astype(jnp.float16).reshape(SEQS, SLOTS, span)
    first_core = c == 0
    back = lax.all_to_all(back, PLANE, 0, 0, tiled=True)
    back = jnp.sum(back.astype(jnp.float32), axis=0) * (1.0 / SENT_SCALE)
    kept = jnp.where(first_core, back[:, :feat], back[:, feat:])
    given = jnp.where(first_core, back[:, feat:], back[:, :feat])
    grad = pl.pallas_call(
        place_rows,
        out_shape=shape((length, feat), jnp.float32),
        in_specs=[vmem] * 3,
        out_specs=vmem,
        compiler_params=small,
    )(places, kept, swap_cores(given))
    return grad[None]


def solution(mesh):
    fine = Mesh(mesh.devices.reshape(SIDE, SIDE, DEEP, 2), CHIPS + ("c",))
    vocab = ("z", "c")
    return jax.shard_map(
        local,
        mesh=fine,
        in_specs=(
            P(PLANE, None, vocab),
            P(PLANE, None),
            P(),
            P(PLANE, None),
            P(PLANE),
            P(None, CHIPS + ("c",)),
        ),
        out_specs=P(PLANE, None, vocab),
        check_vma=False,
    )
```

```python
import functools

import jax
import jax.numpy as jnp
from jax import lax
from jax.experimental import pallas as pl
from jax.experimental.pallas import tpu as pltpu
from jax.sharding import Mesh
from jax.sharding import PartitionSpec as P

weight_scale = 4.0
SIDE = 4
DEEP = 8
SEQS = SIDE * SIDE
SLOTS = 32
ROWS = 256
CHUNK = ROWS // 2
AUX = 128
PLANE = ("y", "x")
CHIPS = ("y", "x", "z")
NT = (((1,), (1,)), ((), ()))
TN = (((0,), (0,)), ((), ()))
SENT_SCALE = 4096.0


def chip_index():
    return lax.axis_index("y") * SIDE + lax.axis_index("x")


def first_row(start, core):
    return start + ((start + core) & 1)


def own_rows(counts_ref, ratio_ref, positions_ref, targets_ref, hidden_ref, keep_ref, aux_ref, give_ref, places_ref):
    seq = chip_index()
    core = lax.axis_index("c")
    start = jnp.int32(0)
    count = jnp.int32(0)
    for i in range(SEQS):
        start = start + jnp.where(i < seq, counts_ref[i], 0)
        count = count + jnp.where(i == seq, counts_ref[i], 0)
    length = hidden_ref.shape[0]
    q = lax.broadcasted_iota(jnp.int32, (2 * SLOTS, 1), 0)
    index = jnp.where(q < SLOTS, first_row(start, core), first_row(start, 1 - core)) - start + 2 * (q & (SLOTS - 1))
    valid = index < count
    at = lax.broadcasted_iota(jnp.int32, (2 * SLOTS, 128), 1)
    near = jnp.where(at == index, positions_ref[:, :128].astype(jnp.float32), 0.0)
    places = jnp.where(valid, jnp.sum(near, axis=1, keepdims=True), -1.0)
    places_ref[...] = jnp.transpose(jnp.broadcast_to(places, (2 * SLOTS, 128)))[:8].astype(jnp.int32)
    at = lax.broadcasted_iota(jnp.int32, (2 * SLOTS, length), 1)
    hit = at == places.astype(jnp.int32)
    rows = jnp.dot(jnp.where(hit, 1.0, 0.0).astype(jnp.bfloat16), hidden_ref[...], preferred_element_type=jnp.float32)
    rows = rows.astype(jnp.bfloat16)
    target = jnp.sum(jnp.where(hit, targets_ref[...].astype(jnp.float32), 0.0), axis=1, keepdims=True).astype(jnp.int32)
    lane = lax.broadcasted_iota(jnp.int32, (SLOTS, AUX), 1)
    own = target[:SLOTS]
    digits = jnp.where(lane == 0, own & 127, 0)
    digits = jnp.where(lane == 1, (own >> 7) & 127, digits)
    digits = jnp.where(lane == 2, own >> 14, digits)
    digits = jnp.where(lane == 3, ratio_ref[0], digits)
    keep_ref[...] = rows[:SLOTS]
    aux_ref[...] = digits.astype(jnp.float32).astype(jnp.bfloat16)
    give_ref[...] = rows[SLOTS:]


def slot_dest(counts_ref, slot_index, core):
    slot = slot_index & (SLOTS - 1)
    dest = jnp.full_like(slot_index, -1)
    start = jnp.int32(0)
    for i in range(SEQS):
        end = start + counts_ref[i]
        first = first_row(start, core)
        mine = ((slot_index >> 5) == i) & (first + 2 * slot < end)
        dest = jnp.where(mine, (first >> 1) + slot, dest)
        start = end
    return dest


def pack_rows(counts_ref, slots_ref, low_ref, high_ref, row_ref):
    core = lax.axis_index("c")
    dest = slot_dest(counts_ref, lax.broadcasted_iota(jnp.int32, (1, SEQS * SLOTS), 1), core)
    at = lax.broadcasted_iota(jnp.int32, (ROWS, SEQS * SLOTS), 0)
    pick = jnp.where(at == dest, 1.0, 0.0).astype(jnp.bfloat16)
    packed = jnp.dot(pick, slots_ref[...], preferred_element_type=jnp.float32)
    feat = (slots_ref.shape[1] - AUX) // 2
    own, near = packed[:, :feat], packed[:, feat:2 * feat]
    for at, part in ((0, jnp.where(core == 0, own, near)), (feat, jnp.where(core == 0, near, own))):
        part = part.astype(jnp.bfloat16)
        low_ref[:, at:at + feat] = part[:CHUNK]
        high_ref[:, at:at + feat] = part[CHUNK:]
    digits = jnp.transpose(packed[:, 2 * feat:])
    row_ref[0:1] = digits[0:1] + 128.0 * digits[1:2] + 16384.0 * digits[2:3]
    row_ref[1:2] = weight_scale / digits[3:4]


def features_of(away, span):
    return pl.ds(pl.multiple_of(((lax.axis_index("z") + away) & (DEEP - 1)) * span, span), span)


def score_rows(own_ref, near_ref, *refs):
    chunks, (own_scores_ref, near_scores_ref, stats_ref, rows) = refs[:2 * DEEP], refs[2 * DEEP:]
    count = own_ref.shape[0]
    for away in range(DEEP):
        features = features_of(away, chunks[0].shape[1])
        rows[:CHUNK, features] = chunks[2 * away][...]
        rows[CHUNK:, features] = chunks[2 * away + 1][...]
    for w_ref, ref in ((own_ref, own_scores_ref), (near_ref, near_scores_ref)):
        ref[:count] = lax.dot_general(w_ref[...], rows[...], NT, preferred_element_type=jnp.float32)
    at = lax.broadcasted_iota(jnp.int32, own_scores_ref.shape, 0)
    parts = [jnp.where(at < count, ref[...], -jnp.inf) for ref in (own_scores_ref, near_scores_ref)]
    own_scores_ref[...], near_scores_ref[...] = parts
    top = jnp.maximum(*[jnp.max(part, axis=0, keepdims=True) for part in parts])
    total = sum(jnp.sum(jnp.exp(part - top), axis=0, keepdims=True) for part in parts)
    stats = jnp.concatenate([top, total], axis=0)
    stats_ref[...] = jnp.broadcast_to(stats[None], stats_ref.shape)


def grad_rows(aways, own_slope_ref, near_slope_ref, own_ref, near_ref, *sums_refs):
    count = own_ref.shape[0]
    for i, away in enumerate(aways):
        features = features_of(away, sums_refs[0].shape[1])
        sums = jnp.dot(own_slope_ref[:, :count], own_ref[:, features], preferred_element_type=jnp.float32)
        sums += jnp.dot(near_slope_ref[:, :count], near_ref[:, features], preferred_element_type=jnp.float32)
        sums = sums * SENT_SCALE
        sums_refs[2 * i][...] = sums[:CHUNK]
        sums_refs[2 * i + 1][...] = sums[CHUNK:]


def slope_rows(aways, stats_ref, row_ref, own_scores_ref, near_scores_ref, own_ref, near_ref, own_slope_ref, near_slope_ref, *sums_refs):
    count = own_ref.shape[0]
    tops = stats_ref[:, 0, :]
    top = jnp.max(tops, axis=0, keepdims=True)
    total = jnp.sum(stats_ref[:, 1, :] * jnp.exp(tops - top), axis=0, keepdims=True)
    chip = chip_index() * DEEP + lax.axis_index("z")
    core = lax.axis_index("c")
    target = row_ref[0:1].astype(jnp.int32)
    at = lax.broadcasted_iota(jnp.int32, own_scores_ref.shape, 0)
    for ref, slope, of_core in ((own_scores_ref, own_slope_ref, core), (near_scores_ref, near_slope_ref, 1 - core)):
        local_target = target - (chip * 2 + of_core) * count
        probs = jnp.exp(ref[...] - top) / total
        onehot = jnp.where((at == local_target) & (at < count), 1.0, 0.0)
        slope[...] = jnp.transpose(row_ref[1:2] * (probs - onehot)).astype(jnp.bfloat16)
    grad_rows(aways, own_slope_ref, near_slope_ref, own_ref, near_ref, *sums_refs)


def spread_rows(counts_ref, low_ref, high_ref, slots_ref):
    dest = slot_dest(counts_ref, lax.broadcasted_iota(jnp.int32, (1, SEQS * SLOTS), 1), lax.axis_index("c"))
    at = lax.broadcasted_iota(jnp.int32, (ROWS, SEQS * SLOTS), 0)
    pick = jnp.where(at == dest, 1.0, 0.0).astype(jnp.bfloat16)
    rest = jnp.concatenate([low_ref[...], high_ref[...]], axis=0)
    part = rest.astype(jnp.bfloat16)
    rest = (rest - part.astype(jnp.float32)).astype(jnp.bfloat16)
    slots = lax.dot_general(pick, part, TN, preferred_element_type=jnp.float32)
    slots_ref[...] = slots + lax.dot_general(pick, rest, TN, preferred_element_type=jnp.float32)


def place_rows(places_ref, kept_ref, got_ref, out_ref):
    length = out_ref.shape[0]
    at = lax.broadcasted_iota(jnp.int32, (length, 2 * SLOTS), 0)
    hit = jnp.where(at == places_ref[0:1], 1.0, 0.0).astype(jnp.bfloat16)
    rest = jnp.concatenate([kept_ref[...], got_ref[...]], axis=0)
    out = None
    for _ in range(3):
        part = rest.astype(jnp.bfloat16)
        rest = rest - part.astype(jnp.float32)
        part = jnp.dot(hit, part, preferred_element_type=jnp.float32)
        out = part if out is None else out + part
    out_ref[...] = out


def swap_cores(x):
    return lax.ppermute(x, "c", [(0, 1), (1, 0)])


def pass_on(x, by):
    return lax.ppermute(x, "z", [(i, (i + by) % DEEP) for i in range(DEEP)])


def gather_chips(low, high):
    lows, highs = {0: low}, {0: high}
    for hop in range(1, DEEP // 2 + 1):
        lows[-hop] = pass_on(lows[1 - hop], 1)
        highs[hop] = pass_on(highs[hop - 1], -1)
        if hop < DEEP // 2:
            highs[-hop] = pass_on(highs[1 - hop], 1)
            lows[hop] = pass_on(lows[hop - 1], -1)
    lows[DEEP // 2] = lows[-(DEEP // 2)]
    return [chunk for away in range(DEEP) for chunk in (lows[(away + 3) % DEEP - 3], highs[(away + 3) % DEEP - 3])]


def reduce_chips(lows, highs):
    def send(x, by):
        return pass_on(x, by).astype(jnp.float32)

    def after(x, *others):
        return lax.optimization_barrier((x.astype(jnp.float16), *others))[0]

    half = DEEP // 2
    low_right, high_left = lows[half], highs[half]
    low_left, high_right = lows[half + 1], highs[half - 1]
    for hop in range(1, half):
        right, left = low_right.astype(jnp.float16), high_left.astype(jnp.float16)
        low_left, high_right = after(low_left, right, left), after(high_right, right, left)
        low_right = send(right, 1) + lows[half - hop]
        high_left = send(left, -1) + highs[half + hop]
        low_left, high_right = send(low_left, -1), send(high_right, 1)
        if hop < half - 1:
            low_left = low_left + lows[half + 1 + hop]
            high_right = high_right + highs[half - 1 - hop]
    low = lows[0] + low_left + send(low_right.astype(jnp.float16), 1)
    high = highs[0] + high_right + send(high_left.astype(jnp.float16), -1)
    return low, high


def local(hidden, mask_positions, counts, targets, mask_ratio, own_weight):
    c = lax.axis_index("c")
    features, vocab_dev = own_weight.shape
    wide = -(-vocab_dev // 128) * 128
    length, feat = hidden.shape[1:]
    span = 2 * feat
    smem = pl.BlockSpec(memory_space=pltpu.SMEM)
    vmem = pl.BlockSpec(memory_space=pltpu.VMEM)
    params = pltpu.CompilerParams(vmem_limit_bytes=16 << 20)
    small = pltpu.CompilerParams(vmem_limit_bytes=8 << 20)
    shape = jax.ShapeDtypeStruct

    keep, aux, give, places = pl.pallas_call(
        own_rows,
        out_shape=(
            shape((SLOTS, feat), jnp.bfloat16),
            shape((SLOTS, AUX), jnp.bfloat16),
            shape((SLOTS, feat), jnp.bfloat16),
            shape((8, 2 * SLOTS), jnp.int32),
        ),
        in_specs=[smem, smem, vmem, vmem, vmem],
        out_specs=(vmem,) * 4,
        compiler_params=pltpu.CompilerParams(vmem_limit_bytes=56 << 20),
    )(counts, mask_ratio, mask_positions, targets, hidden[0])
    got = swap_cores(give)

    slots = jnp.concatenate([keep, got, aux], axis=1)
    give, own_weight = lax.optimization_barrier((give, own_weight))
    held = jnp.where(counts[0] > 0, own_weight, 0)
    slots, held = lax.optimization_barrier((slots, held))
    own_t, near_t = held.T, swap_cores(held).T
    slots = lax.all_to_all(jnp.broadcast_to(slots[None], (SEQS,) + slots.shape), PLANE, 0, 0, tiled=True)
    low, high, row_data = pl.pallas_call(
        pack_rows,
        out_shape=(
            shape((CHUNK, span), jnp.bfloat16),
            shape((CHUNK, span), jnp.bfloat16),
            shape((2, ROWS), jnp.float32),
        ),
        in_specs=[smem, vmem],
        out_specs=(vmem,) * 3,
        compiler_params=small,
    )(counts, slots.reshape(SEQS * SLOTS, span + AUX))

    chunks = gather_chips(low, high)
    own_scores, near_scores, stats = pl.pallas_call(
        score_rows,
        out_shape=(
            shape((wide, ROWS), jnp.float32),
            shape((wide, ROWS), jnp.float32),
            shape((SEQS * DEEP, 2, ROWS), jnp.float32),
        ),
        in_specs=[vmem] * (2 + 2 * DEEP),
        out_specs=(vmem,) * 3,
        scratch_shapes=[pltpu.VMEM((ROWS, DEEP * span), jnp.bfloat16)],
        compiler_params=params,
    )(own_t, near_t, *chunks)

    stats = lax.all_to_all(stats, CHIPS, 0, 0, tiled=True)
    parts = (4, 5, 3), (6, 2, 7, 1, 0)
    sums_shape = shape((CHUNK, span), jnp.float32)
    slope_shape = shape((ROWS, wide), jnp.bfloat16)
    own_slope, near_slope, *sums = pl.pallas_call(
        functools.partial(slope_rows, parts[0]),
        out_shape=(slope_shape, slope_shape) + (sums_shape,) * (2 * len(parts[0])),
        in_specs=[vmem] * 6,
        out_specs=(vmem,) * (2 + 2 * len(parts[0])),
        compiler_params=params,
    )(stats, row_data, own_scores, near_scores, own_t, near_t)
    more = pl.pallas_call(
        functools.partial(grad_rows, parts[1]),
        out_shape=(sums_shape,) * (2 * len(parts[1])),
        in_specs=[vmem] * 4,
        out_specs=(vmem,) * (2 * len(parts[1])),
        compiler_params=params,
    )(own_slope, near_slope, own_t, near_t)
    sums = lax.optimization_barrier((*sums, *more))
    lows = dict(zip(parts[0] + parts[1], sums[::2]))
    highs = dict(zip(parts[0] + parts[1], sums[1::2]))

    low, high = reduce_chips(lows, highs)
    back = pl.pallas_call(
        spread_rows,
        out_shape=shape((SEQS * SLOTS, span), jnp.float32),
        in_specs=[smem, vmem, vmem],
        out_specs=vmem,
        compiler_params=small,
    )(counts, low, high)
    back = back.astype(jnp.float16).reshape(SEQS, SLOTS, span)
    first_core = c == 0
    back = lax.all_to_all(back, PLANE, 0, 0, tiled=True)
    back = jnp.sum(back.astype(jnp.float32), axis=0) * (1.0 / SENT_SCALE)
    kept = jnp.where(first_core, back[:, :feat], back[:, feat:])
    given = jnp.where(first_core, back[:, feat:], back[:, :feat])
    grad = pl.pallas_call(
        place_rows,
        out_shape=shape((length, feat), jnp.float32),
        in_specs=[vmem] * 3,
        out_specs=vmem,
        compiler_params=small,
    )(places, kept, swap_cores(given))
    return grad[None]


def solution(mesh):
    fine = Mesh(mesh.devices.reshape(SIDE, SIDE, DEEP, 2), CHIPS + ("c",))
    vocab = ("z", "c")
    return jax.shard_map(
        local,
        mesh=fine,
        in_specs=(
            P(PLANE, None, vocab),
            P(PLANE, None),
            P(),
            P(PLANE, None),
            P(PLANE),
            P(None, CHIPS + ("c",)),
        ),
        out_specs=P(PLANE, None, vocab),
        check_vma=False,
    )
```

```python
import functools

import jax
import jax.numpy as jnp
from jax import lax
from jax.experimental import pallas as pl
from jax.experimental.pallas import tpu as pltpu
from jax.sharding import Mesh
from jax.sharding import PartitionSpec as P

weight_scale = 4.0
SIDE = 4
DEEP = 8
SEQS = SIDE * SIDE
SLOTS = 32
ROWS = 256
CHUNK = ROWS // 2
AUX = 128
PLANE = ("y", "x")
CHIPS = ("y", "x", "z")
NT = (((1,), (1,)), ((), ()))
TN = (((0,), (0,)), ((), ()))
SENT_SCALE = 4096.0


def chip_index():
    return lax.axis_index("y") * SIDE + lax.axis_index("x")


def first_row(start, core):
    return start + ((start + core) & 1)


def own_rows(counts_ref, ratio_ref, positions_ref, targets_ref, hidden_ref, keep_ref, aux_ref, give_ref, places_ref):
    seq = chip_index()
    core = lax.axis_index("c")
    start = jnp.int32(0)
    count = jnp.int32(0)
    for i in range(SEQS):
        start = start + jnp.where(i < seq, counts_ref[i], 0)
        count = count + jnp.where(i == seq, counts_ref[i], 0)
    length = hidden_ref.shape[0]
    q = lax.broadcasted_iota(jnp.int32, (2 * SLOTS, 1), 0)
    index = jnp.where(q < SLOTS, first_row(start, core), first_row(start, 1 - core)) - start + 2 * (q & (SLOTS - 1))
    valid = index < count
    at = lax.broadcasted_iota(jnp.int32, (2 * SLOTS, 128), 1)
    near = jnp.where(at == index, positions_ref[:, :128].astype(jnp.float32), 0.0)
    places = jnp.where(valid, jnp.sum(near, axis=1, keepdims=True), -1.0)
    places_ref[...] = jnp.transpose(jnp.broadcast_to(places, (2 * SLOTS, 128)))[:8].astype(jnp.int32)
    at = lax.broadcasted_iota(jnp.int32, (2 * SLOTS, length), 1)
    hit = at == places.astype(jnp.int32)
    rows = jnp.dot(jnp.where(hit, 1.0, 0.0).astype(jnp.bfloat16), hidden_ref[...], preferred_element_type=jnp.float32)
    rows = rows.astype(jnp.bfloat16)
    target = jnp.sum(jnp.where(hit, targets_ref[...].astype(jnp.float32), 0.0), axis=1, keepdims=True).astype(jnp.int32)
    lane = lax.broadcasted_iota(jnp.int32, (SLOTS, AUX), 1)
    own = target[:SLOTS]
    digits = jnp.where(lane == 0, own & 127, 0)
    digits = jnp.where(lane == 1, (own >> 7) & 127, digits)
    digits = jnp.where(lane == 2, own >> 14, digits)
    digits = jnp.where(lane == 3, ratio_ref[0], digits)
    keep_ref[...] = rows[:SLOTS]
    aux_ref[...] = digits.astype(jnp.float32).astype(jnp.bfloat16)
    give_ref[...] = rows[SLOTS:]


def slot_dest(counts_ref, slot_index, core):
    slot = slot_index & (SLOTS - 1)
    dest = jnp.full_like(slot_index, -1)
    start = jnp.int32(0)
    for i in range(SEQS):
        end = start + counts_ref[i]
        first = first_row(start, core)
        mine = ((slot_index >> 5) == i) & (first + 2 * slot < end)
        dest = jnp.where(mine, (first >> 1) + slot, dest)
        start = end
    return dest


def pack_rows(counts_ref, slots_ref, low_ref, high_ref, row_ref):
    core = lax.axis_index("c")
    dest = slot_dest(counts_ref, lax.broadcasted_iota(jnp.int32, (1, SEQS * SLOTS), 1), core)
    at = lax.broadcasted_iota(jnp.int32, (ROWS, SEQS * SLOTS), 0)
    pick = jnp.where(at == dest, 1.0, 0.0).astype(jnp.bfloat16)
    packed = jnp.dot(pick, slots_ref[...], preferred_element_type=jnp.float32)
    feat = (slots_ref.shape[1] - AUX) // 2
    own, near = packed[:, :feat], packed[:, feat:2 * feat]
    for at, part in ((0, jnp.where(core == 0, own, near)), (feat, jnp.where(core == 0, near, own))):
        part = part.astype(jnp.bfloat16)
        low_ref[:, at:at + feat] = part[:CHUNK]
        high_ref[:, at:at + feat] = part[CHUNK:]
    digits = jnp.transpose(packed[:, 2 * feat:])
    row_ref[0:1] = digits[0:1] + 128.0 * digits[1:2] + 16384.0 * digits[2:3]
    row_ref[1:2] = weight_scale / digits[3:4]


def features_of(away, span):
    return pl.ds(pl.multiple_of(((lax.axis_index("z") + away) & (DEEP - 1)) * span, span), span)


def add_scores(aways, own_ref, near_ref, chunks, earlier, refs):
    count = own_ref.shape[0]
    for i, away in enumerate(aways):
        block = jnp.concatenate([chunks[2 * i][...], chunks[2 * i + 1][...]], axis=0)
        features = features_of(away, block.shape[1])
        for w_ref, was_ref, ref in zip((own_ref, near_ref), earlier, refs):
            part = lax.dot_general(w_ref[:, features], block, NT, preferred_element_type=jnp.float32)
            if i == 0:
                ref[:count] = part if was_ref is None else was_ref[:count] + part
            else:
                ref[:count] += part


def early_scores(aways, own_ref, near_ref, *refs):
    add_scores(aways, own_ref, near_ref, refs[:-2], (None, None), refs[-2:])


def score_rows(aways, own_ref, near_ref, own_early_ref, near_early_ref, *refs):
    chunks, (own_scores_ref, near_scores_ref, stats_ref) = refs[:-3], refs[-3:]
    count = own_ref.shape[0]
    add_scores(aways, own_ref, near_ref, chunks, (own_early_ref, near_early_ref), (own_scores_ref, near_scores_ref))
    at = lax.broadcasted_iota(jnp.int32, own_scores_ref.shape, 0)
    parts = [jnp.where(at < count, ref[...], -jnp.inf) for ref in (own_scores_ref, near_scores_ref)]
    own_scores_ref[...], near_scores_ref[...] = parts
    top = jnp.maximum(*[jnp.max(part, axis=0, keepdims=True) for part in parts])
    total = sum(jnp.sum(jnp.exp(part - top), axis=0, keepdims=True) for part in parts)
    stats = jnp.concatenate([top, total], axis=0)
    stats_ref[...] = jnp.broadcast_to(stats[None], stats_ref.shape)


def grad_rows(aways, own_slope_ref, near_slope_ref, own_ref, near_ref, *sums_refs):
    count = own_ref.shape[0]
    for i, away in enumerate(aways):
        features = features_of(away, sums_refs[0].shape[1])
        sums = jnp.dot(own_slope_ref[:, :count], own_ref[:, features], preferred_element_type=jnp.float32)
        sums += jnp.dot(near_slope_ref[:, :count], near_ref[:, features], preferred_element_type=jnp.float32)
        sums = sums * SENT_SCALE
        sums_refs[2 * i][...] = sums[:CHUNK]
        sums_refs[2 * i + 1][...] = sums[CHUNK:]


def slope_rows(aways, stats_ref, row_ref, own_scores_ref, near_scores_ref, own_ref, near_ref, own_slope_ref, near_slope_ref, *sums_refs):
    count = own_ref.shape[0]
    tops = stats_ref[:, 0, :]
    top = jnp.max(tops, axis=0, keepdims=True)
    total = jnp.sum(stats_ref[:, 1, :] * jnp.exp(tops - top), axis=0, keepdims=True)
    chip = chip_index() * DEEP + lax.axis_index("z")
    core = lax.axis_index("c")
    target = row_ref[0:1].astype(jnp.int32)
    at = lax.broadcasted_iota(jnp.int32, own_scores_ref.shape, 0)
    for ref, slope, of_core in ((own_scores_ref, own_slope_ref, core), (near_scores_ref, near_slope_ref, 1 - core)):
        local_target = target - (chip * 2 + of_core) * count
        probs = jnp.exp(ref[...] - top) / total
        onehot = jnp.where((at == local_target) & (at < count), 1.0, 0.0)
        slope[...] = jnp.transpose(row_ref[1:2] * (probs - onehot)).astype(jnp.bfloat16)
    grad_rows(aways, own_slope_ref, near_slope_ref, own_ref, near_ref, *sums_refs)


def spread_rows(counts_ref, low_ref, high_ref, slots_ref):
    dest = slot_dest(counts_ref, lax.broadcasted_iota(jnp.int32, (1, SEQS * SLOTS), 1), lax.axis_index("c"))
    at = lax.broadcasted_iota(jnp.int32, (ROWS, SEQS * SLOTS), 0)
    pick = jnp.where(at == dest, 1.0, 0.0).astype(jnp.bfloat16)
    rest = jnp.concatenate([low_ref[...], high_ref[...]], axis=0)
    part = rest.astype(jnp.bfloat16)
    rest = (rest - part.astype(jnp.float32)).astype(jnp.bfloat16)
    slots = lax.dot_general(pick, part, TN, preferred_element_type=jnp.float32)
    slots_ref[...] = slots + lax.dot_general(pick, rest, TN, preferred_element_type=jnp.float32)


def place_rows(places_ref, kept_ref, got_ref, out_ref):
    length = out_ref.shape[0]
    at = lax.broadcasted_iota(jnp.int32, (length, 2 * SLOTS), 0)
    hit = jnp.where(at == places_ref[0:1], 1.0, 0.0).astype(jnp.bfloat16)
    rest = jnp.concatenate([kept_ref[...], got_ref[...]], axis=0)
    out = None
    for _ in range(3):
        part = rest.astype(jnp.bfloat16)
        rest = rest - part.astype(jnp.float32)
        part = jnp.dot(hit, part, preferred_element_type=jnp.float32)
        out = part if out is None else out + part
    out_ref[...] = out


def swap_cores(x):
    return lax.ppermute(x, "c", [(0, 1), (1, 0)])


def pass_on(x, by):
    return lax.ppermute(x, "z", [(i, (i + by) % DEEP) for i in range(DEEP)])


def gather_chips(low, high):
    lows, highs = {0: low}, {0: high}
    for hop in range(1, DEEP // 2 + 1):
        lows[-hop] = pass_on(lows[1 - hop], 1)
        highs[hop] = pass_on(highs[hop - 1], -1)
        if hop < DEEP // 2:
            highs[-hop] = pass_on(highs[1 - hop], 1)
            lows[hop] = pass_on(lows[hop - 1], -1)
    lows[DEEP // 2] = lows[-(DEEP // 2)]
    return [chunk for away in range(DEEP) for chunk in (lows[(away + 3) % DEEP - 3], highs[(away + 3) % DEEP - 3])]


def reduce_chips(lows, highs):
    def send(x, by):
        return pass_on(x, by).astype(jnp.float32)

    def after(x, *others):
        return lax.optimization_barrier((x.astype(jnp.float16), *others))[0]

    half = DEEP // 2
    low_right, high_left = lows[half], highs[half]
    low_left, high_right = lows[half + 1], highs[half - 1]
    for hop in range(1, half):
        right, left = low_right.astype(jnp.float16), high_left.astype(jnp.float16)
        low_left, high_right = after(low_left, right, left), after(high_right, right, left)
        low_right = send(right, 1) + lows[half - hop]
        high_left = send(left, -1) + highs[half + hop]
        low_left, high_right = send(low_left, -1), send(high_right, 1)
        if hop < half - 1:
            low_left = low_left + lows[half + 1 + hop]
            high_right = high_right + highs[half - 1 - hop]
    low = lows[0] + low_left + send(low_right.astype(jnp.float16), 1)
    high = highs[0] + high_right + send(high_left.astype(jnp.float16), -1)
    return low, high


def local(hidden, mask_positions, counts, targets, mask_ratio, own_weight):
    c = lax.axis_index("c")
    features, vocab_dev = own_weight.shape
    wide = -(-vocab_dev // 128) * 128
    length, feat = hidden.shape[1:]
    span = 2 * feat
    smem = pl.BlockSpec(memory_space=pltpu.SMEM)
    vmem = pl.BlockSpec(memory_space=pltpu.VMEM)
    params = pltpu.CompilerParams(vmem_limit_bytes=16 << 20)
    small = pltpu.CompilerParams(vmem_limit_bytes=8 << 20)
    shape = jax.ShapeDtypeStruct

    keep, aux, give, places = pl.pallas_call(
        own_rows,
        out_shape=(
            shape((SLOTS, feat), jnp.bfloat16),
            shape((SLOTS, AUX), jnp.bfloat16),
            shape((SLOTS, feat), jnp.bfloat16),
            shape((8, 2 * SLOTS), jnp.int32),
        ),
        in_specs=[smem, smem, vmem, vmem, vmem],
        out_specs=(vmem,) * 4,
        compiler_params=pltpu.CompilerParams(vmem_limit_bytes=56 << 20),
    )(counts, mask_ratio, mask_positions, targets, hidden[0])
    got = swap_cores(give)

    slots = jnp.concatenate([keep, got, aux], axis=1)
    slots, own_weight = lax.optimization_barrier((slots, own_weight))
    near_t = swap_cores(own_weight).T
    slots = lax.all_to_all(jnp.broadcast_to(slots[None], (SEQS,) + slots.shape), PLANE, 0, 0, tiled=True)
    low, high, row_data = pl.pallas_call(
        pack_rows,
        out_shape=(
            shape((CHUNK, span), jnp.bfloat16),
            shape((CHUNK, span), jnp.bfloat16),
            shape((2, ROWS), jnp.float32),
        ),
        in_specs=[smem, vmem],
        out_specs=(vmem,) * 3,
        compiler_params=small,
    )(counts, slots.reshape(SEQS * SLOTS, span + AUX))

    chunks = gather_chips(low, high)
    pairs = list(zip(chunks[::2], chunks[1::2]))
    own_weight = lax.optimization_barrier((own_weight, pairs[5][0], pairs[3][1]))[0]
    own_t = jnp.where(counts[0] > 0, own_weight, 0).T
    parts = (0, 1, 7, 2, 6), (3, 5, 4)
    score_shapes = (shape((wide, ROWS), jnp.float32),) * 2
    early = pl.pallas_call(
        functools.partial(early_scores, parts[0]),
        out_shape=score_shapes,
        in_specs=[vmem] * (2 + 2 * len(parts[0])),
        out_specs=(vmem,) * 2,
        compiler_params=params,
    )(own_t, near_t, *[chunk for away in parts[0] for chunk in pairs[away]])
    own_scores, near_scores, stats = pl.pallas_call(
        functools.partial(score_rows, parts[1]),
        out_shape=score_shapes + (shape((SEQS * DEEP, 2, ROWS), jnp.float32),),
        in_specs=[vmem] * (4 + 2 * len(parts[1])),
        out_specs=(vmem,) * 3,
        compiler_params=params,
    )(own_t, near_t, *early, *[chunk for away in parts[1] for chunk in pairs[away]])

    stats = lax.all_to_all(stats, CHIPS, 0, 0, tiled=True)
    parts = (4, 5, 3), (6, 2, 7, 1, 0)
    sums_shape = shape((CHUNK, span), jnp.float32)
    slope_shape = shape((ROWS, wide), jnp.bfloat16)
    own_slope, near_slope, *sums = pl.pallas_call(
        functools.partial(slope_rows, parts[0]),
        out_shape=(slope_shape, slope_shape) + (sums_shape,) * (2 * len(parts[0])),
        in_specs=[vmem] * 6,
        out_specs=(vmem,) * (2 + 2 * len(parts[0])),
        compiler_params=params,
    )(stats, row_data, own_scores, near_scores, own_t, near_t)
    more = pl.pallas_call(
        functools.partial(grad_rows, parts[1]),
        out_shape=(sums_shape,) * (2 * len(parts[1])),
        in_specs=[vmem] * 4,
        out_specs=(vmem,) * (2 * len(parts[1])),
        compiler_params=params,
    )(own_slope, near_slope, own_t, near_t)
    sums = lax.optimization_barrier((*sums, *more))
    lows = dict(zip(parts[0] + parts[1], sums[::2]))
    highs = dict(zip(parts[0] + parts[1], sums[1::2]))

    low, high = reduce_chips(lows, highs)
    back = pl.pallas_call(
        spread_rows,
        out_shape=shape((SEQS * SLOTS, span), jnp.float32),
        in_specs=[smem, vmem, vmem],
        out_specs=vmem,
        compiler_params=small,
    )(counts, low, high)
    back = back.astype(jnp.float16).reshape(SEQS, SLOTS, span)
    first_core = c == 0
    back = lax.all_to_all(back, PLANE, 0, 0, tiled=True)
    back = jnp.sum(back.astype(jnp.float32), axis=0) * (1.0 / SENT_SCALE)
    kept = jnp.where(first_core, back[:, :feat], back[:, feat:])
    given = jnp.where(first_core, back[:, feat:], back[:, :feat])
    grad = pl.pallas_call(
        place_rows,
        out_shape=shape((length, feat), jnp.float32),
        in_specs=[vmem] * 3,
        out_specs=vmem,
        compiler_params=small,
    )(places, kept, swap_cores(given))
    return grad[None]


def solution(mesh):
    fine = Mesh(mesh.devices.reshape(SIDE, SIDE, DEEP, 2), CHIPS + ("c",))
    vocab = ("z", "c")
    return jax.shard_map(
        local,
        mesh=fine,
        in_specs=(
            P(PLANE, None, vocab),
            P(PLANE, None),
            P(),
            P(PLANE, None),
            P(PLANE),
            P(None, CHIPS + ("c",)),
        ),
        out_specs=P(PLANE, None, vocab),
        check_vma=False,
    )
```

```python
import functools

import jax
import jax.numpy as jnp
from jax import lax
from jax.experimental import pallas as pl
from jax.experimental.pallas import tpu as pltpu
from jax.sharding import Mesh
from jax.sharding import PartitionSpec as P

weight_scale = 4.0
SIDE = 4
DEEP = 8
SEQS = SIDE * SIDE
SLOTS = 32
ROWS = 256
CHUNK = ROWS // 2
AUX = 128
PLANE = ("y", "x")
CHIPS = ("y", "x", "z")
NT = (((1,), (1,)), ((), ()))
TN = (((0,), (0,)), ((), ()))
SENT_SCALE = 4096.0


def chip_index():
    return lax.axis_index("y") * SIDE + lax.axis_index("x")


def first_row(start, core):
    return start + ((start + core) & 1)


def own_rows(counts_ref, ratio_ref, positions_ref, targets_ref, hidden_ref, keep_ref, aux_ref, give_ref, places_ref):
    seq = chip_index()
    core = lax.axis_index("c")
    start = jnp.int32(0)
    count = jnp.int32(0)
    for i in range(SEQS):
        start = start + jnp.where(i < seq, counts_ref[i], 0)
        count = count + jnp.where(i == seq, counts_ref[i], 0)
    length = hidden_ref.shape[0]
    q = lax.broadcasted_iota(jnp.int32, (2 * SLOTS, 1), 0)
    index = jnp.where(q < SLOTS, first_row(start, core), first_row(start, 1 - core)) - start + 2 * (q & (SLOTS - 1))
    valid = index < count
    at = lax.broadcasted_iota(jnp.int32, (2 * SLOTS, 128), 1)
    near = jnp.where(at == index, positions_ref[:, :128].astype(jnp.float32), 0.0)
    places = jnp.where(valid, jnp.sum(near, axis=1, keepdims=True), -1.0)
    places_ref[...] = jnp.transpose(jnp.broadcast_to(places, (2 * SLOTS, 128)))[:8].astype(jnp.int32)
    at = lax.broadcasted_iota(jnp.int32, (2 * SLOTS, length), 1)
    hit = at == places.astype(jnp.int32)
    rows = jnp.dot(jnp.where(hit, 1.0, 0.0).astype(jnp.bfloat16), hidden_ref[...], preferred_element_type=jnp.float32)
    rows = rows.astype(jnp.bfloat16)
    target = jnp.sum(jnp.where(hit, targets_ref[...].astype(jnp.float32), 0.0), axis=1, keepdims=True).astype(jnp.int32)
    lane = lax.broadcasted_iota(jnp.int32, (SLOTS, AUX), 1)
    own = target[:SLOTS]
    digits = jnp.where(lane == 0, own & 127, 0)
    digits = jnp.where(lane == 1, (own >> 7) & 127, digits)
    digits = jnp.where(lane == 2, own >> 14, digits)
    digits = jnp.where(lane == 3, ratio_ref[0], digits)
    keep_ref[...] = rows[:SLOTS]
    aux_ref[...] = digits.astype(jnp.float32).astype(jnp.bfloat16)
    give_ref[...] = rows[SLOTS:]


def slot_dest(counts_ref, slot_index, core):
    slot = slot_index & (SLOTS - 1)
    dest = jnp.full_like(slot_index, -1)
    start = jnp.int32(0)
    for i in range(SEQS):
        end = start + counts_ref[i]
        first = first_row(start, core)
        mine = ((slot_index >> 5) == i) & (first + 2 * slot < end)
        dest = jnp.where(mine, (first >> 1) + slot, dest)
        start = end
    return dest


def pack_rows(counts_ref, slots_ref, low_ref, high_ref, row_ref):
    core = lax.axis_index("c")
    dest = slot_dest(counts_ref, lax.broadcasted_iota(jnp.int32, (1, SEQS * SLOTS), 1), core)
    at = lax.broadcasted_iota(jnp.int32, (ROWS, SEQS * SLOTS), 0)
    pick = jnp.where(at == dest, 1.0, 0.0).astype(jnp.bfloat16)
    packed = jnp.dot(pick, slots_ref[...], preferred_element_type=jnp.float32)
    feat = (slots_ref.shape[1] - AUX) // 2
    own, near = packed[:, :feat], packed[:, feat:2 * feat]
    for at, part in ((0, jnp.where(core == 0, own, near)), (feat, jnp.where(core == 0, near, own))):
        part = part.astype(jnp.bfloat16)
        low_ref[:, at:at + feat] = part[:CHUNK]
        high_ref[:, at:at + feat] = part[CHUNK:]
    digits = jnp.transpose(packed[:, 2 * feat:])
    row_ref[0:1] = digits[0:1] + 128.0 * digits[1:2] + 16384.0 * digits[2:3]
    row_ref[1:2] = weight_scale / digits[3:4]


def features_of(away, span):
    return pl.ds(pl.multiple_of(((lax.axis_index("z") + away) & (DEEP - 1)) * span, span), span)


def add_scores(aways, own_ref, near_ref, chunks, earlier, refs):
    count = own_ref.shape[0]
    for i, away in enumerate(aways):
        block = jnp.concatenate([chunks[2 * i][...], chunks[2 * i + 1][...]], axis=0)
        features = features_of(away, block.shape[1])
        for w_ref, was_ref, ref in zip((own_ref, near_ref), earlier, refs):
            part = lax.dot_general(w_ref[:, features], block, NT, preferred_element_type=jnp.float32)
            if i == 0:
                ref[:count] = part if was_ref is None else was_ref[:count] + part
            else:
                ref[:count] += part


def early_scores(aways, own_ref, near_ref, *refs):
    add_scores(aways, own_ref, near_ref, refs[:-2], (None, None), refs[-2:])


def score_rows(aways, own_ref, near_ref, own_early_ref, near_early_ref, *refs):
    chunks, (own_scores_ref, near_scores_ref, stats_ref) = refs[:-3], refs[-3:]
    count = own_ref.shape[0]
    add_scores(aways, own_ref, near_ref, chunks, (own_early_ref, near_early_ref), (own_scores_ref, near_scores_ref))
    at = lax.broadcasted_iota(jnp.int32, own_scores_ref.shape, 0)
    parts = [jnp.where(at < count, ref[...], -jnp.inf) for ref in (own_scores_ref, near_scores_ref)]
    own_scores_ref[...], near_scores_ref[...] = parts
    top = jnp.maximum(*[jnp.max(part, axis=0, keepdims=True) for part in parts])
    total = sum(jnp.sum(jnp.exp(part - top), axis=0, keepdims=True) for part in parts)
    stats = jnp.concatenate([top, total], axis=0)
    stats_ref[...] = jnp.broadcast_to(stats[None], stats_ref.shape)


def grad_rows(aways, own_slope_ref, near_slope_ref, own_ref, near_ref, *sums_refs):
    count = own_ref.shape[0]
    for i, away in enumerate(aways):
        features = features_of(away, sums_refs[0].shape[1])
        sums = jnp.dot(own_slope_ref[:, :count], own_ref[:, features], preferred_element_type=jnp.float32)
        sums += jnp.dot(near_slope_ref[:, :count], near_ref[:, features], preferred_element_type=jnp.float32)
        sums = sums * SENT_SCALE
        sums_refs[2 * i][...] = sums[:CHUNK]
        sums_refs[2 * i + 1][...] = sums[CHUNK:]


def slope_rows(aways, stats_ref, row_ref, own_scores_ref, near_scores_ref, own_ref, near_ref, own_slope_ref, near_slope_ref, *sums_refs):
    count = own_ref.shape[0]
    tops = stats_ref[:, 0, :]
    top = jnp.max(tops, axis=0, keepdims=True)
    total = jnp.sum(stats_ref[:, 1, :] * jnp.exp(tops - top), axis=0, keepdims=True)
    chip = chip_index() * DEEP + lax.axis_index("z")
    core = lax.axis_index("c")
    target = row_ref[0:1].astype(jnp.int32)
    at = lax.broadcasted_iota(jnp.int32, own_scores_ref.shape, 0)
    for ref, slope, of_core in ((own_scores_ref, own_slope_ref, core), (near_scores_ref, near_slope_ref, 1 - core)):
        local_target = target - (chip * 2 + of_core) * count
        probs = jnp.exp(ref[...] - top) / total
        onehot = jnp.where((at == local_target) & (at < count), 1.0, 0.0)
        slope[...] = jnp.transpose(row_ref[1:2] * (probs - onehot)).astype(jnp.bfloat16)
    grad_rows(aways, own_slope_ref, near_slope_ref, own_ref, near_ref, *sums_refs)


def spread_rows(counts_ref, low_ref, high_ref, slots_ref):
    dest = slot_dest(counts_ref, lax.broadcasted_iota(jnp.int32, (1, SEQS * SLOTS), 1), lax.axis_index("c"))
    at = lax.broadcasted_iota(jnp.int32, (ROWS, SEQS * SLOTS), 0)
    pick = jnp.where(at == dest, 1.0, 0.0).astype(jnp.bfloat16)
    rest = jnp.concatenate([low_ref[...], high_ref[...]], axis=0)
    part = rest.astype(jnp.bfloat16)
    rest = (rest - part.astype(jnp.float32)).astype(jnp.bfloat16)
    slots = lax.dot_general(pick, part, TN, preferred_element_type=jnp.float32)
    slots_ref[...] = slots + lax.dot_general(pick, rest, TN, preferred_element_type=jnp.float32)


def place_rows(places_ref, kept_ref, got_ref, out_ref):
    length = out_ref.shape[0]
    at = lax.broadcasted_iota(jnp.int32, (length, 2 * SLOTS), 0)
    hit = jnp.where(at == places_ref[0:1], 1.0, 0.0).astype(jnp.bfloat16)
    rest = jnp.concatenate([kept_ref[...], got_ref[...]], axis=0)
    out = None
    for _ in range(3):
        part = rest.astype(jnp.bfloat16)
        rest = rest - part.astype(jnp.float32)
        part = jnp.dot(hit, part, preferred_element_type=jnp.float32)
        out = part if out is None else out + part
    out_ref[...] = out


def swap_cores(x):
    return lax.ppermute(x, "c", [(0, 1), (1, 0)])


def pass_on(x, by):
    return lax.ppermute(x, "z", [(i, (i + by) % DEEP) for i in range(DEEP)])


def gather_chips(low, high):
    lows, highs = {0: low}, {0: high}
    for hop in range(1, DEEP // 2 + 1):
        lows[-hop] = pass_on(lows[1 - hop], 1)
        highs[hop] = pass_on(highs[hop - 1], -1)
        if hop < DEEP // 2:
            highs[-hop] = pass_on(highs[1 - hop], 1)
            lows[hop] = pass_on(lows[hop - 1], -1)
    lows[DEEP // 2] = lows[-(DEEP // 2)]
    return [chunk for away in range(DEEP) for chunk in (lows[(away + 3) % DEEP - 3], highs[(away + 3) % DEEP - 3])]


def reduce_chips(lows, highs):
    def send(x, by):
        return pass_on(x, by).astype(jnp.float32)

    def after(x, *others):
        return lax.optimization_barrier((x.astype(jnp.float16), *others))[0]

    half = DEEP // 2
    low_right, high_left = lows[half], highs[half]
    low_left, high_right = lows[half + 1], highs[half - 1]
    for hop in range(1, half):
        right, left = low_right.astype(jnp.float16), high_left.astype(jnp.float16)
        low_left, high_right = after(low_left, right, left), after(high_right, right, left)
        low_right = send(right, 1) + lows[half - hop]
        high_left = send(left, -1) + highs[half + hop]
        low_left, high_right = send(low_left, -1), send(high_right, 1)
        if hop < half - 1:
            low_left = low_left + lows[half + 1 + hop]
            high_right = high_right + highs[half - 1 - hop]
    low = lows[0] + low_left + send(low_right.astype(jnp.float16), 1)
    high = highs[0] + high_right + send(high_left.astype(jnp.float16), -1)
    return low, high


def local(hidden, mask_positions, counts, targets, mask_ratio, own_weight):
    c = lax.axis_index("c")
    features, vocab_dev = own_weight.shape
    wide = -(-vocab_dev // 128) * 128
    length, feat = hidden.shape[1:]
    span = 2 * feat
    smem = pl.BlockSpec(memory_space=pltpu.SMEM)
    vmem = pl.BlockSpec(memory_space=pltpu.VMEM)
    params = pltpu.CompilerParams(vmem_limit_bytes=16 << 20)
    small = pltpu.CompilerParams(vmem_limit_bytes=8 << 20)
    shape = jax.ShapeDtypeStruct

    keep, aux, give, places = pl.pallas_call(
        own_rows,
        out_shape=(
            shape((SLOTS, feat), jnp.bfloat16),
            shape((SLOTS, AUX), jnp.bfloat16),
            shape((SLOTS, feat), jnp.bfloat16),
            shape((8, 2 * SLOTS), jnp.int32),
        ),
        in_specs=[smem, smem, vmem, vmem, vmem],
        out_specs=(vmem,) * 4,
        compiler_params=pltpu.CompilerParams(vmem_limit_bytes=56 << 20),
    )(counts, mask_ratio, mask_positions, targets, hidden[0])
    got = swap_cores(give)

    slots = jnp.concatenate([keep, got, aux], axis=1)
    counts = jnp.maximum(lax.optimization_barrier((counts, give))[0], 0)
    slots, own_weight, counts = lax.optimization_barrier((slots, own_weight, counts))
    near_t = swap_cores(own_weight).T
    slots = lax.all_to_all(jnp.broadcast_to(slots[None], (SEQS,) + slots.shape), PLANE, 0, 0, tiled=True)
    low, high, row_data = pl.pallas_call(
        pack_rows,
        out_shape=(
            shape((CHUNK, span), jnp.bfloat16),
            shape((CHUNK, span), jnp.bfloat16),
            shape((2, ROWS), jnp.float32),
        ),
        in_specs=[smem, vmem],
        out_specs=(vmem,) * 3,
        compiler_params=small,
    )(counts, slots.reshape(SEQS * SLOTS, span + AUX))

    chunks = gather_chips(low, high)
    pairs = list(zip(chunks[::2], chunks[1::2]))
    own_weight = lax.optimization_barrier((own_weight, pairs[5][0], pairs[3][1]))[0]
    own_t = jnp.where(counts[0] > 0, own_weight, 0).T
    parts = (0, 1, 7, 2, 6), (3, 5, 4)
    score_shapes = (shape((wide, ROWS), jnp.float32),) * 2
    early = pl.pallas_call(
        functools.partial(early_scores, parts[0]),
        out_shape=score_shapes,
        in_specs=[vmem] * (2 + 2 * len(parts[0])),
        out_specs=(vmem,) * 2,
        compiler_params=params,
    )(own_t, near_t, *[chunk for away in parts[0] for chunk in pairs[away]])
    own_scores, near_scores, stats = pl.pallas_call(
        functools.partial(score_rows, parts[1]),
        out_shape=score_shapes + (shape((SEQS * DEEP, 2, ROWS), jnp.float32),),
        in_specs=[vmem] * (4 + 2 * len(parts[1])),
        out_specs=(vmem,) * 3,
        compiler_params=params,
    )(own_t, near_t, *early, *[chunk for away in parts[1] for chunk in pairs[away]])

    stats = lax.all_to_all(stats, CHIPS, 0, 0, tiled=True)
    parts = (4, 5, 3), (6, 2, 7, 1, 0)
    sums_shape = shape((CHUNK, span), jnp.float32)
    slope_shape = shape((ROWS, wide), jnp.bfloat16)
    own_slope, near_slope, *sums = pl.pallas_call(
        functools.partial(slope_rows, parts[0]),
        out_shape=(slope_shape, slope_shape) + (sums_shape,) * (2 * len(parts[0])),
        in_specs=[vmem] * 6,
        out_specs=(vmem,) * (2 + 2 * len(parts[0])),
        compiler_params=params,
    )(stats, row_data, own_scores, near_scores, own_t, near_t)
    more = pl.pallas_call(
        functools.partial(grad_rows, parts[1]),
        out_shape=(sums_shape,) * (2 * len(parts[1])),
        in_specs=[vmem] * 4,
        out_specs=(vmem,) * (2 * len(parts[1])),
        compiler_params=params,
    )(own_slope, near_slope, own_t, near_t)
    sums = lax.optimization_barrier((*sums, *more))
    lows = dict(zip(parts[0] + parts[1], sums[::2]))
    highs = dict(zip(parts[0] + parts[1], sums[1::2]))

    low, high = reduce_chips(lows, highs)
    back = pl.pallas_call(
        spread_rows,
        out_shape=shape((SEQS * SLOTS, span), jnp.float32),
        in_specs=[smem, vmem, vmem],
        out_specs=vmem,
        compiler_params=small,
    )(counts, low, high)
    back = back.astype(jnp.float16).reshape(SEQS, SLOTS, span)
    first_core = c == 0
    back = lax.all_to_all(back, PLANE, 0, 0, tiled=True)
    back = jnp.sum(back.astype(jnp.float32), axis=0) * (1.0 / SENT_SCALE)
    kept = jnp.where(first_core, back[:, :feat], back[:, feat:])
    given = jnp.where(first_core, back[:, feat:], back[:, :feat])
    grad = pl.pallas_call(
        place_rows,
        out_shape=shape((length, feat), jnp.float32),
        in_specs=[vmem] * 3,
        out_specs=vmem,
        compiler_params=small,
    )(places, kept, swap_cores(given))
    return grad[None]


def solution(mesh):
    fine = Mesh(mesh.devices.reshape(SIDE, SIDE, DEEP, 2), CHIPS + ("c",))
    vocab = ("z", "c")
    return jax.shard_map(
        local,
        mesh=fine,
        in_specs=(
            P(PLANE, None, vocab),
            P(PLANE, None),
            P(),
            P(PLANE, None),
            P(PLANE),
            P(None, CHIPS + ("c",)),
        ),
        out_specs=P(PLANE, None, vocab),
        check_vma=False,
    )
```
